32 devices in a mesh: dp: 8 (over y, x, core), tensor: 4 (over z).
Axes of the slice: x: 2, y: 2, z: 4, core: 2. Of those that a mesh axis runs over, the one named last changes fastest.
Arguments:
- layer_input: bfloat16 [8192, 1024], P(('dp', 'tensor')), may hold values from -6 to 6
- query_weight: bfloat16 [1024, 1024], P('dp', 'tensor'), may hold values from -0.1875 to 0.1875
- key_weight: bfloat16 [1024, 1024], P('dp', 'tensor'), may hold values from -0.1875 to 0.1875
- value_weight: bfloat16 [1024, 1024], P('dp', 'tensor'), may hold values from -0.1875 to 0.1875
- mixing_weight: bfloat16 [1024, 1024], P('tensor', 'dp'), may hold values from -1.5 to 1.5
- expand_weight: bfloat16 [1024, 4096], P('dp', 'tensor'), may hold values from -0.1875 to 0.1875
- shrink_weight: bfloat16 [4096, 1024], P('tensor', 'dp'), may hold values from -0.09375 to 0.09375
- query_offset: bfloat16 [1024], P('tensor'), may hold values from -3 to 3
- value_offset: bfloat16 [1024], P('tensor'), may hold values from -3 to 3
- mixing_offset: bfloat16 [1024], replicated, may hold values from -2 to 2
- expand_offset: bfloat16 [4096], P('tensor'), may hold values from -3 to 3
- shrink_offset: bfloat16 [1024], replicated, may hold values from -2 to 2
- first_gain: bfloat16 [1024], replicated, may hold values from 0.25 to 1.75
- first_shift: bfloat16 [1024], replicated, may hold values from -2 to 2
- second_gain: bfloat16 [1024], replicated, may hold values from 0.25 to 1.75
- second_shift: bfloat16 [1024], replicated, may hold values from -2 to 2
- cotangent: bfloat16 [8192, 1024], P(('dp', 'tensor')), may hold values from -6 to 6
Outputs:
- layer_output: bfloat16 [8192, 1024], P(('dp', 'tensor'))
- input_grad: float32 [8192, 1024], P(('dp', 'tensor'))
- query_grad: float32 [1024, 1024], P('dp', 'tensor')
- key_grad: float32 [1024, 1024], P('dp', 'tensor')
- value_grad: float32 [1024, 1024], P('dp', 'tensor')
- mixing_grad: float32 [1024, 1024], P('tensor', 'dp')
- expand_grad: float32 [1024, 4096], P('dp', 'tensor')
- shrink_grad: float32 [4096, 1024], P('tensor', 'dp')
- offset_query: float32 [1024], P('tensor')
- offset_value: float32 [1024], P('tensor')
- offset_mixing: float32 [1024], replicated
- offset_expand: float32 [4096], P('tensor')
- offset_shrink: float32 [1024], replicated
- gain_first: float32 [1024], replicated
- shift_first: float32 [1024], replicated
- gain_second: float32 [1024], replicated
- shift_second: float32 [1024], replicated
The draws below stay inside these ranges and needn't reach their ends.
All inputs are finite; a program needn't handle non-finite values.
Results may differ from the reference program's by a relative error of at most 0.015.
Values may be sent and summed in bfloat16 or wider, within the bound.
A program may use at most 128 MiB of HBM per device.

```python
import jax
import jax.numpy as jnp
from jax import lax

D = 1024
H = 16
HD = 64
FF = 4096
TOK_DEV = 256
SEQ = 1024
TOKENS = 8192
N_TENSOR = 4


def block_scale(rng, shape, split, smallest, largest):
    loudness = 1.0
    for position, shards_of in split:
        heights = jax.random.uniform(jax.random.fold_in(jax.random.fold_in(rng, 6), position), (shards_of,), jnp.float32, smallest / len(split), largest / len(split))
        loudness = loudness * jnp.repeat(jnp.exp(heights), shape[position] // shards_of).reshape((-1,) + (1,) * (len(shape) - 1 - position))
    return loudness


def scatter_about(rng, extent, width, limit, split=(), held_as=jnp.bfloat16):
    array = width * jax.random.normal(rng, extent, jnp.float32)
    if split:
        array = array * block_scale(rng, extent, split, -0.22, 0.18)
    return jnp.clip(array, -limit, limit).astype(held_as)


def setup_inputs(seed: int = 0) -> dict:
    keys = jax.random.split(jax.random.key(seed), 18)
    return {
        "layer_input": scatter_about(keys[0], (TOKENS, D), 1.0, 6.0, ((0, 32),)),
        "query_weight": scatter_about(keys[1], (D, D), D ** -0.5, 0.1875, ((0, 8), (1, 4))),
        "key_weight": scatter_about(keys[2], (D, D), D ** -0.5, 0.1875, ((0, 8), (1, 4))),
        "value_weight": scatter_about(keys[3], (D, D), D ** -0.5, 0.1875, ((0, 8), (1, 4))),
        "mixing_weight": scatter_about(keys[4], (D, D), (max(D * 16 // (TOK_DEV * N_TENSOR), 1)) ** -0.5, 1.5, ((0, 4), (1, 8))),
        "expand_weight": scatter_about(keys[5], (D, FF), D ** -0.5, 0.1875, ((0, 8), (1, 4))),
        "shrink_weight": scatter_about(keys[6], (FF, D), FF ** -0.5, 0.09375, ((0, 4), (1, 8))),
        "query_offset": scatter_about(keys[7], (D,), 0.5, 3.0, ((0, 4),)),
        "value_offset": scatter_about(keys[8], (D,), 0.5, 3.0, ((0, 4),)),
        "mixing_offset": scatter_about(keys[9], (D,), 0.3, 2.0),
        "expand_offset": scatter_about(keys[10], (FF,), 0.5, 3.0, ((0, 4),)),
        "shrink_offset": scatter_about(keys[11], (D,), 0.3, 2.0),
        "first_gain": jnp.clip(1.0 + 0.15 * jax.random.normal(keys[12], (D,), jnp.float32), 0.25, 1.75).astype(jnp.bfloat16),
        "first_shift": scatter_about(keys[13], (D,), 0.3, 2.0),
        "second_gain": jnp.clip(1.0 + 0.15 * jax.random.normal(keys[14], (D,), jnp.float32), 0.25, 1.75).astype(jnp.bfloat16),
        "second_shift": scatter_about(keys[15], (D,), 0.3, 2.0),
        "cotangent": scatter_about(keys[16], (TOKENS, D), 1.0, 6.0, ((0, 32),)),
    }


@jax.custom_vjp
def low(v):
    return lax.optimization_barrier(v.astype(jnp.bfloat16)).astype(jnp.float32)

@jax.custom_vjp
def low_back(v):
    return v

def low_keep(v):
    return (low(v), None)

def low_pass(kept, grad):
    return (grad,)

def back_keep(v):
    return (v, None)

def back_low(kept, grad):
    return (low(grad),)
low.defvjp(low_keep, low_pass)
low_back.defvjp(back_keep, back_low)
EPSILON = 1e-05

def matmul(left, right):
    return jnp.dot(left, right, precision=lax.Precision.HIGHEST, preferred_element_type=jnp.float32)

def layer_norm(inputs, gain, shift):
    centered = inputs - lax.optimization_barrier(jnp.mean(inputs, axis=-1, keepdims=True))
    variance = lax.optimization_barrier(jnp.mean(centered * centered, axis=-1, keepdims=True))
    return centered * lax.rsqrt(variance + EPSILON) * gain + shift

def sequence_layer(sequence, params):
    query_weight, key_weight, value_weight, mixing_weight, expand_weight, shrink_weight, query_offset, value_offset, mixing_offset, expand_offset, shrink_offset, first_gain, first_shift, second_gain, second_shift = params
    length = sequence.shape[0]
    scaling = HD ** (-0.5)
    queries = low(low_back((matmul(sequence, query_weight) + query_offset) * scaling)).reshape(length, H, HD)
    key_rows = low(low_back(matmul(sequence, key_weight))).reshape(length, H, HD)
    values = low(low_back(matmul(sequence, value_weight) + value_offset)).reshape(length, H, HD)
    scores = low_back(jnp.einsum('qhd,khd->hqk', queries, key_rows, precision=lax.Precision.HIGHEST))
    weights = jax.nn.softmax(scores, axis=-1)
    mixture = jnp.einsum('hqk,khd->qhd', low(weights), values, precision=lax.Precision.HIGHEST)
    mixture = low(low_back(mixture.reshape(length, H * HD)))
    attended = sequence + low_back(matmul(mixture, mixing_weight)) + mixing_offset
    first_norm = layer_norm(attended, first_gain, first_shift)
    expanded = low_back(matmul(low(first_norm), expand_weight) + expand_offset)
    hidden = low(jax.nn.gelu(expanded, approximate=False))
    summed = first_norm + low_back(matmul(hidden, shrink_weight)) + shrink_offset
    return layer_norm(summed, second_gain, second_shift)

def reference(layer_input, query_weight, key_weight, value_weight, mixing_weight, expand_weight, shrink_weight, query_offset, value_offset, mixing_offset, expand_offset, shrink_offset, first_gain, first_shift, second_gain, second_shift, cotangent):
    params = tuple((argument.astype(jnp.float32) for argument in (query_weight, key_weight, value_weight, mixing_weight, expand_weight, shrink_weight, query_offset, value_offset, mixing_offset, expand_offset, shrink_offset, first_gain, first_shift, second_gain, second_shift)))
    checked = jax.checkpoint(sequence_layer)

    def forward(inputs, layer_params):
        blocks = inputs.reshape(TOKENS // SEQ, SEQ, D)
        outputs = lax.map(lambda sequence_block: checked(sequence_block, layer_params), blocks)
        return outputs.reshape(TOKENS, D)
    result, pullback = jax.vjp(forward, layer_input.astype(jnp.float32), params)
    input_grad, grads = pullback(cotangent.astype(jnp.float32))
    return (result.astype(jnp.bfloat16), input_grad, grads[0], grads[1], grads[2], grads[3], grads[4], grads[5], grads[6], grads[7], grads[8], grads[9], grads[10], grads[11], grads[12], grads[13], grads[14])
```

```python
import jax
import jax.numpy as jnp
from jax import lax
from jax.sharding import PartitionSpec as P

HD = 64


EPSILON = 1e-05
CONTRACT_ROWS = (((0,), (0,)), ((), ()))
CONTRACT_LAST = (((1,), (1,)), ((), ()))


def layer_norm(inputs, gain, shift):
    centered = inputs - jnp.mean(inputs, axis=-1, keepdims=True)
    variance = jnp.mean(centered * centered, axis=-1, keepdims=True)
    return centered * lax.rsqrt(variance + EPSILON) * gain + shift


def product(left, right):
    return jnp.dot(left, right, preferred_element_type=jnp.float32)


def product_rows(left, right):
    return lax.dot_general(left, right, CONTRACT_ROWS, preferred_element_type=jnp.float32)


def product_last(left, right):
    return lax.dot_general(left, right, CONTRACT_LAST, preferred_element_type=jnp.float32)


def gelu_exact(argument):
    return jax.nn.gelu(argument, approximate=False)


def attend_forward(queries, key_rows, values, block_rows):
    length, heads_here, head_size = queries.shape
    block_count = length // block_rows

    def one_block(query_block):
        scores = jnp.einsum(
            "qhd,khd->hqk", query_block, key_rows, preferred_element_type=jnp.float32
        )
        largest = jnp.max(scores, axis=-1, keepdims=True)
        weights = jnp.exp(scores - largest)
        exp_total = jnp.sum(weights, axis=-1, keepdims=True)
        probs_low = (weights / exp_total).astype(jnp.bfloat16)
        mixture = jnp.einsum("hqk,khd->qhd", probs_low, values, preferred_element_type=jnp.float32)
        log_total = (largest + jnp.log(exp_total))[..., 0]
        return (mixture.astype(jnp.bfloat16), log_total)

    mixture, log_totals = lax.map(
        one_block, queries.reshape(block_count, block_rows, heads_here, head_size)
    )
    return (mixture.reshape(length, heads_here * head_size), log_totals)


def attend_backward(queries, key_rows, values, mixture_low, log_totals, block_rows):
    length, heads_here, head_size = queries.shape
    block_count = length // block_rows

    def one_block(accumulated, inputs):
        key_sum, value_sum = accumulated
        query_block, grad_block, log_block = inputs
        scores = jnp.einsum(
            "qhd,khd->hqk", query_block, key_rows, preferred_element_type=jnp.float32
        )
        probability = jnp.exp(scores - log_block[..., None])
        probs_low = probability.astype(jnp.bfloat16)
        value_sum = value_sum + jnp.einsum(
            "hqk,qhd->khd", probs_low, grad_block, preferred_element_type=jnp.float32
        )
        prob_grad = jnp.einsum(
            "qhd,khd->hqk", grad_block, values, preferred_element_type=jnp.float32
        )
        inner_sum = jnp.sum(prob_grad * probability, axis=-1, keepdims=True)
        score_low = (probability * (prob_grad - inner_sum)).astype(jnp.bfloat16)
        query_low = jnp.einsum(
            "hqk,khd->qhd", score_low, key_rows, preferred_element_type=jnp.float32
        )
        key_sum = key_sum + jnp.einsum(
            "hqk,qhd->khd", score_low, query_block, preferred_element_type=jnp.float32
        )
        return ((key_sum, value_sum), query_low.astype(jnp.bfloat16))

    zeros = jnp.zeros((length, heads_here, head_size), jnp.float32)
    blocked = (length // block_count, heads_here, head_size)
    (key_sum, value_sum), query_low = lax.scan(
        one_block,
        (zeros, zeros),
        (
            queries.reshape((block_count,) + blocked),
            mixture_low.reshape((block_count,) + blocked),
            log_totals,
        ),
    )
    width_here = heads_here * head_size
    return (
        query_low.reshape(length, width_here),
        key_sum.astype(jnp.bfloat16).reshape(length, width_here),
        value_sum.astype(jnp.bfloat16).reshape(length, width_here),
    )


def body(
    layer_input,
    query_weight,
    key_weight,
    value_weight,
    mixing_weight,
    expand_weight,
    shrink_weight,
    query_offset,
    value_offset,
    mixing_offset,
    expand_offset,
    shrink_offset,
    first_gain,
    first_shift,
    second_gain,
    second_shift,
    cotangent,
):
    local_rows = layer_input.shape[0]
    tensor_size = lax.axis_size("tensor")
    length = local_rows * tensor_size
    block_rows = min(512, length)
    heads_here = query_weight.shape[1] // HD
    scaling = HD ** (-0.5)
    head_shape = (length, heads_here, HD)
    gathered = (
        lax.all_gather(query_weight, "dp", axis=0, tiled=True),
        lax.all_gather(key_weight, "dp", axis=0, tiled=True),
        lax.all_gather(value_weight, "dp", axis=0, tiled=True),
        lax.all_gather(mixing_weight, "dp", axis=1, tiled=True),
        lax.all_gather(expand_weight, "dp", axis=0, tiled=True),
        lax.all_gather(shrink_weight, "dp", axis=1, tiled=True),
    )
    query_full, key_full, value_full, mixing_full, expand_full, shrink_full = gathered
    sequence = lax.all_gather(layer_input, "tensor", axis=0, tiled=True)
    queries = ((product(sequence, query_full) + query_offset.astype(jnp.float32)) * scaling).astype(
        jnp.bfloat16
    )
    key_rows = product(sequence, key_full).astype(jnp.bfloat16)
    values = (product(sequence, value_full) + value_offset.astype(jnp.float32)).astype(jnp.bfloat16)
    mixture, log_totals = attend_forward(
        queries.reshape(head_shape),
        key_rows.reshape(head_shape),
        values.reshape(head_shape),
        block_rows,
    )
    attended_part = lax.psum_scatter(
        product(mixture, mixing_full).astype(jnp.bfloat16), "tensor", scatter_dimension=0, tiled=True
    )
    attended = layer_input.astype(jnp.float32) + attended_part + mixing_offset.astype(jnp.float32)
    first_norm, first_back = jax.vjp(
        layer_norm, attended, first_gain.astype(jnp.float32), first_shift.astype(jnp.float32)
    )
    normed = lax.all_gather(first_norm.astype(jnp.bfloat16), "tensor", axis=0, tiled=True)
    expanded = product(normed, expand_full) + expand_offset.astype(jnp.float32)
    hidden_act, gelu_back = jax.vjp(gelu_exact, expanded)
    hidden = hidden_act.astype(jnp.bfloat16)
    shrunk = lax.psum_scatter(
        product(hidden, shrink_full).astype(jnp.bfloat16), "tensor", scatter_dimension=0, tiled=True
    )
    summed = first_norm + shrunk + shrink_offset.astype(jnp.float32)
    normalized, second_back = jax.vjp(
        layer_norm, summed, second_gain.astype(jnp.float32), second_shift.astype(jnp.float32)
    )
    summed_grad, gain_second, shift_second = second_back(cotangent.astype(jnp.float32))
    query_back, key_back, value_back, mixing_back, expand_back, shrink_back = gathered
    branch_rows = lax.all_gather(summed_grad.astype(jnp.bfloat16), "tensor", axis=0, tiled=True)
    shrink_local = product_rows(hidden, branch_rows)
    hidden_grad = product_last(branch_rows, shrink_back)
    expanded_low = gelu_back(hidden_grad)[0].astype(jnp.bfloat16)
    expand_sum = jnp.sum(expanded_low.astype(jnp.float32), axis=0)
    expand_local = product_rows(normed, expanded_low)
    first_grad = (
        lax.psum_scatter(
            product_last(expanded_low, expand_back).astype(jnp.bfloat16), "tensor", scatter_dimension=0, tiled=True
        )
        + summed_grad
    )
    shrink_sum = jnp.sum(summed_grad, axis=0)
    attended_grad, gain_first, shift_first = first_back(first_grad)
    mixing_sum = jnp.sum(attended_grad, axis=0)
    attended_rows = lax.all_gather(attended_grad.astype(jnp.bfloat16), "tensor", axis=0, tiled=True)
    mixing_local = product_rows(mixture, attended_rows)
    mixture_low = product_last(attended_rows, mixing_back).astype(jnp.bfloat16)
    query_low, key_low, value_low = attend_backward(
        queries.reshape(head_shape),
        key_rows.reshape(head_shape),
        values.reshape(head_shape),
        mixture_low,
        log_totals,
        block_rows,
    )
    query_local = product_rows(sequence, query_low) * scaling
    key_local = product_rows(sequence, key_low)
    value_local = product_rows(sequence, value_low)
    query_sum = jnp.sum(query_low.astype(jnp.float32), axis=0) * scaling
    value_sum = jnp.sum(value_low.astype(jnp.float32), axis=0)
    input_grad = (
        lax.psum_scatter(
            (
                product_last(query_low, query_back) * scaling
                + product_last(key_low, key_back)
                + product_last(value_low, value_back)
            ).astype(jnp.bfloat16),
            "tensor",
            scatter_dimension=0,
            tiled=True,
        ).astype(jnp.float32)
        + attended_grad
    )
    query_grad, key_grad, value_grad, mixing_grad, expand_grad, shrink_grad = (
        lax.psum_scatter(query_local.astype(jnp.bfloat16), "dp", scatter_dimension=0, tiled=True).astype(jnp.float32),
        lax.psum_scatter(key_local.astype(jnp.bfloat16), "dp", scatter_dimension=0, tiled=True).astype(jnp.float32),
        lax.psum_scatter(value_local.astype(jnp.bfloat16), "dp", scatter_dimension=0, tiled=True).astype(jnp.float32),
        lax.psum_scatter(mixing_local.astype(jnp.bfloat16), "dp", scatter_dimension=1, tiled=True).astype(jnp.float32),
        lax.psum_scatter(expand_local.astype(jnp.bfloat16), "dp", scatter_dimension=0, tiled=True).astype(jnp.float32),
        lax.psum_scatter(shrink_local.astype(jnp.bfloat16), "dp", scatter_dimension=1, tiled=True).astype(jnp.float32),
    )
    tensor_index = lax.axis_index("tensor")
    selector = (jnp.arange(tensor_size)[:, None] == tensor_index).astype(jnp.float32)

    def spread_out(vector):
        return (selector * vector[None, :]).reshape(-1)

    totals = lax.psum(
        (
            gain_first,
            shift_first,
            gain_second,
            shift_second,
            mixing_sum,
            shrink_sum,
            spread_out(query_sum),
            spread_out(value_sum),
            spread_out(expand_sum),
        ),
        ("dp", "tensor"),
    )

    def own_slice(full_vector, slice_size):
        return lax.dynamic_slice_in_dim(full_vector, tensor_index * slice_size, slice_size, 0)

    offset_query = own_slice(totals[6], query_sum.shape[0])
    offset_value = own_slice(totals[7], value_sum.shape[0])
    offset_expand = own_slice(totals[8], expand_sum.shape[0])
    return (
        normalized.astype(jnp.bfloat16),
        input_grad,
        query_grad,
        key_grad,
        value_grad,
        mixing_grad,
        expand_grad,
        shrink_grad,
        offset_query,
        offset_value,
        totals[4],
        offset_expand,
        totals[5],
        totals[0],
        totals[1],
        totals[2],
        totals[3],
    )


def solution(mesh):
    placed = (
        P(("dp", "tensor"), None),
        P("dp", "tensor"),
        P("dp", "tensor"),
        P("dp", "tensor"),
        P("tensor", "dp"),
        P("dp", "tensor"),
        P("tensor", "dp"),
        P("tensor"),
        P("tensor"),
        P(),
        P("tensor"),
        P(),
        P(),
        P(),
        P(),
        P(),
        P(("dp", "tensor"), None),
    )
    return jax.shard_map(
        body,
        mesh=mesh,
        in_specs=placed,
        out_specs=(
            P(("dp", "tensor"), None),
            P(("dp", "tensor"), None),
            P("dp", "tensor"),
            P("dp", "tensor"),
            P("dp", "tensor"),
            P("tensor", "dp"),
            P("dp", "tensor"),
            P("tensor", "dp"),
            P("tensor"),
            P("tensor"),
            P(),
            P("tensor"),
            P(),
            P(),
            P(),
            P(),
            P(),
        ),
        check_vma=False,
    )
```

```python
import functools

import jax
import jax.numpy as jnp
from jax import lax
from jax.experimental import pallas as pl
from jax.experimental.pallas import tpu as pltpu
from jax.sharding import PartitionSpec as P

HD = 64
EPSILON = 1e-05
MESH = pl.DeviceIdType.MESH
BF = jnp.bfloat16
F32 = jnp.float32
NN = (((1,), (0,)), ((), ()))
NT = (((1,), (1,)), ((), ()))
TN = (((0,), (0,)), ((), ()))
VMEM_LIMIT = 60 * 1024 * 1024
TILE = 512


def mm(left, right, dims):
    return lax.dot_general(left, right, dims, preferred_element_type=F32)


def layer_norm(inputs, gain, shift):
    centered = inputs - jnp.mean(inputs, axis=-1, keepdims=True)
    variance = jnp.mean(centered * centered, axis=-1, keepdims=True)
    return centered * lax.rsqrt(variance + EPSILON) * gain + shift


def norm_parts(inputs):
    centered = inputs - jnp.mean(inputs, axis=-1, keepdims=True)
    variance = jnp.mean(centered * centered, axis=-1, keepdims=True)
    rate = lax.rsqrt(variance + EPSILON)
    return centered * rate, rate


def norm_back(upstream, gain, normal, rate):
    scaled = upstream * gain
    mean_scaled = jnp.mean(scaled, axis=-1, keepdims=True)
    mean_normal = jnp.mean(scaled * normal, axis=-1, keepdims=True)
    return rate * (scaled - mean_scaled - normal * mean_normal)


def column_sum(block):
    return jnp.sum(block, axis=0, keepdims=True)


def tiles(width, body):
    step = min(TILE, width)

    def one(index, carry):
        body(pl.ds(pl.multiple_of(index * step, step), step))
        return carry

    lax.fori_loop(0, width // step, one, 0)


def feed_kernel(
    chunks,
    attended_ref,
    cotangent_ref,
    expand_ref,
    shrink_ref,
    expand_offset_ref,
    vectors_ref,
    output_ref,
    attended_grad_ref,
    expand_grad_ref,
    shrink_grad_ref,
    expand_sum_ref,
    sums_ref,
    normed,
    hidden,
    slope,
    expanded_low,
    summed_low,
    own_part,
    summed_grad,
    send_part,
    recv_part,
    send_sem,
    recv_sem,
):
    rows, width = attended_ref.shape
    slices, _, units = expand_ref.shape
    step = rows // chunks
    t = lax.axis_index("tensor")
    partner = {"tensor": t ^ 1}
    first_gain = vectors_ref[0:1, :]
    first_shift = vectors_ref[1:2, :]
    second_gain = vectors_ref[2:3, :]
    second_shift = vectors_ref[3:4, :]
    shrink_offset = vectors_ref[4:5, :]

    def exchange(kind, chunk, source, target):
        return pltpu.make_async_remote_copy(
            src_ref=source,
            dst_ref=target,
            send_sem=send_sem.at[kind, chunk],
            recv_sem=recv_sem.at[kind, chunk],
            device_id=partner,
            device_id_type=MESH,
        )

    def own(chunk):
        return pl.ds(chunk * step, step)

    def other(chunk):
        return pl.ds(rows + chunk * step, step)

    copies = [
        [exchange(0, c, normed.at[own(c)], normed.at[other(c)]) for c in range(chunks)],
        [
            exchange(1, c, send_part.at[0, own(c)], recv_part.at[0, own(c)])
            for c in range(chunks)
        ],
        [exchange(2, c, summed_low.at[own(c)], summed_low.at[other(c)]) for c in range(chunks)],
        [
            exchange(3, c, send_part.at[1, own(c)], recv_part.at[1, own(c)])
            for c in range(chunks)
        ],
    ]

    barrier = pltpu.get_barrier_semaphore()
    pl.semaphore_signal(barrier, inc=1, device_id=partner, device_id_type=MESH)
    for c in range(chunks):
        normal, _ = norm_parts(attended_ref[own(c), :])
        normed[own(c), :] = (normal * first_gain + first_shift).astype(BF)
    pl.semaphore_wait(barrier, 1)
    for c in range(chunks):
        copies[0][c].start()

    def forward(place, store):
        for s in range(slices):

            def grow(tile):
                value = mm(normed[place, :], expand_ref[s, :, tile], NN)
                value = value + expand_offset_ref[s, :, tile]
                share = 0.5 * (1.0 + lax.erf(value * 0.7071067811865476))
                density = jnp.exp(-0.5 * value * value) * 0.3989422804014327
                hidden[s, place, tile] = (value * share).astype(BF)
                slope[s, place, tile] = (share + value * density).astype(BF)

            tiles(units, grow)

        def shrink(tile):
            total = mm(hidden[0, place, :], shrink_ref[0, tile, :], NT)
            for s in range(1, slices):
                total = total + mm(hidden[s, place, :], shrink_ref[s, tile, :], NT)
            store(tile, total)

        tiles(width, shrink)

    def backward(place, store):
        for s in range(slices):

            def narrow(tile):
                value = mm(summed_low[place, :], shrink_ref[s, :, tile], NN)
                value = value * slope[s, place, tile].astype(F32)
                expanded_low[s, place, tile] = value.astype(BF)

            tiles(units, narrow)

        def widen(tile):
            total = mm(expanded_low[0, place, :], expand_ref[0, tile, :], NT)
            for s in range(1, slices):
                total = total + mm(expanded_low[s, place, :], expand_ref[s, tile, :], NT)
            store(tile, total)

        tiles(width, widen)

    def keep(tile, total):
        own_part[:, tile] = total

    def pass_on(which, chunk):
        def store(tile, total):
            send_part[which, own(chunk), tile] = total.astype(BF)

        return store

    forward(pl.ds(0, rows), keep)
    for c in range(chunks):
        copies[0][c].wait_recv()
        forward(other(c), pass_on(0, c))
        copies[1][c].start()

    sums_ref[...] = jnp.zeros_like(sums_ref)
    for c in range(chunks):
        copies[1][c].wait_recv()
        normal, _ = norm_parts(attended_ref[own(c), :])
        first_norm = normal * first_gain + first_shift
        summed = (
            first_norm
            + (own_part[own(c), :] + recv_part[0, own(c), :].astype(F32))
            + shrink_offset
        )
        normal, rate = norm_parts(summed)
        output_ref[own(c), :] = (normal * second_gain + second_shift).astype(BF)
        upstream = cotangent_ref[own(c), :].astype(F32)
        grad = norm_back(upstream, second_gain, normal, rate)
        summed_grad[own(c), :] = grad
        summed_low[own(c), :] = grad.astype(BF)
        copies[2][c].start()
        sums_ref[0:1, :] += column_sum(upstream * normal)
        sums_ref[1:2, :] += column_sum(upstream)
        sums_ref[2:3, :] += column_sum(grad)

    backward(pl.ds(0, rows), keep)
    for c in range(chunks):
        copies[2][c].wait_recv()
        backward(other(c), pass_on(1, c))
        copies[3][c].start()

    for s in range(slices):

        def weigh(tile):
            left = min(TILE, width)
            for m in range(width // left):
                part = pl.ds(m * left, left)
                shrink_grad_ref[s, part, tile] = mm(
                    summed_low[:, part], hidden[s, :, tile], TN
                ).astype(BF)
                expand_grad_ref[s, part, tile] = mm(
                    normed[:, part], expanded_low[s, :, tile], TN
                ).astype(BF)
            expand_sum_ref[s, :, tile] = column_sum(expanded_low[s, :, tile].astype(F32))

        tiles(units, weigh)

    for c in range(chunks):
        copies[3][c].wait_recv()
        normal, rate = norm_parts(attended_ref[own(c), :])
        upstream = summed_grad[own(c), :] + (
            own_part[own(c), :] + recv_part[1, own(c), :].astype(F32)
        )
        grad = norm_back(upstream, first_gain, normal, rate)
        attended_grad_ref[own(c), :] = grad
        sums_ref[3:4, :] += column_sum(upstream * normal)
        sums_ref[4:5, :] += column_sum(upstream)
        sums_ref[5:6, :] += column_sum(grad)
    for kind in range(4):
        for c in range(chunks):
            copies[kind][c].wait_send()


def feed_forward(attended, cotangent, expand, shrink, expand_offset, vectors):
    rows, width = attended.shape
    slices, _, units = expand.shape
    chunks = 2
    vmem = pl.BlockSpec(memory_space=pltpu.VMEM)
    both = 2 * rows
    return pl.pallas_call(
        functools.partial(feed_kernel, chunks),
        out_shape=(
            jax.ShapeDtypeStruct((rows, width), BF),
            jax.ShapeDtypeStruct((rows, width), F32),
            jax.ShapeDtypeStruct((slices, width, units), BF),
            jax.ShapeDtypeStruct((slices, width, units), BF),
            jax.ShapeDtypeStruct((slices, 1, units), F32),
            jax.ShapeDtypeStruct((8, width), F32),
        ),
        in_specs=[vmem] * 6,
        out_specs=[vmem] * 6,
        scratch_shapes=[
            pltpu.VMEM((both, width), BF),
            pltpu.VMEM((slices, both, units), BF),
            pltpu.VMEM((slices, both, units), BF),
            pltpu.VMEM((slices, both, units), BF),
            pltpu.VMEM((both, width), BF),
            pltpu.VMEM((rows, width), F32),
            pltpu.VMEM((rows, width), F32),
            pltpu.VMEM((2, rows, width), BF),
            pltpu.VMEM((2, rows, width), BF),
            pltpu.SemaphoreType.DMA((4, chunks)),
            pltpu.SemaphoreType.DMA((4, chunks)),
        ],
        compiler_params=pltpu.CompilerParams(
            collective_id=1, has_side_effects=True, vmem_limit_bytes=VMEM_LIMIT
        ),
    )(attended, cotangent, expand, shrink, expand_offset, vectors)


def product(left, right):
    return jnp.dot(left, right, preferred_element_type=F32)


def product_rows(left, right):
    return lax.dot_general(left, right, TN, preferred_element_type=F32)


def product_last(left, right):
    return lax.dot_general(left, right, NT, preferred_element_type=F32)


def attend_forward(queries, key_rows, values, block_rows):
    length, heads_here, head_size = queries.shape
    block_count = length // block_rows

    def one_block(query_block):
        scores = jnp.einsum("qhd,khd->hqk", query_block, key_rows, preferred_element_type=F32)
        largest = jnp.max(scores, axis=-1, keepdims=True)
        weights = jnp.exp(scores - largest)
        exp_total = jnp.sum(weights, axis=-1, keepdims=True)
        probs_low = (weights / exp_total).astype(BF)
        mixture = jnp.einsum("hqk,khd->qhd", probs_low, values, preferred_element_type=F32)
        log_total = (largest + jnp.log(exp_total))[..., 0]
        return (mixture.astype(BF), log_total)

    mixture, log_totals = lax.map(
        one_block, queries.reshape(block_count, block_rows, heads_here, head_size)
    )
    return (mixture.reshape(length, heads_here * head_size), log_totals)


def attend_backward(queries, key_rows, values, mixture_low, log_totals, block_rows):
    length, heads_here, head_size = queries.shape
    block_count = length // block_rows

    def one_block(accumulated, inputs):
        key_sum, value_sum = accumulated
        query_block, grad_block, log_block = inputs
        scores = jnp.einsum("qhd,khd->hqk", query_block, key_rows, preferred_element_type=F32)
        probability = jnp.exp(scores - log_block[..., None])
        probs_low = probability.astype(BF)
        value_sum = value_sum + jnp.einsum(
            "hqk,qhd->khd", probs_low, grad_block, preferred_element_type=F32
        )
        prob_grad = jnp.einsum("qhd,khd->hqk", grad_block, values, preferred_element_type=F32)
        inner_sum = jnp.sum(prob_grad * probability, axis=-1, keepdims=True)
        score_low = (probability * (prob_grad - inner_sum)).astype(BF)
        query_low = jnp.einsum("hqk,khd->qhd", score_low, key_rows, preferred_element_type=F32)
        key_sum = key_sum + jnp.einsum(
            "hqk,qhd->khd", score_low, query_block, preferred_element_type=F32
        )
        return ((key_sum, value_sum), query_low.astype(BF))

    zeros = jnp.zeros((length, heads_here, head_size), F32)
    blocked = (length // block_count, heads_here, head_size)
    (key_sum, value_sum), query_low = lax.scan(
        one_block,
        (zeros, zeros),
        (
            queries.reshape((block_count,) + blocked),
            mixture_low.reshape((block_count,) + blocked),
            log_totals,
        ),
    )
    width_here = heads_here * head_size
    return (
        query_low.reshape(length, width_here),
        key_sum.astype(BF).reshape(length, width_here),
        value_sum.astype(BF).reshape(length, width_here),
    )


def scatter_sum(partial, axis):
    return lax.psum_scatter(
        partial.astype(BF), "dp", scatter_dimension=axis, tiled=True
    ).astype(F32)


def body(
    layer_input,
    query_weight,
    key_weight,
    value_weight,
    mixing_weight,
    expand_weight,
    shrink_weight,
    query_offset,
    value_offset,
    mixing_offset,
    expand_offset,
    shrink_offset,
    first_gain,
    first_shift,
    second_gain,
    second_shift,
    cotangent,
):
    local_rows = layer_input.shape[0]
    tensor_size = lax.axis_size("tensor")
    length = local_rows * tensor_size
    block_rows = min(512, length)
    heads_here = query_weight.shape[1] // HD
    scaling = HD ** (-0.5)
    head_shape = (length, heads_here, HD)
    swap = [(i, i ^ 2) for i in range(tensor_size)]

    def pair(shard):
        return jnp.stack([shard, lax.ppermute(shard, "tensor", swap)])

    query_full = lax.all_gather(query_weight, "dp", axis=0, tiled=True)
    key_full = lax.all_gather(key_weight, "dp", axis=0, tiled=True)
    value_full = lax.all_gather(value_weight, "dp", axis=0, tiled=True)
    mixing_full = lax.all_gather(mixing_weight, "dp", axis=1, tiled=True)
    expand_full = lax.all_gather(pair(expand_weight), "dp", axis=1, tiled=True)
    shrink_full = lax.all_gather(pair(shrink_weight.T), "dp", axis=1, tiled=True)
    offset_pair = pair(expand_offset.astype(F32)[None, :])
    sequence = lax.all_gather(layer_input, "tensor", axis=0, tiled=True)
    queries = ((product(sequence, query_full) + query_offset.astype(F32)) * scaling).astype(BF)
    key_rows = product(sequence, key_full).astype(BF)
    values = (product(sequence, value_full) + value_offset.astype(F32)).astype(BF)
    mixture, log_totals = attend_forward(
        queries.reshape(head_shape),
        key_rows.reshape(head_shape),
        values.reshape(head_shape),
        block_rows,
    )
    attended_part = lax.psum_scatter(
        product(mixture, mixing_full).astype(BF), "tensor", scatter_dimension=0, tiled=True
    )
    attended = layer_input.astype(F32) + attended_part + mixing_offset.astype(F32)
    zero = jnp.zeros_like(first_gain)
    vectors = jnp.stack(
        [first_gain, first_shift, second_gain, second_shift, shrink_offset, zero, zero, zero]
    ).astype(F32)
    output, attended_grad, expand_local, shrink_local, expand_sum, sums = feed_forward(
        attended, cotangent, expand_full, shrink_full, offset_pair, vectors
    )
    attended_rows = lax.all_gather(attended_grad.astype(BF), "tensor", axis=0, tiled=True)
    mixing_local = product_rows(mixture, attended_rows)
    mixture_low = product_last(attended_rows, mixing_full).astype(BF)
    query_low, key_low, value_low = attend_backward(
        queries.reshape(head_shape),
        key_rows.reshape(head_shape),
        values.reshape(head_shape),
        mixture_low,
        log_totals,
        block_rows,
    )
    query_local = product_rows(sequence, query_low) * scaling
    key_local = product_rows(sequence, key_low)
    value_local = product_rows(sequence, value_low)
    query_sum = jnp.sum(query_low.astype(F32), axis=0) * scaling
    value_sum = jnp.sum(value_low.astype(F32), axis=0)
    input_grad = (
        lax.psum_scatter(
            (
                product_last(query_low, query_full) * scaling
                + product_last(key_low, key_full)
                + product_last(value_low, value_full)
            ).astype(BF),
            "tensor",
            scatter_dimension=0,
            tiled=True,
        ).astype(F32)
        + attended_grad
    )
    query_grad = scatter_sum(query_local, 0)
    key_grad = scatter_sum(key_local, 0)
    value_grad = scatter_sum(value_local, 0)
    mixing_grad = scatter_sum(mixing_local, 1)
    expand_parts = lax.psum_scatter(expand_local, "dp", scatter_dimension=1, tiled=True)
    shrink_parts = lax.psum_scatter(shrink_local, "dp", scatter_dimension=1, tiled=True)

    def join(parts):
        theirs = lax.ppermute(parts[1], "tensor", swap)
        return parts[0].astype(F32) + theirs.astype(F32)

    expand_grad = join(expand_parts)
    shrink_grad = join(shrink_parts).T
    tensor_index = lax.axis_index("tensor")

    def spread_out(vector, index):
        selector = (jnp.arange(tensor_size)[:, None] == index).astype(F32)
        return (selector * vector[None, :]).reshape(-1)

    totals = lax.psum(
        (
            sums,
            spread_out(query_sum, tensor_index),
            spread_out(value_sum, tensor_index),
            spread_out(expand_sum[0, 0], tensor_index)
            + spread_out(expand_sum[1, 0], tensor_index ^ 2),
        ),
        ("dp", "tensor"),
    )

    def own_slice(full_vector, slice_size):
        return lax.dynamic_slice_in_dim(full_vector, tensor_index * slice_size, slice_size, 0)

    offset_query = own_slice(totals[1], query_sum.shape[0])
    offset_value = own_slice(totals[2], value_sum.shape[0])
    offset_expand = own_slice(totals[3], expand_offset.shape[0])
    sums = totals[0]
    return (
        output,
        input_grad,
        query_grad,
        key_grad,
        value_grad,
        mixing_grad,
        expand_grad,
        shrink_grad,
        offset_query,
        offset_value,
        sums[5],
        offset_expand,
        sums[2],
        sums[3],
        sums[4],
        sums[0],
        sums[1],
    )


def solution(mesh):
    rows = P(("dp", "tensor"), None)
    tall = P("dp", "tensor")
    wide = P("tensor", "dp")
    split = P("tensor")
    whole = P()
    return jax.shard_map(
        body,
        mesh=mesh,
        in_specs=(rows, tall, tall, tall, wide, tall, wide, split, split)
        + (whole, split, whole, whole, whole, whole, whole, rows),
        out_specs=(rows, rows, tall, tall, tall, wide, tall, wide, split, split)
        + (whole, split, whole, whole, whole, whole, whole),
        check_vma=False,
    )
```

```python
import functools

import jax
import jax.numpy as jnp
from jax import lax
from jax.experimental import pallas as pl
from jax.experimental.pallas import tpu as pltpu
from jax.sharding import PartitionSpec as P

HD = 64
EPSILON = 1e-05
MESH = pl.DeviceIdType.MESH
BF = jnp.bfloat16
F32 = jnp.float32
NN = (((1,), (0,)), ((), ()))
NT = (((1,), (1,)), ((), ()))
TN = (((0,), (0,)), ((), ()))
VMEM_LIMIT = 60 * 1024 * 1024
TILE = 512


def mm(left, right, dims):
    return lax.dot_general(left, right, dims, preferred_element_type=F32)


def layer_norm(inputs, gain, shift):
    centered = inputs - jnp.mean(inputs, axis=-1, keepdims=True)
    variance = jnp.mean(centered * centered, axis=-1, keepdims=True)
    return centered * lax.rsqrt(variance + EPSILON) * gain + shift


def norm_parts(inputs):
    centered = inputs - jnp.mean(inputs, axis=-1, keepdims=True)
    variance = jnp.mean(centered * centered, axis=-1, keepdims=True)
    rate = lax.rsqrt(variance + EPSILON)
    return centered * rate, rate


def norm_back(upstream, gain, normal, rate):
    scaled = upstream * gain
    mean_scaled = jnp.mean(scaled, axis=-1, keepdims=True)
    mean_normal = jnp.mean(scaled * normal, axis=-1, keepdims=True)
    return rate * (scaled - mean_scaled - normal * mean_normal)


def column_sum(block):
    return jnp.sum(block, axis=0, keepdims=True)


def tiles(width, body):
    step = min(TILE, width)

    def one(index, carry):
        body(pl.ds(pl.multiple_of(index * step, step), step))
        return carry

    lax.fori_loop(0, width // step, one, 0)


def chosen(table, index):
    value = jnp.int32(table[0])
    for place in range(1, len(table)):
        value = jnp.where(index == place, jnp.int32(table[place]), value)
    return value


def each(count, start, body):
    if count - start <= 8:
        for index in range(start, count):
            body(index)
        return

    def one(index, carry):
        body(index)
        return carry

    lax.fori_loop(start, count, one, 0)


class Place:
    def __init__(self, devices, ranks):
        self.d = lax.axis_index("dp")
        self.t = lax.axis_index("tensor")
        self.chips = devices // 2
        self.ranks = ranks
        self.c = self.d % 2
        self.p = self.d // 2

    def chip(self, k):
        return {"dp": 2 * (self.p ^ k) + self.c}

    def core(self):
        return {"dp": self.d ^ 1}

    def rank(self, t):
        return {"tensor": t}


def remote(source, target, sems, index, device):
    send, recv = sems
    return pltpu.make_async_remote_copy(
        src_ref=source,
        dst_ref=target,
        send_sem=send.at[index],
        recv_sem=recv.at[index],
        device_id=device,
        device_id_type=MESH,
    )


class Gather:
    def __init__(self, here, view, chip_sems, core_sems):
        self.here, self.view = here, view
        self.chip_sems, self.core_sems = chip_sems, core_sems

    def chip_copy(self, k):
        here = self.here
        mine = self.view(2 * here.p + here.c)
        return remote(mine, mine, self.chip_sems, k, here.chip(k))

    def chip_arrival(self, k):
        here = self.here
        theirs = self.view(2 * (here.p ^ k) + here.c)
        return remote(theirs, theirs, self.chip_sems, k, here.chip(k))

    def core_copy(self, k):
        here = self.here
        shard = self.view(2 * (here.p ^ k) + here.c)
        return remote(shard, shard, self.core_sems, k, here.core())

    def core_arrival(self, k):
        here = self.here
        shard = self.view(2 * (here.p ^ k) + 1 - here.c)
        return remote(shard, shard, self.core_sems, k, here.core())

    def start(self):
        each(self.here.chips, 1, lambda k: self.chip_copy(k).start())
        self.core_copy(0).start()

    def forward(self):
        def one(k):
            self.chip_arrival(k).wait_recv()
            self.core_copy(k).start()

        each(self.here.chips, 1, one)

    def finish(self):
        each(self.here.chips, 0, lambda k: self.core_arrival(k).wait_recv())

    def drain(self):
        each(self.here.chips, 1, lambda k: self.chip_copy(k).wait_send())
        each(self.here.chips, 0, lambda k: self.core_copy(k).wait_send())


def layer_kernel(
    devices,
    chunks,
    input_ref,
    query_ref,
    key_ref,
    value_ref,
    mixing_ref,
    expand_ref,
    shrink_ref,
    head_offset_ref,
    expand_offset_ref,
    vectors_ref,
    cotangent_ref,
    output_ref,
    attended_grad_ref,
    expand_grad_ref,
    shrink_grad_ref,
    expand_sum_ref,
    sums_ref,
    sequence,
    queries,
    key_rows,
    values,
    mixed,
    log_totals,
    head_full,
    mixing_full,
    feed_full,
    offset_full,
    key_columns,
    value_columns,
    mix_heads,
    attended_ref,
    normed,
    hidden,
    slope,
    expanded_low,
    summed_low,
    own_part,
    summed_grad,
    send_part,
    recv_part,
    row_send,
    row_recv,
    mix_send,
    mix_recv,
    weight_send,
    weight_recv,
    pair_send,
    pair_recv,
    chip_send,
    chip_recv,
    core_send,
    core_recv,
    swap_send,
    swap_recv,
):
    ranks, rows, width = sequence.shape
    shard = query_ref.shape[0]
    span = query_ref.shape[1]
    heads = span // HD
    units = expand_ref.shape[1]
    slices = 2
    step = rows // chunks
    length = ranks * rows
    here = Place(devices, ranks)
    d, t, chips = here.d, here.t, here.chips
    last = ranks - 1
    middle = jnp.logical_and(t > 0, t < last)
    partner = here.rank(t ^ 1)
    first_gain = vectors_ref[0:1, :]
    first_shift = vectors_ref[1:2, :]
    second_gain = vectors_ref[2:3, :]
    second_shift = vectors_ref[3:4, :]
    shrink_offset = vectors_ref[4:5, :]
    mixing_offset = vectors_ref[5:6, :]

    barrier = pltpu.get_barrier_semaphore()
    for k in range(1, ranks):
        pl.semaphore_signal(barrier, inc=1, device_id=here.rank(t ^ k), device_id_type=MESH)
    each(
        chips,
        1,
        lambda k: pl.semaphore_signal(
            barrier, inc=1, device_id=here.chip(k), device_id_type=MESH
        ),
    )
    pl.semaphore_signal(barrier, inc=1, device_id=here.core(), device_id_type=MESH)

    mine = pl.ds(pl.multiple_of(d * shard, shard), shard)
    sequence[t] = input_ref[...]
    head_full[0, mine, :] = query_ref[...]
    head_full[1, mine, :] = key_ref[...]
    head_full[2, mine, :] = value_ref[...]
    mixing_full[t, mine, :] = mixing_ref[...]
    feed_full[0, 0, mine, :] = expand_ref[...]
    feed_full[0, 1, mine, :] = shrink_ref[...]
    offset_full[0] = expand_offset_ref[...]

    pl.semaphore_wait(barrier, ranks - 1 + chips - 1 + 1)

    def shard_rows(index):
        return pl.ds(pl.multiple_of(index * shard, shard), shard)

    def gather(number, view):
        return Gather(
            here,
            view,
            (chip_send.at[number], chip_recv.at[number]),
            (core_send.at[number], core_recv.at[number]),
        )

    heads_gather = gather(0, lambda i: head_full.at[:, shard_rows(i)])
    mixing_gather = gather(1, lambda i: mixing_full.at[:, shard_rows(i)])
    feed_gathers = [
        gather(2 + s, lambda i, s=s: feed_full.at[s, :, shard_rows(i)]) for s in range(slices)
    ]

    row_sems = (row_send, row_recv)

    def row_copy(s, side):
        block = sequence.at[s]
        return pltpu.make_async_remote_copy(
            src_ref=block,
            dst_ref=block,
            send_sem=row_send.at[side, s],
            recv_sem=row_recv.at[s],
            device_id=here.rank(jnp.clip(t + (1 if side else -1), 0, last)),
            device_id_type=MESH,
        )

    @pl.when(t < last)
    def _():
        row_copy(t, 1).start()

    @pl.when(t > 0)
    def _():
        row_copy(t, 0).start()

    heads_gather.start()
    heads_gather.forward()
    feed_gathers[0].start()
    heads_gather.finish()

    def project(s):
        block = sequence[s]
        place = pl.ds(pl.multiple_of(s * rows, rows), rows)
        query = (mm(block, head_full[0], NN) + head_offset_ref[0:1, :]) * (HD**-0.5)
        queries[s] = query.astype(BF)
        key = mm(block, head_full[1], NN)
        key_rows[place, :] = key.astype(BF)
        value = mm(block, head_full[2], NN) + head_offset_ref[1:2, :]
        values[place, :] = value.astype(BF)
        value_columns[:, place] = value.T.astype(BF)
        key_columns[:, place] = key.T.astype(BF)

    project(t)

    def weight_copy(k):
        return remote(
            mixing_full.at[t, mine],
            mixing_full.at[t, mine],
            (weight_send, weight_recv),
            k,
            here.rank(t ^ k),
        )

    def weight_arrival(k):
        theirs = mixing_full.at[t ^ k, mine]
        return remote(theirs, theirs, (weight_send, weight_recv), k, here.rank(t ^ k))

    pair_copies = [
        remote(
            feed_full.at[0, :, mine],
            feed_full.at[1, :, mine],
            (pair_send, pair_recv),
            0,
            here.rank(t ^ 2),
        ),
        remote(
            offset_full.at[0], offset_full.at[1], (pair_send, pair_recv), 1, here.rank(t ^ 2)
        ),
    ]

    def start_pairs():
        for k in range(1, ranks):
            weight_copy(k).start()
        for copy in pair_copies:
            copy.start()

    near = [
        [s for _, s in sorted((abs(s - u), s) for s in range(ranks) if s != u)]
        for u in range(ranks)
    ]
    for j in range(ranks - 1):
        s = chosen([near[u][j] for u in range(ranks)], t)
        row_copy(s, 0).wait_recv()

        @pl.when(jnp.logical_and(s < t, t < last))
        def _():
            row_copy(s, 1).start()

        @pl.when(jnp.logical_and(s > t, t > 0))
        def _():
            row_copy(s, 0).start()

        if j == 1:

            @pl.when(jnp.logical_not(middle))
            def _():
                start_pairs()

        project(s)

    def mix_copy(s):
        return pltpu.make_async_remote_copy(
            src_ref=mix_heads.at[s],
            dst_ref=mixed.at[t],
            send_sem=mix_send.at[s],
            recv_sem=mix_recv.at[t],
            device_id=here.rank(s),
            device_id_type=MESH,
        )

    def mix_arrival(s):
        return pltpu.make_async_remote_copy(
            src_ref=mix_heads.at[s],
            dst_ref=mixed.at[s],
            send_sem=mix_send.at[s],
            recv_sem=mix_recv.at[s],
            device_id=here.rank(s),
            device_id_type=MESH,
        )

    lane = lax.broadcasted_iota(jnp.int32, (1, 128), 1)

    def attend(s):
        place = pl.ds(pl.multiple_of(s * rows, rows), rows)
        columns = []
        for h in range(heads):
            pair = slice(128 * (h // 2), 128 * (h // 2) + 128)
            side = (lane // HD) == (h % 2)
            query = jnp.where(side, queries[s, :, pair], jnp.zeros((), BF))
            scores = mm(key_rows[:, pair], query, NT)
            largest = jnp.max(scores, axis=0, keepdims=True)
            weights = jnp.exp(scores - largest)
            total = jnp.sum(weights, axis=0, keepdims=True)
            column = mm(value_columns[h * HD : (h + 1) * HD, :], weights.astype(BF), NN)
            columns.append(column / total)
            log_totals[h : h + 1, place] = largest + jnp.log(total)
        mix_heads[s] = jnp.concatenate(columns, axis=0).T.astype(BF)

    far = [[s for s in reversed(near[u])] + [u] for u in range(ranks)]
    for j in range(ranks):
        s = chosen([far[u][j] for u in range(ranks)], t)
        attend(s)
        if j < ranks - 1:
            mix_copy(s).start()
        if j == 0:

            @pl.when(middle)
            def _():
                start_pairs()

        if j == 1:
            feed_gathers[0].forward()
    mixed[t] = mix_heads[t]

    for k in range(1, ranks):
        weight_arrival(k).wait_recv()
    mixing_gather.start()
    for copy in pair_copies:
        copy.wait_recv()
    feed_gathers[1].start()
    for k in range(1, ranks):
        mix_arrival(t ^ k).wait_recv()
    mixing_gather.forward()
    mixing_gather.finish()

    def mix_tile(tile):
        total = input_ref[:, tile].astype(F32) + vectors_ref[5:6, tile]
        for j in range(ranks):
            total = total + mm(mixed[j], mixing_full[j, tile, :], NT)
        attended_ref[:, tile] = total

    tiles(width, mix_tile)

    def own(chunk):
        return pl.ds(chunk * step, step)

    def other(chunk):
        return pl.ds(rows + chunk * step, step)

    def exchange(kind, chunk, source, target):
        return pltpu.make_async_remote_copy(
            src_ref=source,
            dst_ref=target,
            send_sem=swap_send.at[kind, chunk],
            recv_sem=swap_recv.at[kind, chunk],
            device_id=partner,
            device_id_type=MESH,
        )

    copies = [
        [exchange(0, c, normed.at[own(c)], normed.at[other(c)]) for c in range(chunks)],
        [exchange(1, c, send_part.at[0, own(c)], recv_part.at[0, own(c)]) for c in range(chunks)],
        [exchange(2, c, summed_low.at[own(c)], summed_low.at[other(c)]) for c in range(chunks)],
        [exchange(3, c, send_part.at[1, own(c)], recv_part.at[1, own(c)]) for c in range(chunks)],
    ]
    for c in range(chunks):
        normal, _ = norm_parts(attended_ref[own(c), :])
        normed[own(c), :] = (normal * first_gain + first_shift).astype(BF)
        copies[0][c].start()

    def forward(place, store, ready):
        for s in range(slices):
            ready(s)

            def grow(tile):
                value = mm(normed[place, :], feed_full[s, 0, :, tile], NN)
                value = value + offset_full[s, :, tile]
                share = 0.5 * (1.0 + lax.erf(value * 0.7071067811865476))
                density = jnp.exp(-0.5 * value * value) * 0.3989422804014327
                hidden[s, place, tile] = (value * share).astype(BF)
                slope[s, place, tile] = (share + value * density).astype(BF)

            tiles(units, grow)

        def shrink(tile):
            total = mm(hidden[0, place, :], feed_full[0, 1, tile, :], NT)
            for s in range(1, slices):
                total = total + mm(hidden[s, place, :], feed_full[s, 1, tile, :], NT)
            store(tile, total)

        tiles(width, shrink)

    def backward(place, store):
        for s in range(slices):

            def narrow(tile):
                value = mm(summed_low[place, :], feed_full[s, 1, :, tile], NN)
                value = value * slope[s, place, tile].astype(F32)
                expanded_low[s, place, tile] = value.astype(BF)

            tiles(units, narrow)

        def widen(tile):
            total = mm(expanded_low[0, place, :], feed_full[0, 0, tile, :], NT)
            for s in range(1, slices):
                total = total + mm(expanded_low[s, place, :], feed_full[s, 0, tile, :], NT)
            store(tile, total)

        tiles(width, widen)

    def keep(tile, total):
        own_part[:, tile] = total

    def pass_on(which, chunk):
        def store(tile, total):
            send_part[which, own(chunk), tile] = total.astype(BF)

        return store

    def arrive(s):
        if s == 0:
            feed_gathers[0].finish()
        else:
            feed_gathers[s].forward()
            feed_gathers[s].finish()

    forward(pl.ds(0, rows), keep, arrive)
    for c in range(chunks):
        copies[0][c].wait_recv()
        forward(other(c), pass_on(0, c), lambda s: None)
        copies[1][c].start()

    sums_ref[...] = jnp.zeros_like(sums_ref)
    for c in range(chunks):
        copies[1][c].wait_recv()
        normal, _ = norm_parts(attended_ref[own(c), :])
        first_norm = normal * first_gain + first_shift
        summed = (
            first_norm
            + (own_part[own(c), :] + recv_part[0, own(c), :].astype(F32))
            + shrink_offset
        )
        normal, rate = norm_parts(summed)
        output_ref[own(c), :] = (normal * second_gain + second_shift).astype(BF)
        upstream = cotangent_ref[own(c), :].astype(F32)
        grad = norm_back(upstream, second_gain, normal, rate)
        summed_grad[own(c), :] = grad
        summed_low[own(c), :] = grad.astype(BF)
        copies[2][c].start()
        sums_ref[0:1, :] += column_sum(upstream * normal)
        sums_ref[1:2, :] += column_sum(upstream)
        sums_ref[2:3, :] += column_sum(grad)

    backward(pl.ds(0, rows), keep)
    for c in range(chunks):
        copies[2][c].wait_recv()
        backward(other(c), pass_on(1, c))
        copies[3][c].start()

    for s in range(slices):

        def weigh(tile):
            left = min(TILE, width)
            for m in range(width // left):
                part = pl.ds(m * left, left)
                shrink_grad_ref[s, part, tile] = mm(
                    summed_low[:, part], hidden[s, :, tile], TN
                ).astype(BF)
                expand_grad_ref[s, part, tile] = mm(
                    normed[:, part], expanded_low[s, :, tile], TN
                ).astype(BF)
            expand_sum_ref[s, :, tile] = column_sum(expanded_low[s, :, tile].astype(F32))

        tiles(units, weigh)

    for c in range(chunks):
        copies[3][c].wait_recv()
        normal, rate = norm_parts(attended_ref[own(c), :])
        upstream = summed_grad[own(c), :] + (
            own_part[own(c), :] + recv_part[1, own(c), :].astype(F32)
        )
        grad = norm_back(upstream, first_gain, normal, rate)
        attended_grad_ref[own(c), :] = grad
        sums_ref[3:4, :] += column_sum(upstream * normal)
        sums_ref[4:5, :] += column_sum(upstream)
        sums_ref[5:6, :] += column_sum(grad)

    for kind in range(4):
        for c in range(chunks):
            copies[kind][c].wait_send()
    for each_gather in [heads_gather, mixing_gather] + feed_gathers:
        each_gather.drain()
    for copy in pair_copies:
        copy.wait_send()
    for k in range(1, ranks):
        weight_copy(k).wait_send()
        mix_copy(t ^ k).wait_send()
    for s in range(ranks):

        @pl.when(jnp.logical_and(s <= t, t < last))
        def _():
            row_copy(s, 1).wait_send()

        @pl.when(jnp.logical_and(s >= t, t > 0))
        def _():
            row_copy(s, 0).wait_send()


def layer(devices, ranks, inputs):
    layer_input = inputs[0]
    rows, width = layer_input.shape
    span = inputs[1].shape[1]
    units = inputs[5].shape[1]
    slices = 2
    chunks = 2
    chips = devices // 2
    length = ranks * rows
    both = 2 * rows
    vmem = pl.BlockSpec(memory_space=pltpu.VMEM)
    dma = pltpu.SemaphoreType.DMA
    outs = (
        jax.ShapeDtypeStruct((rows, width), BF),
        jax.ShapeDtypeStruct((rows, width), F32),
        jax.ShapeDtypeStruct((slices, width, units), BF),
        jax.ShapeDtypeStruct((slices, width, units), BF),
        jax.ShapeDtypeStruct((slices, 1, units), F32),
        jax.ShapeDtypeStruct((8, width), F32),
        jax.ShapeDtypeStruct((ranks, rows, width), BF),
        jax.ShapeDtypeStruct((ranks, rows, span), BF),
        jax.ShapeDtypeStruct((length, span), BF),
        jax.ShapeDtypeStruct((length, span), BF),
        jax.ShapeDtypeStruct((ranks, rows, span), BF),
        jax.ShapeDtypeStruct((8, length), F32),
        jax.ShapeDtypeStruct((3, width, span), BF),
        jax.ShapeDtypeStruct((ranks, width, span), BF),
    )
    return pl.pallas_call(
        functools.partial(layer_kernel, devices, chunks),
        out_shape=outs,
        in_specs=[vmem] * len(inputs),
        out_specs=[vmem] * len(outs),
        scratch_shapes=[
            pltpu.VMEM((slices, 2, width, units), BF),
            pltpu.VMEM((slices, 1, units), F32),
            pltpu.VMEM((span, length), BF),
            pltpu.VMEM((span, length), BF),
            pltpu.VMEM((ranks, rows, span), BF),
            pltpu.VMEM((rows, width), F32),
            pltpu.VMEM((both, width), BF),
            pltpu.VMEM((slices, both, units), BF),
            pltpu.VMEM((slices, both, units), BF),
            pltpu.VMEM((slices, both, units), BF),
            pltpu.VMEM((both, width), BF),
            pltpu.VMEM((rows, width), F32),
            pltpu.VMEM((rows, width), F32),
            pltpu.VMEM((2, rows, width), BF),
            pltpu.VMEM((2, rows, width), BF),
            dma((2, ranks)),
            dma((ranks,)),
            dma((ranks,)),
            dma((ranks,)),
            dma((ranks,)),
            dma((ranks,)),
            dma((2,)),
            dma((2,)),
            dma((4, chips)),
            dma((4, chips)),
            dma((4, chips)),
            dma((4, chips)),
            dma((4, chunks)),
            dma((4, chunks)),
        ],
        compiler_params=pltpu.CompilerParams(
            collective_id=1, has_side_effects=True, vmem_limit_bytes=VMEM_LIMIT
        ),
    )(*inputs)


def product(left, right):
    return jnp.dot(left, right, preferred_element_type=F32)


def product_rows(left, right):
    return lax.dot_general(left, right, TN, preferred_element_type=F32)


def product_last(left, right):
    return lax.dot_general(left, right, NT, preferred_element_type=F32)


def attend_forward(queries, key_rows, values, block_rows):
    length, heads_here, head_size = queries.shape
    block_count = length // block_rows

    def one_block(query_block):
        scores = jnp.einsum("qhd,khd->hqk", query_block, key_rows, preferred_element_type=F32)
        largest = jnp.max(scores, axis=-1, keepdims=True)
        weights = jnp.exp(scores - largest)
        exp_total = jnp.sum(weights, axis=-1, keepdims=True)
        probs_low = (weights / exp_total).astype(BF)
        mixture = jnp.einsum("hqk,khd->qhd", probs_low, values, preferred_element_type=F32)
        log_total = (largest + jnp.log(exp_total))[..., 0]
        return (mixture.astype(BF), log_total)

    mixture, log_totals = lax.map(
        one_block, queries.reshape(block_count, block_rows, heads_here, head_size)
    )
    return (mixture.reshape(length, heads_here * head_size), log_totals)


def attend_backward(queries, key_rows, values, mixture_low, log_totals, block_rows):
    length, heads_here, head_size = queries.shape
    block_count = length // block_rows

    def one_block(accumulated, inputs):
        key_sum, value_sum = accumulated
        query_block, grad_block, log_block = inputs
        scores = jnp.einsum("qhd,khd->hqk", query_block, key_rows, preferred_element_type=F32)
        probability = jnp.exp(scores - log_block[..., None])
        probs_low = probability.astype(BF)
        value_sum = value_sum + jnp.einsum(
            "hqk,qhd->khd", probs_low, grad_block, preferred_element_type=F32
        )
        prob_grad = jnp.einsum("qhd,khd->hqk", grad_block, values, preferred_element_type=F32)
        inner_sum = jnp.sum(prob_grad * probability, axis=-1, keepdims=True)
        score_low = (probability * (prob_grad - inner_sum)).astype(BF)
        query_low = jnp.einsum("hqk,khd->qhd", score_low, key_rows, preferred_element_type=F32)
        key_sum = key_sum + jnp.einsum(
            "hqk,qhd->khd", score_low, query_block, preferred_element_type=F32
        )
        return ((key_sum, value_sum), query_low.astype(BF))

    zeros = jnp.zeros((length, heads_here, head_size), F32)
    blocked = (length // block_count, heads_here, head_size)
    (key_sum, value_sum), query_low = lax.scan(
        one_block,
        (zeros, zeros),
        (
            queries.reshape((block_count,) + blocked),
            mixture_low.reshape((block_count,) + blocked),
            log_totals,
        ),
    )
    width_here = heads_here * head_size
    return (
        query_low.reshape(length, width_here),
        key_sum.astype(BF).reshape(length, width_here),
        value_sum.astype(BF).reshape(length, width_here),
    )


def scatter_sum(partial, axis):
    return lax.psum_scatter(
        partial.astype(BF), "dp", scatter_dimension=axis, tiled=True
    ).astype(F32)


def body(
    layer_input,
    query_weight,
    key_weight,
    value_weight,
    mixing_weight,
    expand_weight,
    shrink_weight,
    query_offset,
    value_offset,
    mixing_offset,
    expand_offset,
    shrink_offset,
    first_gain,
    first_shift,
    second_gain,
    second_shift,
    cotangent,
):
    local_rows = layer_input.shape[0]
    tensor_size = lax.axis_size("tensor")
    tensor_index = lax.axis_index("tensor")
    length = local_rows * tensor_size
    block_rows = min(512, length)
    heads_here = query_weight.shape[1] // HD
    scaling = HD ** (-0.5)
    head_shape = (length, heads_here, HD)
    swap = [(i, i ^ 2) for i in range(tensor_size)]

    zero = jnp.zeros_like(first_gain)
    vectors = jnp.stack(
        [first_gain, first_shift, second_gain, second_shift, shrink_offset, mixing_offset, zero, zero]
    ).astype(F32)
    (
        output,
        attended_grad,
        expand_local,
        shrink_local,
        expand_sum,
        sums,
        sequence,
        queries,
        key_rows,
        values,
        mixture_own,
        log_totals,
        head_full,
        mixing_full,
    ) = layer(
        lax.axis_size("dp"),
        tensor_size,
        (
            layer_input,
            query_weight,
            key_weight,
            value_weight,
            mixing_weight.T,
            expand_weight,
            shrink_weight.T,
            jnp.stack([query_offset, value_offset]).astype(F32),
            expand_offset.astype(F32)[None, :],
            vectors,
            cotangent,
        ),
    )
    sequence = sequence.reshape(length, -1)
    queries = queries.reshape(length, -1)
    query_full, key_full, value_full = head_full[0], head_full[1], head_full[2]
    mixture = lax.all_to_all(mixture_own, "tensor", 0, 0, tiled=True).reshape(length, -1)
    mixing_full = mixing_full[tensor_index].T
    log_totals = jnp.moveaxis(
        log_totals[:heads_here].reshape(heads_here, length // block_rows, block_rows), 1, 0
    )
    attended_rows = lax.all_gather(attended_grad.astype(BF), "tensor", axis=0, tiled=True)
    mixing_local = product_rows(mixture, attended_rows)
    mixture_low = product_last(attended_rows, mixing_full).astype(BF)
    query_low, key_low, value_low = attend_backward(
        queries.reshape(head_shape),
        key_rows.reshape(head_shape),
        values.reshape(head_shape),
        mixture_low,
        log_totals,
        block_rows,
    )
    query_local = product_rows(sequence, query_low) * scaling
    key_local = product_rows(sequence, key_low)
    value_local = product_rows(sequence, value_low)
    query_sum = jnp.sum(query_low.astype(F32), axis=0) * scaling
    value_sum = jnp.sum(value_low.astype(F32), axis=0)
    input_grad = (
        lax.psum_scatter(
            (
                product_last(query_low, query_full) * scaling
                + product_last(key_low, key_full)
                + product_last(value_low, value_full)
            ).astype(BF),
            "tensor",
            scatter_dimension=0,
            tiled=True,
        ).astype(F32)
        + attended_grad
    )
    query_grad = scatter_sum(query_local, 0)
    key_grad = scatter_sum(key_local, 0)
    value_grad = scatter_sum(value_local, 0)
    mixing_grad = scatter_sum(mixing_local, 1)
    expand_parts = lax.psum_scatter(expand_local, "dp", scatter_dimension=1, tiled=True)
    shrink_parts = lax.psum_scatter(shrink_local, "dp", scatter_dimension=1, tiled=True)

    def join(parts):
        theirs = lax.ppermute(parts[1], "tensor", swap)
        return parts[0].astype(F32) + theirs.astype(F32)

    expand_grad = join(expand_parts)
    shrink_grad = join(shrink_parts).T

    def spread_out(vector, index):
        selector = (jnp.arange(tensor_size)[:, None] == index).astype(F32)
        return (selector * vector[None, :]).reshape(-1)

    totals = lax.psum(
        (
            sums,
            spread_out(query_sum, tensor_index),
            spread_out(value_sum, tensor_index),
            spread_out(expand_sum[0, 0], tensor_index)
            + spread_out(expand_sum[1, 0], tensor_index ^ 2),
        ),
        ("dp", "tensor"),
    )

    def own_slice(full_vector, slice_size):
        return lax.dynamic_slice_in_dim(full_vector, tensor_index * slice_size, slice_size, 0)

    offset_query = own_slice(totals[1], query_sum.shape[0])
    offset_value = own_slice(totals[2], value_sum.shape[0])
    offset_expand = own_slice(totals[3], expand_offset.shape[0])
    sums = totals[0]
    return (
        output,
        input_grad,
        query_grad,
        key_grad,
        value_grad,
        mixing_grad,
        expand_grad,
        shrink_grad,
        offset_query,
        offset_value,
        sums[5],
        offset_expand,
        sums[2],
        sums[3],
        sums[4],
        sums[0],
        sums[1],
    )


def solution(mesh):
    rows = P(("dp", "tensor"), None)
    tall = P("dp", "tensor")
    wide = P("tensor", "dp")
    split = P("tensor")
    whole = P()
    return jax.shard_map(
        body,
        mesh=mesh,
        in_specs=(rows, tall, tall, tall, wide, tall, wide, split, split)
        + (whole, split, whole, whole, whole, whole, whole, rows),
        out_specs=(rows, rows, tall, tall, tall, wide, tall, wide, split, split)
        + (whole, split, whole, whole, whole, whole, whole),
        check_vma=False,
    )
```

```python
import functools

import jax
import jax.numpy as jnp
from jax import lax
from jax.experimental import pallas as pl
from jax.experimental.pallas import tpu as pltpu
from jax.sharding import PartitionSpec as P

HD = 64
EPSILON = 1e-05
MESH = pl.DeviceIdType.MESH
BF = jnp.bfloat16
F32 = jnp.float32
NN = (((1,), (0,)), ((), ()))
NT = (((1,), (1,)), ((), ()))
TN = (((0,), (0,)), ((), ()))
VMEM_LIMIT = 60 * 1024 * 1024
TILE = 512


def mm(left, right, dims):
    return lax.dot_general(left, right, dims, preferred_element_type=F32)


def norm_parts(inputs):
    centered = inputs - jnp.mean(inputs, axis=-1, keepdims=True)
    variance = jnp.mean(centered * centered, axis=-1, keepdims=True)
    rate = lax.rsqrt(variance + EPSILON)
    return centered * rate, rate


def norm_back(upstream, gain, normal, rate):
    scaled = upstream * gain
    mean_scaled = jnp.mean(scaled, axis=-1, keepdims=True)
    mean_normal = jnp.mean(scaled * normal, axis=-1, keepdims=True)
    return rate * (scaled - mean_scaled - normal * mean_normal)


def column_sum(block):
    return jnp.sum(block, axis=0, keepdims=True)


def tiles(width, body):
    step = min(TILE, width)

    def one(index, carry):
        body(pl.ds(pl.multiple_of(index * step, step), step))
        return carry

    lax.fori_loop(0, width // step, one, 0)


def chosen(table, index):
    value = jnp.int32(table[0])
    for place in range(1, len(table)):
        value = jnp.where(index == place, jnp.int32(table[place]), value)
    return value


def each(count, start, body):
    if count - start <= 8:
        for index in range(start, count):
            body(index)
        return

    def one(index, carry):
        body(index)
        return carry

    lax.fori_loop(start, count, one, 0)


class Place:
    def __init__(self, devices, ranks):
        self.d = lax.axis_index("dp")
        self.t = lax.axis_index("tensor")
        self.chips = devices // 2
        self.ranks = ranks
        self.c = self.d % 2
        self.p = self.d // 2

    def chip(self, k):
        return {"dp": 2 * (self.p ^ k) + self.c}

    def core(self):
        return {"dp": self.d ^ 1}

    def rank(self, t):
        return {"tensor": t}


def remote(source, target, sems, index, device):
    send, recv = sems
    return pltpu.make_async_remote_copy(
        src_ref=source,
        dst_ref=target,
        send_sem=send.at[index],
        recv_sem=recv.at[index],
        device_id=device,
        device_id_type=MESH,
    )


class Gather:
    def __init__(self, here, view, chip_sems, core_sems):
        self.here, self.view = here, view
        self.chip_sems, self.core_sems = chip_sems, core_sems

    def chip_copy(self, k):
        here = self.here
        mine = self.view(2 * here.p + here.c)
        return remote(mine, mine, self.chip_sems, k, here.chip(k))

    def chip_arrival(self, k):
        here = self.here
        theirs = self.view(2 * (here.p ^ k) + here.c)
        return remote(theirs, theirs, self.chip_sems, k, here.chip(k))

    def core_copy(self, k):
        here = self.here
        shard = self.view(2 * (here.p ^ k) + here.c)
        return remote(shard, shard, self.core_sems, k, here.core())

    def core_arrival(self, k):
        here = self.here
        shard = self.view(2 * (here.p ^ k) + 1 - here.c)
        return remote(shard, shard, self.core_sems, k, here.core())

    def start(self):
        each(self.here.chips, 1, lambda k: self.chip_copy(k).start())
        self.core_copy(0).start()

    def forward(self):
        def one(k):
            self.chip_arrival(k).wait_recv()
            self.core_copy(k).start()

        each(self.here.chips, 1, one)

    def finish(self):
        each(self.here.chips, 0, lambda k: self.core_arrival(k).wait_recv())

    def drain(self):
        each(self.here.chips, 1, lambda k: self.chip_copy(k).wait_send())
        each(self.here.chips, 0, lambda k: self.core_copy(k).wait_send())


class Reduce:
    def __init__(self, here, source, core_slot, chip_slot, chip_sems, core_sems):
        self.here, self.source = here, source
        self.core_slot, self.chip_slot = core_slot, chip_slot
        self.chip_sems, self.core_sems = chip_sems, core_sems

    def core_copy(self, k):
        here = self.here
        shard = self.source(2 * (here.p ^ k) + 1 - here.c)
        return remote(shard, self.core_slot(k), self.core_sems, k, here.core())

    def chip_copy(self, k):
        here = self.here
        shard = self.source(2 * (here.p ^ k) + here.c)
        return remote(shard, self.chip_slot(k), self.chip_sems, k, here.chip(k))

    def start(self):
        each(self.here.chips, 1, lambda k: self.core_copy(k).start())
        self.core_copy(0).start()

    def combine(self):
        here = self.here

        def one(k):
            self.core_copy(k).wait_recv()
            shard = self.source(2 * (here.p ^ k) + here.c)
            shard[...] = shard[...] + self.core_slot(k)[...]

        def send(k):
            one(k)
            self.chip_copy(k).start()

        each(here.chips, 1, send)
        one(0)

    def total(self):
        here = self.here
        each(here.chips, 1, lambda k: self.chip_copy(k).wait_recv())
        value = self.source(here.d)[...].astype(F32)
        for k in range(1, here.chips):
            value = value + self.chip_slot(k)[...].astype(F32)
        return value

    def drain(self):
        each(self.here.chips, 1, lambda k: self.chip_copy(k).wait_send())
        each(self.here.chips, 0, lambda k: self.core_copy(k).wait_send())


def layer_kernel(
    devices,
    chunks,
    input_ref,
    query_ref,
    key_ref,
    value_ref,
    mixing_ref,
    expand_ref,
    shrink_ref,
    head_offset_ref,
    expand_offset_ref,
    vectors_ref,
    cotangent_ref,
    output_ref,
    input_grad_ref,
    head_grad_ref,
    mixing_grad_ref,
    expand_grad_ref,
    shrink_grad_ref,
    sums_ref,
    sequence,
    queries,
    key_rows,
    values,
    mixed,
    log_totals,
    head_full,
    mixing_full,
    feed_full,
    offset_full,
    key_columns,
    value_columns,
    mix_heads,
    attended_ref,
    normed,
    hidden,
    slope,
    summed_low,
    own_part,
    summed_grad,
    send_part,
    recv_part,
    feed_sum,
    feed_chip,
    feed_pair,
    mixing_sum,
    mixing_chip,
    mixing_rank,
    head_sum,
    head_chip,
    attended_low,
    mix_back_send,
    mix_back,
    query_low,
    key_low,
    value_low,
    line_part,
    vector_own,
    vector_core,
    vector_chip,
    vector_rank,
    row_send,
    row_recv,
    mix_send,
    mix_recv,
    weight_send,
    weight_recv,
    pair_send,
    pair_recv,
    chip_send,
    chip_recv,
    core_send,
    core_recv,
    swap_send,
    swap_recv,
    back_send,
    back_recv,
    line_send,
    line_recv,
    rank_send,
    rank_recv,
    free_sem,
):
    ranks = mixed.shape[0]
    rows, width = input_ref.shape
    shard = query_ref.shape[0]
    span = query_ref.shape[1]
    heads = span // HD
    units = expand_ref.shape[1]
    slices = 2
    step = rows // chunks
    length = ranks * rows
    here = Place(devices, ranks)
    d, t, chips = here.d, here.t, here.chips
    last = ranks - 1
    middle = jnp.logical_and(t > 0, t < last)
    partner = here.rank(t ^ 1)
    first_gain = vectors_ref[0:1, :]
    first_shift = vectors_ref[1:2, :]
    second_gain = vectors_ref[2:3, :]
    second_shift = vectors_ref[3:4, :]
    shrink_offset = vectors_ref[4:5, :]
    mixing_offset = vectors_ref[5:6, :]

    barrier = pltpu.get_barrier_semaphore()
    for k in range(1, ranks):
        pl.semaphore_signal(barrier, inc=1, device_id=here.rank(t ^ k), device_id_type=MESH)
    each(
        chips,
        1,
        lambda k: pl.semaphore_signal(
            barrier, inc=1, device_id=here.chip(k), device_id_type=MESH
        ),
    )
    pl.semaphore_signal(barrier, inc=1, device_id=here.core(), device_id_type=MESH)

    mine = pl.ds(pl.multiple_of(d * shard, shard), shard)
    sequence[pl.ds(pl.multiple_of(t * rows, rows), rows), :] = input_ref[...]
    head_full[0, mine, :] = query_ref[...]
    head_full[1, mine, :] = key_ref[...]
    head_full[2, mine, :] = value_ref[...]
    mixing_full[t, mine, :] = mixing_ref[...]
    feed_full[0, 0, mine, :] = expand_ref[...]
    feed_full[0, 1, mine, :] = shrink_ref[...]
    offset_full[0] = expand_offset_ref[...]

    pl.semaphore_wait(barrier, ranks - 1 + chips - 1 + 1)

    def shard_rows(index):
        return pl.ds(pl.multiple_of(index * shard, shard), shard)

    def gather(number, view):
        return Gather(
            here,
            view,
            (chip_send.at[number], chip_recv.at[number]),
            (core_send.at[number], core_recv.at[number]),
        )

    heads_gather = gather(0, lambda i: head_full.at[:, shard_rows(i)])
    mixing_gather = gather(1, lambda i: mixing_full.at[:, shard_rows(i)])
    feed_gathers = [
        gather(2 + s, lambda i, s=s: feed_full.at[s, :, shard_rows(i)]) for s in range(slices)
    ]

    row_sems = (row_send, row_recv)

    def row_copy(s, side):
        block = sequence.at[pl.ds(pl.multiple_of(s * rows, rows), rows)]
        return pltpu.make_async_remote_copy(
            src_ref=block,
            dst_ref=block,
            send_sem=row_send.at[side, s],
            recv_sem=row_recv.at[s],
            device_id=here.rank(jnp.clip(t + (1 if side else -1), 0, last)),
            device_id_type=MESH,
        )

    @pl.when(t < last)
    def _():
        row_copy(t, 1).start()

    @pl.when(t > 0)
    def _():
        row_copy(t, 0).start()

    heads_gather.start()
    heads_gather.forward()
    feed_gathers[0].start()
    heads_gather.finish()

    def project(s):
        place = pl.ds(pl.multiple_of(s * rows, rows), rows)
        block = sequence[place, :]
        query = (mm(block, head_full[0], NN) + head_offset_ref[0:1, :]) * (HD**-0.5)
        queries[s] = query.astype(BF)
        key = mm(block, head_full[1], NN)
        key_rows[place, :] = key.astype(BF)
        value = mm(block, head_full[2], NN) + head_offset_ref[1:2, :]
        values[place, :] = value.astype(BF)
        value_columns[:, place] = value.T.astype(BF)
        key_columns[:, place] = key.T.astype(BF)

    project(t)

    def weight_copy(k):
        return remote(
            mixing_full.at[t, mine],
            mixing_full.at[t, mine],
            (weight_send, weight_recv),
            k,
            here.rank(t ^ k),
        )

    def weight_arrival(k):
        theirs = mixing_full.at[t ^ k, mine]
        return remote(theirs, theirs, (weight_send, weight_recv), k, here.rank(t ^ k))

    pair_copies = [
        remote(
            feed_full.at[0, :, mine],
            feed_full.at[1, :, mine],
            (pair_send, pair_recv),
            0,
            here.rank(t ^ 2),
        ),
        remote(
            offset_full.at[0], offset_full.at[1], (pair_send, pair_recv), 1, here.rank(t ^ 2)
        ),
    ]

    def start_pairs():
        for k in range(1, ranks):
            weight_copy(k).start()
        for copy in pair_copies:
            copy.start()

    near = [
        [s for _, s in sorted((abs(s - u), s) for s in range(ranks) if s != u)]
        for u in range(ranks)
    ]
    for j in range(ranks - 1):
        s = chosen([near[u][j] for u in range(ranks)], t)
        row_copy(s, 0).wait_recv()

        @pl.when(jnp.logical_and(s < t, t < last))
        def _():
            row_copy(s, 1).start()

        @pl.when(jnp.logical_and(s > t, t > 0))
        def _():
            row_copy(s, 0).start()

        if j == 1:

            @pl.when(jnp.logical_not(middle))
            def _():
                start_pairs()

        project(s)

    def mix_copy(s):
        return pltpu.make_async_remote_copy(
            src_ref=mix_heads.at[s],
            dst_ref=mixed.at[t],
            send_sem=mix_send.at[s],
            recv_sem=mix_recv.at[t],
            device_id=here.rank(s),
            device_id_type=MESH,
        )

    def mix_arrival(s):
        return pltpu.make_async_remote_copy(
            src_ref=mix_heads.at[s],
            dst_ref=mixed.at[s],
            send_sem=mix_send.at[s],
            recv_sem=mix_recv.at[s],
            device_id=here.rank(s),
            device_id_type=MESH,
        )

    lane = lax.broadcasted_iota(jnp.int32, (1, 128), 1)

    def attend(s):
        place = pl.ds(pl.multiple_of(s * rows, rows), rows)
        columns = []
        for h in range(heads):
            pair = slice(128 * (h // 2), 128 * (h // 2) + 128)
            side = (lane // HD) == (h % 2)
            query = jnp.where(side, queries[s, :, pair], jnp.zeros((), BF))
            scores = mm(key_rows[:, pair], query, NT)
            largest = jnp.max(scores, axis=0, keepdims=True)
            weights = jnp.exp(scores - largest)
            total = jnp.sum(weights, axis=0, keepdims=True)
            column = mm(value_columns[h * HD : (h + 1) * HD, :], weights.astype(BF), NN)
            columns.append(column / total)
            log_totals[h : h + 1, place] = largest + jnp.log(total)
        mix_heads[s] = jnp.concatenate(columns, axis=0).T.astype(BF)

    far = [[s for s in reversed(near[u])] + [u] for u in range(ranks)]
    for j in range(ranks):
        s = chosen([far[u][j] for u in range(ranks)], t)
        attend(s)
        if j < ranks - 1:
            mix_copy(s).start()
        if j == 0:

            @pl.when(middle)
            def _():
                start_pairs()

        if j == 1:
            feed_gathers[0].forward()
    mixed[t] = mix_heads[t]

    for k in range(1, ranks):
        weight_arrival(k).wait_recv()
    mixing_gather.start()
    for copy in pair_copies:
        copy.wait_recv()
    feed_gathers[1].start()
    for k in range(1, ranks):
        mix_arrival(t ^ k).wait_recv()
    mixing_gather.forward()
    mixing_gather.finish()

    def mix_tile(tile):
        total = input_ref[:, tile].astype(F32) + vectors_ref[5:6, tile]
        for j in range(ranks):
            total = total + mm(mixed[j], mixing_full[j, tile, :], NT)
        attended_ref[:, tile] = total

    tiles(width, mix_tile)

    def own(chunk):
        return pl.ds(chunk * step, step)

    def other(chunk):
        return pl.ds(rows + chunk * step, step)

    def exchange(kind, chunk, source, target):
        return pltpu.make_async_remote_copy(
            src_ref=source,
            dst_ref=target,
            send_sem=swap_send.at[kind, chunk],
            recv_sem=swap_recv.at[kind, chunk],
            device_id=partner,
            device_id_type=MESH,
        )

    copies = [
        [exchange(0, c, normed.at[own(c)], normed.at[other(c)]) for c in range(chunks)],
        [exchange(1, c, send_part.at[0, own(c)], recv_part.at[0, own(c)]) for c in range(chunks)],
        [exchange(2, c, summed_low.at[own(c)], summed_low.at[other(c)]) for c in range(chunks)],
        [exchange(3, c, send_part.at[1, own(c)], recv_part.at[1, own(c)]) for c in range(chunks)],
    ]
    for c in range(chunks):
        normal, _ = norm_parts(attended_ref[own(c), :])
        normed[own(c), :] = (normal * first_gain + first_shift).astype(BF)
        copies[0][c].start()

    def forward(place, store, ready):
        for s in range(slices):
            ready(s)

            def grow(tile):
                value = mm(normed[place, :], feed_full[s, 0, :, tile], NN)
                value = value + offset_full[s, :, tile]
                share = 0.5 * (1.0 + lax.erf(value * 0.7071067811865476))
                density = jnp.exp(-0.5 * value * value) * 0.3989422804014327
                hidden[s, place, tile] = (value * share).astype(BF)
                slope[s, place, tile] = (share + value * density).astype(BF)

            tiles(units, grow)

        def shrink(tile):
            total = mm(hidden[0, place, :], feed_full[0, 1, tile, :], NT)
            for s in range(1, slices):
                total = total + mm(hidden[s, place, :], feed_full[s, 1, tile, :], NT)
            store(tile, total)

        tiles(width, shrink)

    def backward(place, store):
        for s in range(slices):

            def narrow(tile):
                value = mm(summed_low[place, :], feed_full[s, 1, :, tile], NN)
                value = value * slope[s, place, tile].astype(F32)
                slope[s, place, tile] = value.astype(BF)

            tiles(units, narrow)

        def widen(tile):
            total = mm(slope[0, place, :], feed_full[0, 0, tile, :], NT)
            for s in range(1, slices):
                total = total + mm(slope[s, place, :], feed_full[s, 0, tile, :], NT)
            store(tile, total)

        tiles(width, widen)

    def keep(tile, total):
        own_part[:, tile] = total

    def pass_on(which, chunk):
        def store(tile, total):
            send_part[which, own(chunk), tile] = total.astype(BF)

        return store

    def arrive(s):
        if s == 0:
            feed_gathers[0].finish()
        else:
            feed_gathers[s].forward()
            feed_gathers[s].finish()

    forward(pl.ds(0, rows), keep, arrive)
    for c in range(chunks):
        copies[0][c].wait_recv()
        forward(other(c), pass_on(0, c), lambda s: None)
        copies[1][c].start()

    vector_own[...] = jnp.zeros_like(vector_own)
    for c in range(chunks):
        copies[1][c].wait_recv()
        normal, _ = norm_parts(attended_ref[own(c), :])
        first_norm = normal * first_gain + first_shift
        summed = (
            first_norm
            + (own_part[own(c), :] + recv_part[0, own(c), :].astype(F32))
            + shrink_offset
        )
        normal, rate = norm_parts(summed)
        output_ref[own(c), :] = (normal * second_gain + second_shift).astype(BF)
        upstream = cotangent_ref[own(c), :].astype(F32)
        grad = norm_back(upstream, second_gain, normal, rate)
        summed_grad[own(c), :] = grad
        summed_low[own(c), :] = grad.astype(BF)
        copies[2][c].start()
        vector_own[0:1, :] += column_sum(upstream * normal)
        vector_own[1:2, :] += column_sum(upstream)
        vector_own[2:3, :] += column_sum(grad)

    backward(pl.ds(0, rows), keep)
    for c in range(chunks):
        copies[2][c].wait_recv()
        backward(other(c), pass_on(1, c))
        copies[3][c].start()

    for each_gather in feed_gathers:
        each_gather.drain()
    for copy in pair_copies:
        copy.wait_send()
    pl.semaphore_signal(free_sem, inc=1, device_id=here.core(), device_id_type=MESH)

    def spare_rows(k):
        return pl.ds(pl.multiple_of(width // 2 + k * shard, shard), shard)

    def reduce(number, source, core_slot, chip_slot):
        return Reduce(
            here,
            source,
            core_slot,
            chip_slot,
            (chip_send.at[number], chip_recv.at[number]),
            (core_send.at[number], core_recv.at[number]),
        )

    feed_reduces = [
        reduce(
            4 + s,
            lambda i, s=s: feed_sum.at[s, :, shard_rows(i)],
            lambda k, s=s: feed_full.at[s, :, shard_rows(k)],
            lambda k, s=s: feed_chip.at[s, k - 1],
        )
        for s in range(slices)
    ]
    mixing_reduce = reduce(
        6,
        lambda i: mixing_sum.at[shard_rows(i)],
        lambda k: feed_full.at[0, 0, spare_rows(k)],
        lambda k: mixing_chip.at[k - 1],
    )
    head_reduce = reduce(
        7,
        lambda i: head_sum.at[shard_rows(i)],
        lambda k: feed_full.at[0, 1, spare_rows(k), 0 : 3 * span],
        lambda k: head_chip.at[k - 1],
    )

    for s in reversed(range(slices)):

        def weigh(tile):
            left = min(TILE, width)
            for m in range(width // left):
                part = pl.ds(m * left, left)
                feed_sum[s, 1, part, tile] = mm(summed_low[:, part], hidden[s, :, tile], TN).astype(BF)
                feed_sum[s, 0, part, tile] = mm(normed[:, part], slope[s, :, tile], TN).astype(BF)
            vector_own[6 + s : 7 + s, tile] = column_sum(slope[s, :, tile].astype(F32))

        tiles(units, weigh)
        if s == slices - 1:
            pl.semaphore_wait(free_sem, 1)
        feed_reduces[s].start()

    def back_copy(s, chunk):
        return pltpu.make_async_remote_copy(
            src_ref=mix_back_send.at[s, own(chunk)],
            dst_ref=mix_back.at[t, own(chunk)],
            send_sem=back_send.at[chunk, s],
            recv_sem=back_recv.at[chunk, t],
            device_id=here.rank(s),
            device_id_type=MESH,
        )

    def back_arrival(s, chunk):
        return pltpu.make_async_remote_copy(
            src_ref=mix_back_send.at[s, own(chunk)],
            dst_ref=mix_back.at[s, own(chunk)],
            send_sem=back_send.at[chunk, s],
            recv_sem=back_recv.at[chunk, s],
            device_id=here.rank(s),
            device_id_type=MESH,
        )

    for c in range(chunks):
        copies[3][c].wait_recv()
        normal, rate = norm_parts(attended_ref[own(c), :])
        upstream = summed_grad[own(c), :] + (
            own_part[own(c), :] + recv_part[1, own(c), :].astype(F32)
        )
        grad = norm_back(upstream, first_gain, normal, rate)
        input_grad_ref[own(c), :] = grad
        attended_low[own(c), :] = grad.astype(BF)
        for j in range(ranks):
            s = chosen([far[u][j] for u in range(ranks)], t)
            block = mm(attended_low[own(c), :], mixing_full[s], NN).astype(BF)
            if j < ranks - 1:
                mix_back_send[s, own(c), :] = block
                back_copy(s, c).start()
            else:
                mix_back[s, own(c), :] = block
        vector_own[3:4, :] += column_sum(upstream * normal)
        vector_own[4:5, :] += column_sum(upstream)
        vector_own[5:6, :] += column_sum(grad)

    for j in range(ranks):
        mixing_sum[:, j * span : (j + 1) * span] = mm(attended_low[...], mixed[j], TN).astype(BF)
    mixing_reduce.start()
    for s in reversed(range(slices)):
        feed_reduces[s].combine()
    mixing_reduce.combine()

    own_part[...] = jnp.zeros_like(own_part)
    summed_grad[...] = jnp.zeros_like(summed_grad)

    def attend_back(s):
        place = pl.ds(pl.multiple_of(s * rows, rows), rows)
        inner = (mix_back[s].astype(F32) * mix_heads[s].astype(F32)).T
        columns = []
        for h in range(heads):
            pair = slice(128 * (h // 2), 128 * (h // 2) + 128)
            side = (lane // HD) == (h % 2)
            none = jnp.zeros((), BF)
            query = jnp.where(side, queries[s, :, pair], none)
            upstream = jnp.where(side, mix_back[s, :, pair], none)
            delta = jnp.sum(inner[h * HD : (h + 1) * HD, :], axis=0, keepdims=True)
            log_total = log_totals[h : h + 1, place]
            column = None
            for k in range(ranks):
                part = slice(k * rows, (k + 1) * rows)
                lanes = slice(k * span + pair.start, k * span + pair.stop)
                scores = mm(key_rows[part, pair], query, NT)
                probs = jnp.exp(scores - log_total)
                prob_grad = mm(values[part, pair], upstream, NT)
                score_low = (probs * (prob_grad - delta)).astype(BF)
                summed_grad[:, lanes] += mm(probs.astype(BF), upstream, NN)
                own_part[:, lanes] += mm(score_low, query, NN)
                term = mm(key_columns[h * HD : (h + 1) * HD, part], score_low, NN)
                column = term if column is None else column + term
            columns.append(column)
        low = jnp.concatenate(columns, axis=0).T.astype(BF)
        query_low[place, :] = (low.astype(F32) * HD**-0.5).astype(BF)

    for j in range(ranks):
        s = t if j == 0 else chosen([near[u][j - 1] for u in range(ranks)], t)
        if j > 0:
            for c in range(chunks):
                back_arrival(s, c).wait_recv()
        attend_back(s)
    for k in range(ranks):
        part = slice(k * rows, (k + 1) * rows)
        lanes = slice(k * span, (k + 1) * span)
        key_low[part, :] = own_part[:, lanes].astype(BF)
        value_low[part, :] = summed_grad[:, lanes].astype(BF)

    def input_part(s, tile):
        place = pl.ds(pl.multiple_of(s * rows, rows), rows)
        return (
            mm(query_low[place, :], head_full[0, tile, :], NT)
            + mm(key_low[place, :], head_full[1, tile, :], NT)
            + mm(value_low[place, :], head_full[2, tile, :], NT)
        )

    def arrival_time(u, s):
        if s > u:
            u, s = last - u, last - s
        return s if u == last else s + 1 + last - 1 - u

    line_order = [
        sorted([s for s in range(ranks) if s != u], key=lambda s, u=u: (arrival_time(u, s), s))
        for u in range(ranks)
    ]

    def line_rows(j):
        return pl.ds((j % 2) * rows, rows)

    def line_send_ref(j, chunk):
        return hidden.at[j // 2, pl.ds((j % 2) * rows + chunk * step, step)]

    def line_copy(j, s, chunk):
        slot = jnp.where(s == t + 1, ranks, s)
        return pltpu.make_async_remote_copy(
            src_ref=line_send_ref(j, chunk),
            dst_ref=line_part.at[slot, own(chunk)],
            send_sem=line_send.at[j, chunk],
            recv_sem=line_recv.at[slot, chunk],
            device_id=here.rank(jnp.clip(jnp.where(s < t, t - 1, t + 1), 0, last)),
            device_id_type=MESH,
        )

    def line_arrival(slot, chunk):
        return pltpu.make_async_remote_copy(
            src_ref=line_part.at[slot, own(chunk)],
            dst_ref=line_part.at[slot, own(chunk)],
            send_sem=line_send.at[0, chunk],
            recv_sem=line_recv.at[slot, chunk],
            device_id=partner,
            device_id_type=MESH,
        )

    targets = [chosen([line_order[u][j] for u in range(ranks)], t) for j in range(ranks - 1)]
    opens = [
        jnp.logical_or(jnp.logical_and(s < t, t == last), jnp.logical_and(s > t, t == 0))
        for s in targets
    ]
    for j, s in enumerate(targets):

        def store(tile):
            hidden[j // 2, line_rows(j), tile] = input_part(s, tile).astype(BF)

        tiles(width, store)

        @pl.when(opens[j])
        def _():
            for c in range(chunks):
                line_copy(j, s, c).start()

    def weigh_heads(tile):
        for i, low in enumerate((query_low, key_low, value_low)):
            head_sum[tile, i * span : (i + 1) * span] = mm(sequence[:, tile], low[...], TN).astype(BF)

    tiles(width, weigh_heads)
    head_reduce.start()
    vector_own[8:9, 0:span] = column_sum(query_low[...].astype(F32))
    vector_own[8:9, span : 2 * span] = column_sum(value_low[...].astype(F32))

    def vector_core_copy():
        return remote(
            vector_own, vector_core, (core_send.at[8], core_recv.at[8]), 0, here.core()
        )

    vector_core_copy().start()

    def store_own(tile):
        input_grad_ref[:, tile] = input_grad_ref[:, tile] + input_part(t, tile)

    tiles(width, store_own)

    def feed_total(s):
        return feed_reduces[s].total()

    def pair_back():
        return remote(
            feed_sum.at[1, :, mine], feed_pair, (pair_send, pair_recv), 2, here.rank(t ^ 2)
        )

    feed_sum[1, :, mine, :] = feed_total(1).astype(BF)
    pair_back().start()

    def pass_line(j, s):
        @pl.when(jnp.logical_not(opens[j]))
        def _():
            for c in range(chunks):
                line_arrival(s, c).wait_recv()
                block = line_send_ref(j, c)
                block[...] = (
                    block[...].astype(F32) + line_part[s, own(c), :].astype(F32)
                ).astype(BF)
                line_copy(j, s, c).start()

    vector_core_copy().wait()
    vector_own[...] = vector_own[...] + vector_core[...]

    def vector_chip_copy(k):
        return remote(
            vector_own,
            vector_chip.at[k - 1],
            (chip_send.at[8], chip_recv.at[8]),
            k,
            here.chip(k),
        )

    each(chips, 1, lambda k: vector_chip_copy(k).start())
    head_reduce.combine()

    def span_lanes(j):
        return pl.ds(pl.multiple_of(j * span, span), span)

    def mixing_rank_copy(k):
        return remote(
            mixing_sum.at[mine, span_lanes(t ^ k)],
            mixing_rank.at[k - 1],
            (rank_send.at[0], rank_recv.at[0]),
            k,
            here.rank(t ^ k),
        )

    pass_line(0, targets[0])
    mixing_sum[mine, :] = mixing_reduce.total().astype(BF)
    for k in range(1, ranks):
        mixing_rank_copy(k).start()
    for k in range(1, ranks - 1):
        pass_line(k, targets[k])

    each(chips, 1, lambda k: vector_chip_copy(k).wait())
    vector_sum = vector_own[...]
    for k in range(1, chips):
        vector_sum = vector_sum + vector_chip[k - 1]
    vector_core[...] = vector_sum

    def vector_rank_copy(k):
        return remote(
            vector_core,
            vector_rank.at[k - 1],
            (rank_send.at[1], rank_recv.at[1]),
            k,
            here.rank(t ^ k),
        )

    for k in range(1, ranks):
        vector_rank_copy(k).start()

    head_total = head_reduce.total()
    for i in range(3):
        head_grad_ref[i] = head_total[:, i * span : (i + 1) * span]
    feed_own = feed_total(0)
    for k in range(1, ranks):
        mixing_rank_copy(k).wait()
    mixing_grad = mixing_sum[mine, span_lanes(t)].astype(F32)
    for k in range(1, ranks):
        mixing_grad = mixing_grad + mixing_rank[k - 1].astype(F32)
    mixing_grad_ref[...] = mixing_grad
    pair_back().wait()
    expand_grad_ref[...] = feed_own[0] + feed_pair[0].astype(F32)
    shrink_grad_ref[...] = feed_own[1] + feed_pair[1].astype(F32)
    for k in range(1, ranks):
        vector_rank_copy(k).wait()
    vector_sum = vector_core[...]
    sums_ref[...] = vector_sum
    everywhere = vector_sum[0:6, :]
    for k in range(1, ranks):
        everywhere = everywhere + vector_rank[k - 1, 0:6, :]
    sums_ref[0:6, :] = everywhere
    sums_ref[6:7, :] = vector_sum[6:7, :] + vector_rank[1, 7:8, :]

    @pl.when(t < last)
    def _():
        for c in range(chunks):
            line_arrival(t, c).wait_recv()
            input_grad_ref[own(c), :] += line_part[t, own(c), :].astype(F32)

    @pl.when(t > 0)
    def _():
        for c in range(chunks):
            line_arrival(ranks, c).wait_recv()
            input_grad_ref[own(c), :] += line_part[ranks, own(c), :].astype(F32)

    for j in range(ranks - 1):
        for c in range(chunks):
            line_copy(j, targets[j], c).wait_send()
            back_copy(t ^ (j + 1), c).wait_send()
    for each_reduce in feed_reduces + [mixing_reduce, head_reduce]:
        each_reduce.drain()
    for kind in range(4):
        for c in range(chunks):
            copies[kind][c].wait_send()
    for each_gather in (heads_gather, mixing_gather):
        each_gather.drain()
    for k in range(1, ranks):
        weight_copy(k).wait_send()
        mix_copy(t ^ k).wait_send()
    for s in range(ranks):

        @pl.when(jnp.logical_and(s <= t, t < last))
        def _():
            row_copy(s, 1).wait_send()

        @pl.when(jnp.logical_and(s >= t, t > 0))
        def _():
            row_copy(s, 0).wait_send()


def layer(devices, ranks, inputs):
    layer_input = inputs[0]
    rows, width = layer_input.shape
    span = inputs[1].shape[1]
    units = inputs[5].shape[1]
    slices = 2
    chunks = 2
    chips = devices // 2
    length = ranks * rows
    both = 2 * rows
    vmem = pl.BlockSpec(memory_space=pltpu.VMEM)
    dma = pltpu.SemaphoreType.DMA
    shard = width // devices
    outs = (
        jax.ShapeDtypeStruct((rows, width), BF),
        jax.ShapeDtypeStruct((rows, width), F32),
        jax.ShapeDtypeStruct((3, shard, span), F32),
        jax.ShapeDtypeStruct((shard, span), F32),
        jax.ShapeDtypeStruct((shard, units), F32),
        jax.ShapeDtypeStruct((shard, units), F32),
        jax.ShapeDtypeStruct((16, width), F32),
    )
    return pl.pallas_call(
        functools.partial(layer_kernel, devices, chunks),
        out_shape=outs,
        in_specs=[vmem] * len(inputs),
        out_specs=[vmem] * len(outs),
        scratch_shapes=[
            pltpu.VMEM((length, width), BF),
            pltpu.VMEM((ranks, rows, span), BF),
            pltpu.VMEM((length, span), BF),
            pltpu.VMEM((length, span), BF),
            pltpu.VMEM((ranks, rows, span), BF),
            pltpu.VMEM((8, length), F32),
            pltpu.VMEM((3, width, span), BF),
            pltpu.VMEM((ranks, width, span), BF),
            pltpu.VMEM((slices, 2, width, units), BF),
            pltpu.VMEM((slices, 1, units), F32),
            pltpu.VMEM((span, length), BF),
            pltpu.VMEM((span, length), BF),
            pltpu.VMEM((ranks, rows, span), BF),
            pltpu.VMEM((rows, width), F32),
            pltpu.VMEM((both, width), BF),
            pltpu.VMEM((slices, both, units), BF),
            pltpu.VMEM((slices, both, units), BF),
            pltpu.VMEM((both, width), BF),
            pltpu.VMEM((rows, width), F32),
            pltpu.VMEM((rows, width), F32),
            pltpu.VMEM((2, rows, width), BF),
            pltpu.VMEM((2, rows, width), BF),
            pltpu.VMEM((slices, 2, width, units), BF),
            pltpu.VMEM((slices, chips - 1, 2, shard, units), BF),
            pltpu.VMEM((2, shard, units), BF),
            pltpu.VMEM((width, ranks * span), BF),
            pltpu.VMEM((chips - 1, shard, ranks * span), BF),
            pltpu.VMEM((ranks - 1, shard, span), BF),
            pltpu.VMEM((width, 3 * span), BF),
            pltpu.VMEM((chips - 1, shard, 3 * span), BF),
            pltpu.VMEM((rows, width), BF),
            pltpu.VMEM((ranks, rows, span), BF),
            pltpu.VMEM((ranks, rows, span), BF),
            pltpu.VMEM((length, span), BF),
            pltpu.VMEM((length, span), BF),
            pltpu.VMEM((length, span), BF),
            pltpu.VMEM((ranks + 1, rows, width), BF),
            pltpu.VMEM((16, width), F32),
            pltpu.VMEM((16, width), F32),
            pltpu.VMEM((chips - 1, 16, width), F32),
            pltpu.VMEM((ranks - 1, 16, width), F32),
            dma((2, ranks)),
            dma((ranks,)),
            dma((ranks,)),
            dma((ranks,)),
            dma((ranks,)),
            dma((ranks,)),
            dma((3,)),
            dma((3,)),
            dma((9, chips)),
            dma((9, chips)),
            dma((9, chips)),
            dma((9, chips)),
            dma((4, chunks)),
            dma((4, chunks)),
            dma((chunks, ranks)),
            dma((chunks, ranks)),
            dma((ranks - 1, chunks)),
            dma((ranks + 1, chunks)),
            dma((2, ranks)),
            dma((2, ranks)),
            pltpu.SemaphoreType.REGULAR,
        ],
        compiler_params=pltpu.CompilerParams(
            collective_id=1, has_side_effects=True, vmem_limit_bytes=VMEM_LIMIT
        ),
    )(*inputs)


def body(
    layer_input,
    query_weight,
    key_weight,
    value_weight,
    mixing_weight,
    expand_weight,
    shrink_weight,
    query_offset,
    value_offset,
    mixing_offset,
    expand_offset,
    shrink_offset,
    first_gain,
    first_shift,
    second_gain,
    second_shift,
    cotangent,
):
    span = query_weight.shape[1]
    zero = jnp.zeros_like(first_gain)
    vectors = jnp.stack(
        [first_gain, first_shift, second_gain, second_shift, shrink_offset, mixing_offset, zero, zero]
    ).astype(F32)
    output, input_grad, head_grad, mixing_grad, expand_grad, shrink_grad, sums = layer(
        lax.axis_size("dp"),
        lax.axis_size("tensor"),
        (
            layer_input,
            query_weight,
            key_weight,
            value_weight,
            mixing_weight.T,
            expand_weight,
            shrink_weight.T,
            jnp.stack([query_offset, value_offset]).astype(F32),
            expand_offset.astype(F32)[None, :],
            vectors,
            cotangent,
        ),
    )
    return (
        output,
        input_grad,
        head_grad[0],
        head_grad[1],
        head_grad[2],
        mixing_grad.T,
        expand_grad,
        shrink_grad.T,
        sums[8, :span],
        sums[8, span : 2 * span],
        sums[5],
        sums[6, : expand_offset.shape[0]],
        sums[2],
        sums[3],
        sums[4],
        sums[0],
        sums[1],
    )


def solution(mesh):
    rows = P(("dp", "tensor"), None)
    tall = P("dp", "tensor")
    wide = P("tensor", "dp")
    split = P("tensor")
    whole = P()
    return jax.shard_map(
        body,
        mesh=mesh,
        in_specs=(rows, tall, tall, tall, wide, tall, wide, split, split)
        + (whole, split, whole, whole, whole, whole, whole, rows),
        out_specs=(rows, rows, tall, tall, tall, wide, tall, wide, split, split)
        + (whole, split, whole, whole, whole, whole, whole),
        check_vma=False,
    )
```

```python
import functools

import jax
import jax.numpy as jnp
from jax import lax
from jax.experimental import pallas as pl
from jax.experimental.pallas import tpu as pltpu
from jax.sharding import PartitionSpec as P

HD = 64
EPSILON = 1e-05
MESH = pl.DeviceIdType.MESH
BF = jnp.bfloat16
F32 = jnp.float32
NN = (((1,), (0,)), ((), ()))
NT = (((1,), (1,)), ((), ()))
TN = (((0,), (0,)), ((), ()))
VMEM_LIMIT = 60 * 1024 * 1024
TILE = 512


def mm(left, right, dims):
    return lax.dot_general(left, right, dims, preferred_element_type=F32)


def norm_parts(inputs):
    centered = inputs - jnp.mean(inputs, axis=-1, keepdims=True)
    variance = jnp.mean(centered * centered, axis=-1, keepdims=True)
    rate = lax.rsqrt(variance + EPSILON)
    return centered * rate, rate


def norm_back(upstream, gain, normal, rate):
    scaled = upstream * gain
    mean_scaled = jnp.mean(scaled, axis=-1, keepdims=True)
    mean_normal = jnp.mean(scaled * normal, axis=-1, keepdims=True)
    return rate * (scaled - mean_scaled - normal * mean_normal)


def column_sum(block):
    return jnp.sum(block, axis=0, keepdims=True)


def tiles(width, body):
    step = min(TILE, width)

    def one(index, carry):
        body(pl.ds(pl.multiple_of(index * step, step), step))
        return carry

    lax.fori_loop(0, width // step, one, 0)


def chosen(table, index):
    value = jnp.int32(table[0])
    for place in range(1, len(table)):
        value = jnp.where(index == place, jnp.int32(table[place]), value)
    return value


def each(count, start, body):
    if count - start <= 8:
        for index in range(start, count):
            body(index)
        return

    def one(index, carry):
        body(index)
        return carry

    lax.fori_loop(start, count, one, 0)


class Place:
    def __init__(self, devices, ranks):
        self.d = lax.axis_index("dp")
        self.t = lax.axis_index("tensor")
        self.chips = devices // 2
        self.ranks = ranks
        self.c = self.d % 2
        self.p = self.d // 2

    def chip(self, k):
        return {"dp": 2 * (self.p ^ k) + self.c}

    def core(self):
        return {"dp": self.d ^ 1}

    def rank(self, t):
        return {"tensor": t}


def remote(source, target, sems, index, device):
    send, recv = sems
    return pltpu.make_async_remote_copy(
        src_ref=source,
        dst_ref=target,
        send_sem=send.at[index],
        recv_sem=recv.at[index],
        device_id=device,
        device_id_type=MESH,
    )


class Gather:
    def __init__(self, here, view, chip_sems, core_sems):
        self.here, self.view = here, view
        self.chip_sems, self.core_sems = chip_sems, core_sems

    def chip_copy(self, k):
        here = self.here
        mine = self.view(2 * here.p + here.c)
        return remote(mine, mine, self.chip_sems, k, here.chip(k))

    def chip_arrival(self, k):
        here = self.here
        theirs = self.view(2 * (here.p ^ k) + here.c)
        return remote(theirs, theirs, self.chip_sems, k, here.chip(k))

    def core_copy(self, k):
        here = self.here
        shard = self.view(2 * (here.p ^ k) + here.c)
        return remote(shard, shard, self.core_sems, k, here.core())

    def core_arrival(self, k):
        here = self.here
        shard = self.view(2 * (here.p ^ k) + 1 - here.c)
        return remote(shard, shard, self.core_sems, k, here.core())

    def start(self):
        each(self.here.chips, 1, lambda k: self.chip_copy(k).start())
        self.core_copy(0).start()

    def forward(self):
        def one(k):
            self.chip_arrival(k).wait_recv()
            self.core_copy(k).start()

        each(self.here.chips, 1, one)

    def finish(self):
        each(self.here.chips, 0, lambda k: self.core_arrival(k).wait_recv())

    def drain(self):
        each(self.here.chips, 1, lambda k: self.chip_copy(k).wait_send())
        each(self.here.chips, 0, lambda k: self.core_copy(k).wait_send())


class Reduce:
    def __init__(self, here, source, core_slot, chip_slot, chip_sems, core_sems):
        self.here, self.source = here, source
        self.core_slot, self.chip_slot = core_slot, chip_slot
        self.chip_sems, self.core_sems = chip_sems, core_sems

    def core_copy(self, k):
        here = self.here
        shard = self.source(2 * (here.p ^ k) + 1 - here.c)
        return remote(shard, self.core_slot(k), self.core_sems, k, here.core())

    def chip_copy(self, k):
        here = self.here
        shard = self.source(2 * (here.p ^ k) + here.c)
        return remote(shard, self.chip_slot(k), self.chip_sems, k, here.chip(k))

    def start(self):
        each(self.here.chips, 1, lambda k: self.core_copy(k).start())
        self.core_copy(0).start()

    def combine(self):
        here = self.here

        def one(k):
            self.core_copy(k).wait_recv()
            shard = self.source(2 * (here.p ^ k) + here.c)
            shard[...] = shard[...] + self.core_slot(k)[...]

        def send(k):
            one(k)
            self.chip_copy(k).start()

        each(here.chips, 1, send)
        one(0)

    def total(self):
        here = self.here
        each(here.chips, 1, lambda k: self.chip_copy(k).wait_recv())
        value = self.source(here.d)[...].astype(F32)
        for k in range(1, here.chips):
            value = value + self.chip_slot(k)[...].astype(F32)
        return value

    def drain(self):
        each(self.here.chips, 1, lambda k: self.chip_copy(k).wait_send())
        each(self.here.chips, 0, lambda k: self.core_copy(k).wait_send())


class TreeGather(Gather):
    def __init__(self, here, view, chip_sems, core_sems, rising):
        super().__init__(here, view, chip_sems, core_sems)
        self.rising = rising
        self.steps = here.chips.bit_length() - 1

    def bit(self, i):
        return 1 << i if self.rising else self.here.chips >> (i + 1)

    def held(self, i, j):
        return j if self.rising else j << (self.steps - i)

    def step_copy(self, i, j):
        here = self.here
        mask = self.held(i, j)
        shard = self.view(2 * (here.p ^ mask) + here.c)
        bit = self.bit(i)
        return remote(shard, shard, self.chip_sems, mask ^ bit, here.chip(bit))

    def step_arrival(self, i, j):
        here = self.here
        bit = self.bit(i)
        key = self.held(i, j) ^ bit
        shard = self.view(2 * (here.p ^ key) + here.c)
        return remote(shard, shard, self.chip_sems, key, here.chip(bit))

    def start(self):
        each(1, 0, lambda j: self.step_copy(0, j).start())
        self.core_copy(0).start()

    def advance(self, i):
        count = 1 << i
        each(count, 0, lambda j: self.step_arrival(i, j).wait_recv())
        if i + 1 < self.steps:
            each(2 * count, 0, lambda j: self.step_copy(i + 1, j).start())
        each(count, 0, lambda j: self.core_copy(self.held(i, j) ^ self.bit(i)).start())

    def advance_rest(self):
        for i in range(1, self.steps):
            self.advance(i)

    def drain(self):
        for i in range(self.steps):
            each(1 << i, 0, lambda j: self.step_copy(i, j).wait_send())
        each(self.here.chips, 0, lambda k: self.core_copy(k).wait_send())


class TreeReduce(Reduce):
    def __init__(self, here, source, core_slot, chip_slot, chip_sems, core_sems, rising):
        super().__init__(here, source, core_slot, chip_slot, chip_sems, core_sems)
        self.rising = rising
        self.steps = here.chips.bit_length() - 1

    def bit(self, i):
        return 1 << i if self.rising else self.here.chips >> (i + 1)

    def rest(self, i, j):
        return j << (i + 1) if self.rising else j

    def count(self, i):
        return 1 << (self.steps - 1 - i)

    def step_copy(self, i, j):
        here = self.here
        bit = self.bit(i)
        key = self.rest(i, j) ^ bit
        shard = self.source(2 * (here.p ^ key) + here.c)
        return remote(shard, self.chip_slot(key), self.chip_sems, key, here.chip(bit))

    def combine(self):
        here = self.here

        def one(k):
            self.core_copy(k).wait_recv()
            shard = self.source(2 * (here.p ^ k) + here.c)
            shard[...] = shard[...] + self.core_slot(k)[...]

        each(here.chips, 1, one)
        one(0)
        each(self.count(0), 0, lambda j: self.step_copy(0, j).start())

    def advance(self, i):
        here = self.here

        def one(j):
            mask = self.rest(i, j)
            self.step_copy(i, j).wait_recv()
            shard = self.source(2 * (here.p ^ mask) + here.c)
            shard[...] = shard[...] + self.chip_slot(mask ^ self.bit(i))[...]

        each(self.count(i), 0, one)
        each(self.count(i + 1), 0, lambda j: self.step_copy(i + 1, j).start())

    def advance_rest(self):
        for i in range(1, self.steps - 1):
            self.advance(i)

    def total(self):
        final = self.steps - 1
        self.step_copy(final, 0).wait_recv()
        value = self.source(self.here.d)[...].astype(F32)
        return value + self.chip_slot(self.bit(final))[...].astype(F32)

    def drain(self):
        for i in range(self.steps):
            each(self.count(i), 0, lambda j: self.step_copy(i, j).wait_send())
        each(self.here.chips, 0, lambda k: self.core_copy(k).wait_send())


def place_kernel(
    layer_output_ref,
    input_sum_ref,
    head_sum_ref,
    mixing_sum_ref,
    expand_sum_ref,
    shrink_sum_ref,
    sums_ref,
    output_ref,
    input_ref,
    query_ref,
    key_ref,
    value_ref,
    mixing_ref,
    expand_ref,
    shrink_ref,
    query_offset_ref,
    value_offset_ref,
    mixing_offset_ref,
    expand_offset_ref,
    shrink_offset_ref,
    first_gain_ref,
    first_shift_ref,
    second_gain_ref,
    second_shift_ref,
):
    output_ref[...] = layer_output_ref[...]
    input_ref[...] = input_sum_ref[...]
    query_ref[...] = head_sum_ref[0]
    key_ref[...] = head_sum_ref[1]
    value_ref[...] = head_sum_ref[2]
    mixing_ref[...] = mixing_sum_ref[...].T
    expand_ref[...] = expand_sum_ref[...]
    shrink_ref[...] = shrink_sum_ref[...].T

    def row(ref, index, start=0):
        size = ref.shape[0]
        ref[...] = sums_ref[index : index + 1, start : start + size].reshape(size)

    row(query_offset_ref, 8)
    row(value_offset_ref, 8, query_offset_ref.shape[0])
    row(mixing_offset_ref, 5)
    row(expand_offset_ref, 6)
    row(shrink_offset_ref, 2)
    row(first_gain_ref, 3)
    row(first_shift_ref, 4)
    row(second_gain_ref, 0)
    row(second_shift_ref, 1)


def place_outputs(results, units, span):
    rows, width = results[1].shape
    shard = results[2].shape[1]
    shapes = [
        ((rows, width), BF),
        ((rows, width), F32),
        ((shard, span), F32),
        ((shard, span), F32),
        ((shard, span), F32),
        ((span, shard), F32),
        ((shard, units), F32),
        ((units, shard), F32),
        ((span,), F32),
        ((span,), F32),
        ((width,), F32),
        ((units,), F32),
    ] + [((width,), F32)] * 5
    vmem = pl.BlockSpec(memory_space=pltpu.VMEM)
    return pl.pallas_call(
        place_kernel,
        out_shape=tuple(jax.ShapeDtypeStruct(shape, kind) for shape, kind in shapes),
        in_specs=[vmem] * len(results),
        out_specs=[vmem] * len(shapes),
    )(*results)


def layer_kernel(
    devices,
    chunks,
    input_ref,
    query_ref,
    key_ref,
    value_ref,
    mixing_ref,
    expand_ref,
    shrink_ref,
    query_offset_ref,
    value_offset_ref,
    mixing_offset_ref,
    expand_offset_ref,
    shrink_offset_ref,
    first_gain_ref,
    first_shift_ref,
    second_gain_ref,
    second_shift_ref,
    cotangent_ref,
    output_ref,
    input_grad_ref,
    head_grad_ref,
    mixing_grad_ref,
    expand_grad_ref,
    shrink_grad_ref,
    sums_ref,
    sequence,
    queries,
    key_rows,
    values,
    mixed,
    log_totals,
    head_full,
    mixing_full,
    feed_full,
    offset_full,
    head_offset_ref,
    vectors_ref,
    key_columns,
    value_columns,
    mix_heads,
    attended_ref,
    normed,
    hidden,
    slope,
    summed_low,
    own_part,
    summed_grad,
    send_part,
    recv_part,
    feed_sum,
    feed_chip,
    feed_pair,
    mixing_sum,
    mixing_chip,
    mixing_rank,
    head_sum,
    head_chip,
    attended_low,
    mix_back_send,
    mix_back,
    query_low,
    key_low,
    value_low,
    line_part,
    vector_own,
    vector_core,
    vector_chip,
    vector_rank,
    row_send,
    row_recv,
    mix_send,
    mix_recv,
    weight_send,
    weight_recv,
    pair_send,
    pair_recv,
    chip_send,
    chip_recv,
    core_send,
    core_recv,
    swap_send,
    swap_recv,
    back_send,
    back_recv,
    line_send,
    line_recv,
    rank_send,
    rank_recv,
    free_sem,
):
    ranks = mixed.shape[0]
    rows, width = input_ref.shape
    shard = query_ref.shape[0]
    span = query_ref.shape[1]
    heads = span // HD
    units = expand_ref.shape[1]
    slices = 2
    step = rows // chunks
    length = ranks * rows
    here = Place(devices, ranks)
    d, t, chips = here.d, here.t, here.chips
    last = ranks - 1
    middle = jnp.logical_and(t > 0, t < last)
    partner = here.rank(t ^ 1)
    barrier = pltpu.get_barrier_semaphore()
    for k in range(1, ranks):
        pl.semaphore_signal(barrier, inc=1, device_id=here.rank(t ^ k), device_id_type=MESH)
    each(
        chips,
        1,
        lambda k: pl.semaphore_signal(
            barrier, inc=1, device_id=here.chip(k), device_id_type=MESH
        ),
    )
    pl.semaphore_signal(barrier, inc=1, device_id=here.core(), device_id_type=MESH)

    mine = pl.ds(pl.multiple_of(d * shard, shard), shard)
    sequence[pl.ds(pl.multiple_of(t * rows, rows), rows), :] = input_ref[...]
    head_full[0, mine, :] = query_ref[...]
    head_full[1, mine, :] = key_ref[...]
    head_full[2, mine, :] = value_ref[...]

    pl.semaphore_wait(barrier, ranks - 1 + chips - 1 + 1)

    def shard_rows(index):
        return pl.ds(pl.multiple_of(index * shard, shard), shard)

    def gather(number, view):
        return Gather(
            here,
            view,
            (chip_send.at[number], chip_recv.at[number]),
            (core_send.at[number], core_recv.at[number]),
        )

    heads_gather = gather(0, lambda i: head_full.at[:, shard_rows(i)])
    mixing_gather = gather(1, lambda i: mixing_full.at[:, shard_rows(i)])
    feed_gathers = [
        [
            TreeGather(
                here,
                lambda i, s=s, kind=kind: feed_full.at[s, kind, shard_rows(i)],
                (chip_send.at[2 + 2 * s + kind], chip_recv.at[2 + 2 * s + kind]),
                (core_send.at[2 + 2 * s + kind], core_recv.at[2 + 2 * s + kind]),
                kind == 0,
            )
            for kind in range(2)
        ]
        for s in range(slices)
    ]

    def own(chunk):
        return pl.ds(chunk * step, step)

    def row_copy(s, side, chunk):
        block = sequence.at[pl.ds(pl.multiple_of(s * rows + chunk * step, step), step)]
        return pltpu.make_async_remote_copy(
            src_ref=block,
            dst_ref=block,
            send_sem=row_send.at[side, s, chunk],
            recv_sem=row_recv.at[s, chunk],
            device_id=here.rank(jnp.clip(t + (1 if side else -1), 0, last)),
            device_id_type=MESH,
        )

    @pl.when(t < last)
    def _():
        for c in range(chunks):
            row_copy(t, 1, c).start()

    @pl.when(t > 0)
    def _():
        for c in range(chunks):
            row_copy(t, 0, c).start()

    heads_gather.start()
    feed_full[0, 0, mine, :] = expand_ref[...]
    feed_full[0, 1, mine, :] = shrink_ref[...].T
    mixing_full[t, mine, :] = mixing_ref[...].T

    def weight_copy(k):
        return remote(
            mixing_full.at[t, mine],
            mixing_full.at[t, mine],
            (weight_send, weight_recv),
            k,
            here.rank(t ^ k),
        )

    def weight_arrival(k):
        theirs = mixing_full.at[t ^ k, mine]
        return remote(theirs, theirs, (weight_send, weight_recv), k, here.rank(t ^ k))

    pair_copies = [
        remote(
            feed_full.at[0, :, mine],
            feed_full.at[1, :, mine],
            (pair_send, pair_recv),
            0,
            here.rank(t ^ 2),
        ),
        remote(
            offset_full.at[0], offset_full.at[1], (pair_send, pair_recv), 1, here.rank(t ^ 2)
        ),
    ]

    def start_weights():
        for k in range(1, ranks):
            weight_copy(k).start()

    def start_pairs():
        for copy in pair_copies:
            copy.start()

    start_weights()

    def as_row(ref):
        return ref[...].astype(F32).reshape(1, ref.shape[0])

    head_offset_ref[0:1, :] = as_row(query_offset_ref)
    head_offset_ref[1:2, :] = as_row(value_offset_ref)
    offset_full[0] = as_row(expand_offset_ref)
    for index, ref in enumerate(
        (
            first_gain_ref,
            first_shift_ref,
            second_gain_ref,
            second_shift_ref,
            shrink_offset_ref,
            mixing_offset_ref,
        )
    ):
        vectors_ref[index : index + 1, :] = as_row(ref)
    first_gain = vectors_ref[0:1, :]
    first_shift = vectors_ref[1:2, :]
    second_gain = vectors_ref[2:3, :]
    second_shift = vectors_ref[3:4, :]
    shrink_offset = vectors_ref[4:5, :]
    mixing_offset = vectors_ref[5:6, :]

    start_pairs()
    heads_gather.forward()
    for kind in feed_gathers[0]:
        kind.start()
    heads_gather.finish()

    def project(s):
        place = pl.ds(pl.multiple_of(s * rows, rows), rows)
        block = sequence[place, :]
        query = (mm(block, head_full[0], NN) + head_offset_ref[0:1, :]) * (HD**-0.5)
        queries[s] = query.astype(BF)
        key = mm(block, head_full[1], NN)
        key_rows[place, :] = key.astype(BF)
        value = mm(block, head_full[2], NN) + head_offset_ref[1:2, :]
        values[place, :] = value.astype(BF)
        value_columns[:, place] = value.T.astype(BF)
        key_columns[:, place] = key.T.astype(BF)

    project(t)

    def gather_mixing():
        for k in range(1, ranks):
            weight_arrival(k).wait_recv()
        mixing_gather.start()

    def second_slice():
        for copy in pair_copies:
            copy.wait_recv()
        for kind in feed_gathers[1]:
            kind.start()

    def second_step():
        for kind in feed_gathers[1]:
            kind.advance(0)

    near = [
        [s for _, s in sorted((abs(s - u), s) for s in range(ranks) if s != u)]
        for u in range(ranks)
    ]
    for j in range(ranks - 1):
        s = chosen([near[u][j] for u in range(ranks)], t)
        for c in range(chunks):
            row_copy(s, 0, c).wait_recv()

            @pl.when(jnp.logical_and(s < t, t < last))
            def _():
                row_copy(s, 1, c).start()

            @pl.when(jnp.logical_and(s > t, t > 0))
            def _():
                row_copy(s, 0, c).start()

        project(s)
        if j == 0:
            for kind in feed_gathers[0]:
                kind.advance(0)
            gather_mixing()
        if j == 1:
            for kind in feed_gathers[0]:
                kind.advance_rest()
        if j == 2:

            @pl.when(jnp.logical_not(middle))
            def _():
                second_slice()


    def mix_copy(s):
        return pltpu.make_async_remote_copy(
            src_ref=mix_heads.at[s],
            dst_ref=mixed.at[t],
            send_sem=mix_send.at[s],
            recv_sem=mix_recv.at[t],
            device_id=here.rank(s),
            device_id_type=MESH,
        )

    def mix_arrival(s):
        return pltpu.make_async_remote_copy(
            src_ref=mix_heads.at[s],
            dst_ref=mixed.at[s],
            send_sem=mix_send.at[s],
            recv_sem=mix_recv.at[s],
            device_id=here.rank(s),
            device_id_type=MESH,
        )

    lane = lax.broadcasted_iota(jnp.int32, (1, 128), 1)

    def attend(s):
        place = pl.ds(pl.multiple_of(s * rows, rows), rows)
        columns = []
        for h in range(heads):
            pair = slice(128 * (h // 2), 128 * (h // 2) + 128)
            side = (lane // HD) == (h % 2)
            query = jnp.where(side, queries[s, :, pair], jnp.zeros((), BF))
            scores = [
                mm(key_rows[k * rows : (k + 1) * rows, pair], query, NT) for k in range(ranks)
            ]
            largest = functools.reduce(
                jnp.maximum, [jnp.max(block, axis=0, keepdims=True) for block in scores]
            )
            total, column = 0.0, 0.0
            for k in range(ranks):
                weights = jnp.exp(scores[k] - largest)
                total = total + jnp.sum(weights, axis=0, keepdims=True)
                column = column + mm(
                    value_columns[h * HD : (h + 1) * HD, k * rows : (k + 1) * rows],
                    weights.astype(BF),
                    NN,
                )
            columns.append(column / total)
            log_totals[h : h + 1, place] = largest + jnp.log(total)
        mix_heads[s] = jnp.concatenate(columns, axis=0).T.astype(BF)

    far = [[s for s in reversed(near[u])] + [u] for u in range(ranks)]
    for j in range(ranks):
        s = chosen([far[u][j] for u in range(ranks)], t)
        attend(s)
        if j < ranks - 1:
            mix_copy(s).start()
        if j == 0:

            @pl.when(middle)
            def _():
                second_slice()

        if j == 1:
            mixing_gather.forward()

    mixed[t] = mix_heads[t]
    second_step()
    for k in range(1, ranks):
        mix_arrival(t ^ k).wait_recv()
    mixing_gather.finish()

    def mix_tile(tile):
        total = input_ref[:, tile].astype(F32) + vectors_ref[5:6, tile]
        for j in range(ranks):
            total = total + mm(mixed[j], mixing_full[j, tile, :], NT)
        attended_ref[:, tile] = total

    tiles(width, mix_tile)

    def other(chunk):
        return pl.ds(rows + chunk * step, step)

    def exchange(kind, chunk, source, target):
        return pltpu.make_async_remote_copy(
            src_ref=source,
            dst_ref=target,
            send_sem=swap_send.at[kind, chunk],
            recv_sem=swap_recv.at[kind, chunk],
            device_id=partner,
            device_id_type=MESH,
        )

    copies = [
        [exchange(0, c, normed.at[own(c)], normed.at[other(c)]) for c in range(chunks)],
        [exchange(1, c, send_part.at[0, own(c)], recv_part.at[0, own(c)]) for c in range(chunks)],
        [exchange(2, c, summed_low.at[own(c)], summed_low.at[other(c)]) for c in range(chunks)],
        [exchange(3, c, send_part.at[1, own(c)], recv_part.at[1, own(c)]) for c in range(chunks)],
    ]
    for c in range(chunks):
        normal, _ = norm_parts(attended_ref[own(c), :])
        normed[own(c), :] = (normal * first_gain + first_shift).astype(BF)
        copies[0][c].start()

    def forward(place, store, ready):
        for s in range(slices):
            ready(s)

            def grow(tile):
                value = mm(normed[place, :], feed_full[s, 0, :, tile], NN)
                value = value + offset_full[s, :, tile]
                share = 0.5 * (1.0 + lax.erf(value * 0.7071067811865476))
                density = jnp.exp(-0.5 * value * value) * 0.3989422804014327
                hidden[s, place, tile] = (value * share).astype(BF)
                slope[s, place, tile] = (share + value * density).astype(BF)

            tiles(units, grow)

        def shrink(tile):
            total = mm(hidden[0, place, :], feed_full[0, 1, tile, :], NT)
            for s in range(1, slices):
                total = total + mm(hidden[s, place, :], feed_full[s, 1, tile, :], NT)
            store(tile, total)

        tiles(width, shrink)

    def backward(place, store):
        for s in range(slices):

            def narrow(tile):
                value = mm(summed_low[place, :], feed_full[s, 1, :, tile], NN)
                value = value * slope[s, place, tile].astype(F32)
                slope[s, place, tile] = value.astype(BF)

            tiles(units, narrow)

        def widen(tile):
            total = mm(slope[0, place, :], feed_full[0, 0, tile, :], NT)
            for s in range(1, slices):
                total = total + mm(slope[s, place, :], feed_full[s, 0, tile, :], NT)
            store(tile, total)

        tiles(width, widen)

    def keep(tile, total):
        own_part[:, tile] = total

    def pass_on(which, chunk):
        def store(tile, total):
            send_part[which, own(chunk), tile] = total.astype(BF)

        return store

    def arrive(s):
        for kind in feed_gathers[s]:
            if s > 0:
                kind.advance_rest()
            kind.finish()

    forward(pl.ds(0, rows), keep, arrive)
    for c in range(chunks):
        copies[0][c].wait_recv()
        forward(other(c), pass_on(0, c), lambda s: None)
        copies[1][c].start()

    vector_own[...] = jnp.zeros_like(vector_own)
    for c in range(chunks):
        copies[1][c].wait_recv()
        normal, _ = norm_parts(attended_ref[own(c), :])
        first_norm = normal * first_gain + first_shift
        summed = (
            first_norm
            + (own_part[own(c), :] + recv_part[0, own(c), :].astype(F32))
            + shrink_offset
        )
        normal, rate = norm_parts(summed)
        output_ref[own(c), :] = (normal * second_gain + second_shift).astype(BF)
        upstream = cotangent_ref[own(c), :].astype(F32)
        grad = norm_back(upstream, second_gain, normal, rate)
        summed_grad[own(c), :] = grad
        summed_low[own(c), :] = grad.astype(BF)
        copies[2][c].start()
        vector_own[0:1, :] += column_sum(upstream * normal)
        vector_own[1:2, :] += column_sum(upstream)
        vector_own[2:3, :] += column_sum(grad)

    backward(pl.ds(0, rows), keep)
    for c in range(chunks):
        copies[2][c].wait_recv()
        backward(other(c), pass_on(1, c))
        copies[3][c].start()

    for kind in feed_gathers[0] + feed_gathers[1]:
        kind.drain()
    for copy in pair_copies:
        copy.wait_send()
    pl.semaphore_signal(free_sem, inc=1, device_id=here.core(), device_id_type=MESH)

    def spare_rows(k):
        return pl.ds(pl.multiple_of(width // 2 + k * shard, shard), shard)

    def reduce(number, source, core_slot, chip_slot):
        return Reduce(
            here,
            source,
            core_slot,
            chip_slot,
            (chip_send.at[number], chip_recv.at[number]),
            (core_send.at[number], core_recv.at[number]),
        )

    feed_reduces = [
        [
            TreeReduce(
                here,
                lambda i, s=s, kind=kind: feed_sum.at[s, kind, shard_rows(i)],
                lambda k, s=s, kind=kind: feed_full.at[s, kind, shard_rows(k)],
                lambda k, s=s, kind=kind: feed_chip.at[s, k - 1, kind],
                (chip_send.at[6 + 2 * s + kind], chip_recv.at[6 + 2 * s + kind]),
                (core_send.at[6 + 2 * s + kind], core_recv.at[6 + 2 * s + kind]),
                kind == 0,
            )
            for kind in range(2)
        ]
        for s in range(slices)
    ]
    mixing_reduce = reduce(
        10,
        lambda i: mixing_sum.at[shard_rows(i)],
        lambda k: feed_full.at[0, 0, spare_rows(k)],
        lambda k: mixing_chip.at[k - 1],
    )
    head_reduce = reduce(
        11,
        lambda i: head_sum.at[shard_rows(i)],
        lambda k: feed_full.at[0, 1, spare_rows(k), 0 : 3 * span],
        lambda k: head_chip.at[k - 1],
    )

    for s in reversed(range(slices)):

        def weigh(tile):
            left = min(TILE, width)
            for m in range(width // left):
                part = pl.ds(m * left, left)
                feed_sum[s, 1, part, tile] = mm(summed_low[:, part], hidden[s, :, tile], TN).astype(BF)
                feed_sum[s, 0, part, tile] = mm(normed[:, part], slope[s, :, tile], TN).astype(BF)
            vector_own[6 + s : 7 + s, tile] = column_sum(slope[s, :, tile].astype(F32))

        tiles(units, weigh)
        if s == slices - 1:
            pl.semaphore_wait(free_sem, 1)
        for kind in feed_reduces[s]:
            kind.start()

    def back_copy(s, chunk):
        return pltpu.make_async_remote_copy(
            src_ref=mix_back_send.at[s, own(chunk)],
            dst_ref=mix_back.at[t, own(chunk)],
            send_sem=back_send.at[chunk, s],
            recv_sem=back_recv.at[chunk, t],
            device_id=here.rank(s),
            device_id_type=MESH,
        )

    def back_arrival(s, chunk):
        return pltpu.make_async_remote_copy(
            src_ref=mix_back_send.at[s, own(chunk)],
            dst_ref=mix_back.at[s, own(chunk)],
            send_sem=back_send.at[chunk, s],
            recv_sem=back_recv.at[chunk, s],
            device_id=here.rank(s),
            device_id_type=MESH,
        )

    for c in range(chunks):
        copies[3][c].wait_recv()
        normal, rate = norm_parts(attended_ref[own(c), :])
        upstream = summed_grad[own(c), :] + (
            own_part[own(c), :] + recv_part[1, own(c), :].astype(F32)
        )
        grad = norm_back(upstream, first_gain, normal, rate)
        input_grad_ref[own(c), :] = grad
        attended_low[own(c), :] = grad.astype(BF)
        for j in range(ranks):
            s = chosen([far[u][j] for u in range(ranks)], t)
            block = mm(attended_low[own(c), :], mixing_full[s], NN).astype(BF)
            if j < ranks - 1:
                mix_back_send[s, own(c), :] = block
                back_copy(s, c).start()
            else:
                mix_back[s, own(c), :] = block
        vector_own[3:4, :] += column_sum(upstream * normal)
        vector_own[4:5, :] += column_sum(upstream)
        vector_own[5:6, :] += column_sum(grad)

    for j in range(ranks):
        mixing_sum[:, j * span : (j + 1) * span] = mm(attended_low[...], mixed[j], TN).astype(BF)
    mixing_reduce.start()
    for kind in feed_reduces[1]:
        kind.combine()

    own_part[...] = jnp.zeros_like(own_part)
    summed_grad[...] = jnp.zeros_like(summed_grad)

    def pair_back():
        return remote(
            feed_sum.at[1, :, mine], feed_pair, (pair_send, pair_recv), 2, here.rank(t ^ 2)
        )

    def pair_start():
        for kind in range(2):
            feed_sum[1, kind, mine, :] = feed_reduces[1][kind].total().astype(BF)
        pair_back().start()

    def attend_back(s):
        place = pl.ds(pl.multiple_of(s * rows, rows), rows)
        inner = (mix_back[s].astype(F32) * mix_heads[s].astype(F32)).T
        columns = []
        for h in range(heads):
            pair = slice(128 * (h // 2), 128 * (h // 2) + 128)
            side = (lane // HD) == (h % 2)
            none = jnp.zeros((), BF)
            query = jnp.where(side, queries[s, :, pair], none)
            upstream = jnp.where(side, mix_back[s, :, pair], none)
            delta = jnp.sum(inner[h * HD : (h + 1) * HD, :], axis=0, keepdims=True)
            log_total = log_totals[h : h + 1, place]
            column = None
            for k in range(ranks):
                part = slice(k * rows, (k + 1) * rows)
                lanes = slice(k * span + pair.start, k * span + pair.stop)
                scores = mm(key_rows[part, pair], query, NT)
                probs = jnp.exp(scores - log_total)
                prob_grad = mm(values[part, pair], upstream, NT)
                score_low = (probs * (prob_grad - delta)).astype(BF)
                summed_grad[:, lanes] += mm(probs.astype(BF), upstream, NN)
                own_part[:, lanes] += mm(score_low, query, NN)
                term = mm(key_columns[h * HD : (h + 1) * HD, part], score_low, NN)
                column = term if column is None else column + term
            columns.append(column)
        low = jnp.concatenate(columns, axis=0).T.astype(BF)
        query_low[place, :] = (low.astype(F32) * HD**-0.5).astype(BF)

    for j in range(ranks):
        s = t if j == 0 else chosen([near[u][j - 1] for u in range(ranks)], t)
        if j > 0:
            for c in range(chunks):
                back_arrival(s, c).wait_recv()
        attend_back(s)
        if j == 1:
            for kind in feed_reduces[1]:
                kind.advance(0)
            for kind in feed_reduces[0]:
                kind.combine()
            mixing_reduce.combine()
        if j == 3:
            for kind in feed_reduces[1]:
                kind.advance_rest()
            pair_start()
            for kind in feed_reduces[0]:
                kind.advance(0)
    for k in range(ranks):
        part = slice(k * rows, (k + 1) * rows)
        lanes = slice(k * span, (k + 1) * span)
        key_low[part, :] = own_part[:, lanes].astype(BF)
        value_low[part, :] = summed_grad[:, lanes].astype(BF)

    def input_part(s, tile):
        place = pl.ds(pl.multiple_of(s * rows, rows), rows)
        return (
            mm(query_low[place, :], head_full[0, tile, :], NT)
            + mm(key_low[place, :], head_full[1, tile, :], NT)
            + mm(value_low[place, :], head_full[2, tile, :], NT)
        )

    def arrival_time(u, s):
        if s > u:
            u, s = last - u, last - s
        return s if u == last else s + 1 + last - 1 - u

    line_order = [
        sorted([s for s in range(ranks) if s != u], key=lambda s, u=u: (arrival_time(u, s), s))
        for u in range(ranks)
    ]

    def line_rows(j):
        return pl.ds((j % 2) * rows, rows)

    def line_send_ref(j, chunk):
        return hidden.at[j // 2, pl.ds((j % 2) * rows + chunk * step, step)]

    def line_copy(j, s, chunk):
        slot = jnp.where(s == t + 1, ranks, s)
        return pltpu.make_async_remote_copy(
            src_ref=line_send_ref(j, chunk),
            dst_ref=line_part.at[slot, own(chunk)],
            send_sem=line_send.at[j, chunk],
            recv_sem=line_recv.at[slot, chunk],
            device_id=here.rank(jnp.clip(jnp.where(s < t, t - 1, t + 1), 0, last)),
            device_id_type=MESH,
        )

    def line_arrival(slot, chunk):
        return pltpu.make_async_remote_copy(
            src_ref=line_part.at[slot, own(chunk)],
            dst_ref=line_part.at[slot, own(chunk)],
            send_sem=line_send.at[0, chunk],
            recv_sem=line_recv.at[slot, chunk],
            device_id=partner,
            device_id_type=MESH,
        )

    targets = [chosen([line_order[u][j] for u in range(ranks)], t) for j in range(ranks - 1)]
    opens = [
        jnp.logical_or(jnp.logical_and(s < t, t == last), jnp.logical_and(s > t, t == 0))
        for s in targets
    ]
    for j, s in enumerate(targets):

        def store(tile):
            hidden[j // 2, line_rows(j), tile] = input_part(s, tile).astype(BF)

        tiles(width, store)

        @pl.when(opens[j])
        def _():
            for c in range(chunks):
                line_copy(j, s, c).start()

    def weigh_heads(tile):
        for i, low in enumerate((query_low, key_low, value_low)):
            head_sum[tile, i * span : (i + 1) * span] = mm(sequence[:, tile], low[...], TN).astype(BF)

    tiles(width, weigh_heads)
    head_reduce.start()
    vector_own[8:9, 0:span] = column_sum(query_low[...].astype(F32))
    vector_own[8:9, span : 2 * span] = column_sum(value_low[...].astype(F32))

    def vector_core_copy():
        return remote(
            vector_own, vector_core, (core_send.at[12], core_recv.at[12]), 0, here.core()
        )

    vector_core_copy().start()

    def store_own(tile):
        input_grad_ref[:, tile] = input_grad_ref[:, tile] + input_part(t, tile)

    tiles(width, store_own)

    def pass_line(j, s):
        @pl.when(jnp.logical_not(opens[j]))
        def _():
            for c in range(chunks):
                line_arrival(s, c).wait_recv()
                block = line_send_ref(j, c)
                block[...] = (
                    block[...].astype(F32) + line_part[s, own(c), :].astype(F32)
                ).astype(BF)
                line_copy(j, s, c).start()

    vector_core_copy().wait()
    vector_own[...] = vector_own[...] + vector_core[...]

    def vector_chip_copy(k):
        return remote(
            vector_own,
            vector_chip.at[k - 1],
            (chip_send.at[12], chip_recv.at[12]),
            k,
            here.chip(k),
        )

    each(chips, 1, lambda k: vector_chip_copy(k).start())
    head_reduce.combine()

    def span_lanes(j):
        return pl.ds(pl.multiple_of(j * span, span), span)

    def mixing_rank_copy(k):
        return remote(
            mixing_sum.at[mine, span_lanes(t ^ k)],
            mixing_rank.at[k - 1],
            (rank_send.at[0], rank_recv.at[0]),
            k,
            here.rank(t ^ k),
        )

    pass_line(0, targets[0])
    mixing_sum[mine, :] = mixing_reduce.total().astype(BF)
    for k in range(1, ranks):
        mixing_rank_copy(k).start()
    for k in range(1, ranks - 1):
        pass_line(k, targets[k])

    each(chips, 1, lambda k: vector_chip_copy(k).wait())
    vector_sum = vector_own[...]
    for k in range(1, chips):
        vector_sum = vector_sum + vector_chip[k - 1]
    vector_core[...] = vector_sum

    def vector_rank_copy(k):
        return remote(
            vector_core,
            vector_rank.at[k - 1],
            (rank_send.at[1], rank_recv.at[1]),
            k,
            here.rank(t ^ k),
        )

    for k in range(1, ranks):
        vector_rank_copy(k).start()

    head_total = head_reduce.total()
    for i in range(3):
        head_grad_ref[i] = head_total[:, i * span : (i + 1) * span]
    feed_own = []
    for kind in feed_reduces[0]:
        kind.advance_rest()
        feed_own.append(kind.total())
    for k in range(1, ranks):
        mixing_rank_copy(k).wait()
    mixing_grad = mixing_sum[mine, span_lanes(t)].astype(F32)
    for k in range(1, ranks):
        mixing_grad = mixing_grad + mixing_rank[k - 1].astype(F32)
    mixing_grad_ref[...] = mixing_grad
    pair_back().wait()
    expand_grad_ref[...] = feed_own[0] + feed_pair[0].astype(F32)
    shrink_grad_ref[...] = feed_own[1] + feed_pair[1].astype(F32)
    for k in range(1, ranks):
        vector_rank_copy(k).wait()
    vector_sum = vector_core[...]
    sums_ref[...] = vector_sum
    everywhere = vector_sum[0:6, :]
    for k in range(1, ranks):
        everywhere = everywhere + vector_rank[k - 1, 0:6, :]
    sums_ref[0:6, :] = everywhere
    sums_ref[6:7, :] = vector_sum[6:7, :] + vector_rank[1, 7:8, :]

    @pl.when(t < last)
    def _():
        for c in range(chunks):
            line_arrival(t, c).wait_recv()
            input_grad_ref[own(c), :] += line_part[t, own(c), :].astype(F32)

    @pl.when(t > 0)
    def _():
        for c in range(chunks):
            line_arrival(ranks, c).wait_recv()
            input_grad_ref[own(c), :] += line_part[ranks, own(c), :].astype(F32)

    for j in range(ranks - 1):
        for c in range(chunks):
            line_copy(j, targets[j], c).wait_send()
            back_copy(t ^ (j + 1), c).wait_send()
    for each_reduce in feed_reduces[0] + feed_reduces[1] + [mixing_reduce, head_reduce]:
        each_reduce.drain()
    for kind in range(4):
        for c in range(chunks):
            copies[kind][c].wait_send()
    for each_gather in (heads_gather, mixing_gather):
        each_gather.drain()
    for k in range(1, ranks):
        mix_copy(t ^ k).wait_send()
        weight_copy(k).wait_send()
    for s in range(ranks):

        @pl.when(jnp.logical_and(s <= t, t < last))
        def _():
            for c in range(chunks):
                row_copy(s, 1, c).wait_send()

        @pl.when(jnp.logical_and(s >= t, t > 0))
        def _():
            for c in range(chunks):
                row_copy(s, 0, c).wait_send()


def layer(devices, ranks, inputs):
    layer_input = inputs[0]
    rows, width = layer_input.shape
    span = inputs[1].shape[1]
    units = inputs[5].shape[1]
    slices = 2
    chunks = 2
    chips = devices // 2
    length = ranks * rows
    both = 2 * rows
    vmem = pl.BlockSpec(memory_space=pltpu.VMEM)
    dma = pltpu.SemaphoreType.DMA
    shard = width // devices
    outs = (
        jax.ShapeDtypeStruct((rows, width), BF),
        jax.ShapeDtypeStruct((rows, width), F32),
        jax.ShapeDtypeStruct((3, shard, span), F32),
        jax.ShapeDtypeStruct((shard, span), F32),
        jax.ShapeDtypeStruct((shard, units), F32),
        jax.ShapeDtypeStruct((shard, units), F32),
        jax.ShapeDtypeStruct((16, width), F32),
    )
    return pl.pallas_call(
        functools.partial(layer_kernel, devices, chunks),
        out_shape=outs,
        in_specs=[vmem] * len(inputs),
        out_specs=[vmem] * len(outs),
        scratch_shapes=[
            pltpu.VMEM((length, width), BF),
            pltpu.VMEM((ranks, rows, span), BF),
            pltpu.VMEM((length, span), BF),
            pltpu.VMEM((length, span), BF),
            pltpu.VMEM((ranks, rows, span), BF),
            pltpu.VMEM((8, length), F32),
            pltpu.VMEM((3, width, span), BF),
            pltpu.VMEM((ranks, width, span), BF),
            pltpu.VMEM((slices, 2, width, units), BF),
            pltpu.VMEM((slices, 1, units), F32),
            pltpu.VMEM((8, span), F32),
            pltpu.VMEM((8, width), F32),
            pltpu.VMEM((span, length), BF),
            pltpu.VMEM((span, length), BF),
            pltpu.VMEM((ranks, rows, span), BF),
            pltpu.VMEM((rows, width), F32),
            pltpu.VMEM((both, width), BF),
            pltpu.VMEM((slices, both, units), BF),
            pltpu.VMEM((slices, both, units), BF),
            pltpu.VMEM((both, width), BF),
            pltpu.VMEM((rows, width), F32),
            pltpu.VMEM((rows, width), F32),
            pltpu.VMEM((2, rows, width), BF),
            pltpu.VMEM((2, rows, width), BF),
            pltpu.VMEM((slices, 2, width, units), BF),
            pltpu.VMEM((slices, chips - 1, 2, shard, units), BF),
            pltpu.VMEM((2, shard, units), BF),
            pltpu.VMEM((width, ranks * span), BF),
            pltpu.VMEM((chips - 1, shard, ranks * span), BF),
            pltpu.VMEM((ranks - 1, shard, span), BF),
            pltpu.VMEM((width, 3 * span), BF),
            pltpu.VMEM((chips - 1, shard, 3 * span), BF),
            pltpu.VMEM((rows, width), BF),
            pltpu.VMEM((ranks, rows, span), BF),
            pltpu.VMEM((ranks, rows, span), BF),
            pltpu.VMEM((length, span), BF),
            pltpu.VMEM((length, span), BF),
            pltpu.VMEM((length, span), BF),
            pltpu.VMEM((ranks + 1, rows, width), BF),
            pltpu.VMEM((16, width), F32),
            pltpu.VMEM((16, width), F32),
            pltpu.VMEM((chips - 1, 16, width), F32),
            pltpu.VMEM((ranks - 1, 16, width), F32),
            dma((2, ranks, chunks)),
            dma((ranks, chunks)),
            dma((ranks,)),
            dma((ranks,)),
            dma((ranks,)),
            dma((ranks,)),
            dma((3,)),
            dma((3,)),
            dma((13, chips)),
            dma((13, chips)),
            dma((13, chips)),
            dma((13, chips)),
            dma((4, chunks)),
            dma((4, chunks)),
            dma((chunks, ranks)),
            dma((chunks, ranks)),
            dma((ranks - 1, chunks)),
            dma((ranks + 1, chunks)),
            dma((2, ranks)),
            dma((2, ranks)),
            pltpu.SemaphoreType.REGULAR,
        ],
        compiler_params=pltpu.CompilerParams(
            collective_id=1, has_side_effects=True, vmem_limit_bytes=VMEM_LIMIT
        ),
    )(*inputs)


def body(
    layer_input,
    query_weight,
    key_weight,
    value_weight,
    mixing_weight,
    expand_weight,
    shrink_weight,
    query_offset,
    value_offset,
    mixing_offset,
    expand_offset,
    shrink_offset,
    first_gain,
    first_shift,
    second_gain,
    second_shift,
    cotangent,
):
    results = layer(
        lax.axis_size("dp"),
        lax.axis_size("tensor"),
        (
            layer_input,
            query_weight,
            key_weight,
            value_weight,
            mixing_weight,
            expand_weight,
            shrink_weight,
            query_offset,
            value_offset,
            mixing_offset,
            expand_offset,
            shrink_offset,
            first_gain,
            first_shift,
            second_gain,
            second_shift,
            cotangent,
        ),
    )
    return place_outputs(results, expand_weight.shape[1], query_weight.shape[1])


def solution(mesh):
    rows = P(("dp", "tensor"), None)
    tall = P("dp", "tensor")
    wide = P("tensor", "dp")
    split = P("tensor")
    whole = P()
    return jax.shard_map(
        body,
        mesh=mesh,
        in_specs=(rows, tall, tall, tall, wide, tall, wide, split, split)
        + (whole, split, whole, whole, whole, whole, whole, rows),
        out_specs=(rows, rows, tall, tall, tall, wide, tall, wide, split, split)
        + (whole, split, whole, whole, whole, whole, whole),
        check_vma=False,
    )
```

```python
import functools

import jax
import jax.numpy as jnp
from jax import lax
from jax.experimental import pallas as pl
from jax.experimental.pallas import tpu as pltpu
from jax.sharding import PartitionSpec as P

HD = 64
EPSILON = 1e-05
MESH = pl.DeviceIdType.MESH
BF = jnp.bfloat16
F32 = jnp.float32
NN = (((1,), (0,)), ((), ()))
NT = (((1,), (1,)), ((), ()))
TN = (((0,), (0,)), ((), ()))
VMEM_LIMIT = 60 * 1024 * 1024
TILE = 512


def mm(left, right, dims):
    return lax.dot_general(left, right, dims, preferred_element_type=F32)


def norm_parts(inputs):
    centered = inputs - jnp.mean(inputs, axis=-1, keepdims=True)
    variance = jnp.mean(centered * centered, axis=-1, keepdims=True)
    rate = lax.rsqrt(variance + EPSILON)
    return centered * rate, rate


def norm_back(upstream, gain, normal, rate):
    scaled = upstream * gain
    mean_scaled = jnp.mean(scaled, axis=-1, keepdims=True)
    mean_normal = jnp.mean(scaled * normal, axis=-1, keepdims=True)
    return rate * (scaled - mean_scaled - normal * mean_normal)


def column_sum(block):
    return jnp.sum(block, axis=0, keepdims=True)


def tiles(width, body):
    step = min(TILE, width)

    def one(index, carry):
        body(pl.ds(pl.multiple_of(index * step, step), step))
        return carry

    lax.fori_loop(0, width // step, one, 0)


def chosen(table, index):
    value = jnp.int32(table[0])
    for place in range(1, len(table)):
        value = jnp.where(index == place, jnp.int32(table[place]), value)
    return value


def each(count, start, body):
    if count - start <= 8:
        for index in range(start, count):
            body(index)
        return

    def one(index, carry):
        body(index)
        return carry

    lax.fori_loop(start, count, one, 0)


class Place:
    def __init__(self, devices, ranks):
        self.d = lax.axis_index("dp")
        self.t = lax.axis_index("tensor")
        self.chips = devices // 2
        self.ranks = ranks
        self.c = self.d % 2
        self.p = self.d // 2

    def chip(self, k):
        return {"dp": 2 * (self.p ^ k) + self.c}

    def core(self):
        return {"dp": self.d ^ 1}

    def rank(self, t):
        return {"tensor": t}


def remote(source, target, sems, index, device):
    send, recv = sems
    return pltpu.make_async_remote_copy(
        src_ref=source,
        dst_ref=target,
        send_sem=send.at[index],
        recv_sem=recv.at[index],
        device_id=device,
        device_id_type=MESH,
    )


class Gather:
    def __init__(self, here, view, chip_sems, core_sems):
        self.here, self.view = here, view
        self.chip_sems, self.core_sems = chip_sems, core_sems

    def chip_copy(self, k):
        here = self.here
        mine = self.view(2 * here.p + here.c)
        return remote(mine, mine, self.chip_sems, k, here.chip(k))

    def chip_arrival(self, k):
        here = self.here
        theirs = self.view(2 * (here.p ^ k) + here.c)
        return remote(theirs, theirs, self.chip_sems, k, here.chip(k))

    def core_copy(self, k):
        here = self.here
        shard = self.view(2 * (here.p ^ k) + here.c)
        return remote(shard, shard, self.core_sems, k, here.core())

    def core_arrival(self, k):
        here = self.here
        shard = self.view(2 * (here.p ^ k) + 1 - here.c)
        return remote(shard, shard, self.core_sems, k, here.core())

    def start(self):
        each(self.here.chips, 1, lambda k: self.chip_copy(k).start())
        self.core_copy(0).start()

    def forward(self):
        def one(k):
            self.chip_arrival(k).wait_recv()
            self.core_copy(k).start()

        each(self.here.chips, 1, one)

    def finish(self):
        each(self.here.chips, 0, lambda k: self.core_arrival(k).wait_recv())

    def drain(self):
        each(self.here.chips, 1, lambda k: self.chip_copy(k).wait_send())
        each(self.here.chips, 0, lambda k: self.core_copy(k).wait_send())


class Reduce:
    def __init__(self, here, source, core_slot, chip_slot, chip_sems, core_sems):
        self.here, self.source = here, source
        self.core_slot, self.chip_slot = core_slot, chip_slot
        self.chip_sems, self.core_sems = chip_sems, core_sems

    def core_copy(self, k):
        here = self.here
        shard = self.source(2 * (here.p ^ k) + 1 - here.c)
        return remote(shard, self.core_slot(k), self.core_sems, k, here.core())

    def chip_copy(self, k):
        here = self.here
        shard = self.source(2 * (here.p ^ k) + here.c)
        return remote(shard, self.chip_slot(k), self.chip_sems, k, here.chip(k))

    def start(self):
        each(self.here.chips, 1, lambda k: self.core_copy(k).start())
        self.core_copy(0).start()

    def combine(self):
        here = self.here

        def one(k):
            self.core_copy(k).wait_recv()
            shard = self.source(2 * (here.p ^ k) + here.c)
            shard[...] = shard[...] + self.core_slot(k)[...]

        def send(k):
            one(k)
            self.chip_copy(k).start()

        each(here.chips, 1, send)
        one(0)

    def total(self):
        here = self.here
        each(here.chips, 1, lambda k: self.chip_copy(k).wait_recv())
        value = self.source(here.d)[...].astype(F32)
        for k in range(1, here.chips):
            value = value + self.chip_slot(k)[...].astype(F32)
        return value

    def drain(self):
        each(self.here.chips, 1, lambda k: self.chip_copy(k).wait_send())
        each(self.here.chips, 0, lambda k: self.core_copy(k).wait_send())


class TreeGather(Gather):
    def __init__(self, here, view, chip_sems, core_sems, rising):
        super().__init__(here, view, chip_sems, core_sems)
        self.rising = rising
        self.steps = here.chips.bit_length() - 1

    def bit(self, i):
        return 1 << i if self.rising else self.here.chips >> (i + 1)

    def held(self, i, j):
        return j if self.rising else j << (self.steps - i)

    def step_copy(self, i, j):
        here = self.here
        mask = self.held(i, j)
        shard = self.view(2 * (here.p ^ mask) + here.c)
        bit = self.bit(i)
        return remote(shard, shard, self.chip_sems, mask ^ bit, here.chip(bit))

    def step_arrival(self, i, j):
        here = self.here
        bit = self.bit(i)
        key = self.held(i, j) ^ bit
        shard = self.view(2 * (here.p ^ key) + here.c)
        return remote(shard, shard, self.chip_sems, key, here.chip(bit))

    def start(self):
        each(1, 0, lambda j: self.step_copy(0, j).start())
        self.core_copy(0).start()

    def advance(self, i):
        count = 1 << i
        each(count, 0, lambda j: self.step_arrival(i, j).wait_recv())
        if i + 1 < self.steps:
            each(2 * count, 0, lambda j: self.step_copy(i + 1, j).start())
        each(count, 0, lambda j: self.core_copy(self.held(i, j) ^ self.bit(i)).start())

    def advance_rest(self):
        for i in range(1, self.steps):
            self.advance(i)

    def drain(self):
        for i in range(self.steps):
            each(1 << i, 0, lambda j: self.step_copy(i, j).wait_send())
        each(self.here.chips, 0, lambda k: self.core_copy(k).wait_send())


class TreeReduce(Reduce):
    def __init__(self, here, source, core_slot, chip_slot, chip_sems, core_sems, rising):
        super().__init__(here, source, core_slot, chip_slot, chip_sems, core_sems)
        self.rising = rising
        self.steps = here.chips.bit_length() - 1

    def bit(self, i):
        return 1 << i if self.rising else self.here.chips >> (i + 1)

    def rest(self, i, j):
        return j << (i + 1) if self.rising else j

    def count(self, i):
        return 1 << (self.steps - 1 - i)

    def step_copy(self, i, j):
        here = self.here
        bit = self.bit(i)
        key = self.rest(i, j) ^ bit
        shard = self.source(2 * (here.p ^ key) + here.c)
        return remote(shard, self.chip_slot(key), self.chip_sems, key, here.chip(bit))

    def combine(self):
        here = self.here

        def one(k):
            self.core_copy(k).wait_recv()
            shard = self.source(2 * (here.p ^ k) + here.c)
            shard[...] = shard[...] + self.core_slot(k)[...]

        each(here.chips, 1, one)
        one(0)
        each(self.count(0), 0, lambda j: self.step_copy(0, j).start())

    def advance(self, i):
        here = self.here

        def one(j):
            mask = self.rest(i, j)
            self.step_copy(i, j).wait_recv()
            shard = self.source(2 * (here.p ^ mask) + here.c)
            shard[...] = shard[...] + self.chip_slot(mask ^ self.bit(i))[...]

        each(self.count(i), 0, one)
        each(self.count(i + 1), 0, lambda j: self.step_copy(i + 1, j).start())

    def advance_rest(self):
        for i in range(1, self.steps - 1):
            self.advance(i)

    def total(self):
        final = self.steps - 1
        self.step_copy(final, 0).wait_recv()
        value = self.source(self.here.d)[...].astype(F32)
        return value + self.chip_slot(self.bit(final))[...].astype(F32)

    def drain(self):
        for i in range(self.steps):
            each(self.count(i), 0, lambda j: self.step_copy(i, j).wait_send())
        each(self.here.chips, 0, lambda k: self.core_copy(k).wait_send())


def place_kernel(
    layer_output_ref,
    input_sum_ref,
    head_sum_ref,
    mixing_sum_ref,
    expand_sum_ref,
    shrink_sum_ref,
    sums_ref,
    output_ref,
    input_ref,
    query_ref,
    key_ref,
    value_ref,
    mixing_ref,
    expand_ref,
    shrink_ref,
    query_offset_ref,
    value_offset_ref,
    mixing_offset_ref,
    expand_offset_ref,
    shrink_offset_ref,
    first_gain_ref,
    first_shift_ref,
    second_gain_ref,
    second_shift_ref,
):
    output_ref[...] = layer_output_ref[...]
    input_ref[...] = input_sum_ref[...]
    query_ref[...] = head_sum_ref[0]
    key_ref[...] = head_sum_ref[1]
    value_ref[...] = head_sum_ref[2]
    mixing_ref[...] = mixing_sum_ref[...].T
    expand_ref[...] = expand_sum_ref[...]
    shrink_ref[...] = shrink_sum_ref[...].T

    def row(ref, index, start=0):
        size = ref.shape[0]
        ref[...] = sums_ref[index : index + 1, start : start + size].reshape(size)

    row(query_offset_ref, 8)
    row(value_offset_ref, 8, query_offset_ref.shape[0])
    row(mixing_offset_ref, 5)
    row(expand_offset_ref, 6)
    row(shrink_offset_ref, 2)
    row(first_gain_ref, 3)
    row(first_shift_ref, 4)
    row(second_gain_ref, 0)
    row(second_shift_ref, 1)


def place_outputs(results, units, span):
    rows, width = results[1].shape
    shard = results[2].shape[1]
    shapes = [
        ((rows, width), BF),
        ((rows, width), F32),
        ((shard, span), F32),
        ((shard, span), F32),
        ((shard, span), F32),
        ((span, shard), F32),
        ((shard, units), F32),
        ((units, shard), F32),
        ((span,), F32),
        ((span,), F32),
        ((width,), F32),
        ((units,), F32),
    ] + [((width,), F32)] * 5
    vmem = pl.BlockSpec(memory_space=pltpu.VMEM)
    return pl.pallas_call(
        place_kernel,
        out_shape=tuple(jax.ShapeDtypeStruct(shape, kind) for shape, kind in shapes),
        in_specs=[vmem] * len(results),
        out_specs=[vmem] * len(shapes),
    )(*results)


def layer_kernel(
    devices,
    chunks,
    input_ref,
    query_ref,
    key_ref,
    value_ref,
    mixing_ref,
    expand_ref,
    shrink_ref,
    query_offset_ref,
    value_offset_ref,
    mixing_offset_ref,
    expand_offset_ref,
    shrink_offset_ref,
    first_gain_ref,
    first_shift_ref,
    second_gain_ref,
    second_shift_ref,
    cotangent_ref,
    output_ref,
    input_grad_ref,
    head_grad_ref,
    mixing_grad_ref,
    expand_grad_ref,
    shrink_grad_ref,
    sums_ref,
    sequence,
    queries,
    key_rows,
    values,
    mixed,
    log_totals,
    head_full,
    mixing_full,
    feed_full,
    offset_full,
    head_offset_ref,
    vectors_ref,
    key_columns,
    value_columns,
    mix_heads,
    attended_ref,
    normed,
    hidden,
    slope,
    summed_low,
    own_part,
    summed_grad,
    send_part,
    recv_part,
    feed_sum,
    feed_chip,
    feed_pair,
    early_core,
    mixing_sum,
    mixing_chip,
    mixing_rank,
    head_sum,
    head_chip,
    attended_low,
    mix_back_send,
    mix_back,
    query_low,
    key_low,
    value_low,
    line_part,
    vector_own,
    vector_core,
    vector_chip,
    vector_rank,
    row_send,
    row_recv,
    mix_send,
    mix_recv,
    weight_send,
    weight_recv,
    pair_send,
    pair_recv,
    chip_send,
    chip_recv,
    core_send,
    core_recv,
    swap_send,
    swap_recv,
    back_send,
    back_recv,
    line_send,
    line_recv,
    rank_send,
    rank_recv,
    free_sem,
):
    ranks = mixed.shape[0]
    rows, width = input_ref.shape
    shard = query_ref.shape[0]
    span = query_ref.shape[1]
    heads = span // HD
    units = expand_ref.shape[1]
    slices = 2
    step = rows // chunks
    length = ranks * rows
    here = Place(devices, ranks)
    d, t, chips = here.d, here.t, here.chips
    last = ranks - 1
    middle = jnp.logical_and(t > 0, t < last)
    partner = here.rank(t ^ 1)
    barrier = pltpu.get_barrier_semaphore()
    for k in range(1, ranks):
        pl.semaphore_signal(barrier, inc=1, device_id=here.rank(t ^ k), device_id_type=MESH)
    each(
        chips,
        1,
        lambda k: pl.semaphore_signal(
            barrier, inc=1, device_id=here.chip(k), device_id_type=MESH
        ),
    )
    pl.semaphore_signal(barrier, inc=1, device_id=here.core(), device_id_type=MESH)

    mine = pl.ds(pl.multiple_of(d * shard, shard), shard)
    sequence[pl.ds(pl.multiple_of(t * rows, rows), rows), :] = input_ref[...]
    head_full[0, mine, :] = query_ref[...]
    head_full[1, mine, :] = key_ref[...]
    head_full[2, mine, :] = value_ref[...]

    pl.semaphore_wait(barrier, ranks - 1 + chips - 1 + 1)

    def shard_rows(index):
        return pl.ds(pl.multiple_of(index * shard, shard), shard)

    def gather(number, view):
        return Gather(
            here,
            view,
            (chip_send.at[number], chip_recv.at[number]),
            (core_send.at[number], core_recv.at[number]),
        )

    heads_gather = gather(0, lambda i: head_full.at[:, shard_rows(i)])
    mixing_gather = gather(1, lambda i: mixing_full.at[:, shard_rows(i)])
    feed_gathers = [
        [
            TreeGather(
                here,
                lambda i, s=s, kind=kind: feed_full.at[s, kind, shard_rows(i)],
                (chip_send.at[2 + 2 * s + kind], chip_recv.at[2 + 2 * s + kind]),
                (core_send.at[2 + 2 * s + kind], core_recv.at[2 + 2 * s + kind]),
                kind == 0,
            )
            for kind in range(2)
        ]
        for s in range(slices)
    ]

    def own(chunk):
        return pl.ds(chunk * step, step)

    def row_copy(s, side, chunk):
        block = sequence.at[pl.ds(pl.multiple_of(s * rows + chunk * step, step), step)]
        return pltpu.make_async_remote_copy(
            src_ref=block,
            dst_ref=block,
            send_sem=row_send.at[side, s, chunk],
            recv_sem=row_recv.at[s, chunk],
            device_id=here.rank(jnp.clip(t + (1 if side else -1), 0, last)),
            device_id_type=MESH,
        )

    @pl.when(t < last)
    def _():
        for c in range(chunks):
            row_copy(t, 1, c).start()

    @pl.when(t > 0)
    def _():
        for c in range(chunks):
            row_copy(t, 0, c).start()

    heads_gather.start()
    feed_full[0, 0, mine, :] = expand_ref[...]
    feed_full[0, 1, mine, :] = shrink_ref[...].T
    mixing_full[t, mine, :] = mixing_ref[...].T

    def weight_copy(k):
        return remote(
            mixing_full.at[t, mine],
            mixing_full.at[t, mine],
            (weight_send, weight_recv),
            k,
            here.rank(t ^ k),
        )

    def weight_arrival(k):
        theirs = mixing_full.at[t ^ k, mine]
        return remote(theirs, theirs, (weight_send, weight_recv), k, here.rank(t ^ k))

    pair_copies = [
        remote(
            feed_full.at[0, :, mine],
            feed_full.at[1, :, mine],
            (pair_send, pair_recv),
            0,
            here.rank(t ^ 2),
        ),
        remote(
            offset_full.at[0], offset_full.at[1], (pair_send, pair_recv), 1, here.rank(t ^ 2)
        ),
    ]

    def start_weights():
        for k in range(1, ranks):
            weight_copy(k).start()

    def start_pairs():
        for copy in pair_copies:
            copy.start()

    start_weights()

    def as_row(ref):
        return ref[...].astype(F32).reshape(1, ref.shape[0])

    head_offset_ref[0:1, :] = as_row(query_offset_ref)
    head_offset_ref[1:2, :] = as_row(value_offset_ref)
    offset_full[0] = as_row(expand_offset_ref)
    for index, ref in enumerate(
        (
            first_gain_ref,
            first_shift_ref,
            second_gain_ref,
            second_shift_ref,
            shrink_offset_ref,
            mixing_offset_ref,
        )
    ):
        vectors_ref[index : index + 1, :] = as_row(ref)
    first_gain = vectors_ref[0:1, :]
    first_shift = vectors_ref[1:2, :]
    second_gain = vectors_ref[2:3, :]
    second_shift = vectors_ref[3:4, :]
    shrink_offset = vectors_ref[4:5, :]
    mixing_offset = vectors_ref[5:6, :]

    heads_gather.forward()
    for kind in feed_gathers[0]:
        kind.start()
    heads_gather.finish()

    def project(s):
        place = pl.ds(pl.multiple_of(s * rows, rows), rows)
        block = sequence[place, :]
        query = (mm(block, head_full[0], NN) + head_offset_ref[0:1, :]) * (HD**-0.5)
        queries[s] = query.astype(BF)
        key = mm(block, head_full[1], NN)
        key_rows[place, :] = key.astype(BF)
        value = mm(block, head_full[2], NN) + head_offset_ref[1:2, :]
        values[place, :] = value.astype(BF)
        value_columns[:, place] = value.T.astype(BF)
        key_columns[:, place] = key.T.astype(BF)

    project(t)

    def gather_mixing():
        for k in range(1, ranks):
            weight_arrival(k).wait_recv()
        mixing_gather.start()

    def second_slice():
        for copy in pair_copies:
            copy.wait_recv()
        for kind in feed_gathers[1]:
            kind.start()

    def second_step():
        for kind in feed_gathers[1]:
            kind.advance(0)

    near = [
        [s for _, s in sorted((abs(s - u), s) for s in range(ranks) if s != u)]
        for u in range(ranks)
    ]
    for j in range(ranks - 1):
        s = chosen([near[u][j] for u in range(ranks)], t)
        for c in range(chunks):
            row_copy(s, 0, c).wait_recv()

            @pl.when(jnp.logical_and(s < t, t < last))
            def _():
                row_copy(s, 1, c).start()

            @pl.when(jnp.logical_and(s > t, t > 0))
            def _():
                row_copy(s, 0, c).start()

        if j == 1:

            @pl.when(jnp.logical_not(middle))
            def _():
                start_pairs()

            project(arrived)
            project(s)
            for kind in feed_gathers[0]:
                kind.advance(0)

            @pl.when(jnp.logical_not(middle))
            def _():
                gather_mixing()

        if j == 2:
            project(s)

        arrived = s

    def mix_copy(s):
        return pltpu.make_async_remote_copy(
            src_ref=mix_heads.at[s],
            dst_ref=mixed.at[t],
            send_sem=mix_send.at[s],
            recv_sem=mix_recv.at[t],
            device_id=here.rank(s),
            device_id_type=MESH,
        )

    def mix_arrival(s):
        return pltpu.make_async_remote_copy(
            src_ref=mix_heads.at[s],
            dst_ref=mixed.at[s],
            send_sem=mix_send.at[s],
            recv_sem=mix_recv.at[s],
            device_id=here.rank(s),
            device_id_type=MESH,
        )

    lane = lax.broadcasted_iota(jnp.int32, (1, 128), 1)

    def attend(s):
        place = pl.ds(pl.multiple_of(s * rows, rows), rows)
        columns = []
        for h in range(heads):
            pair = slice(128 * (h // 2), 128 * (h // 2) + 128)
            side = (lane // HD) == (h % 2)
            query = jnp.where(side, queries[s, :, pair], jnp.zeros((), BF))
            scores = [
                mm(key_rows[k * rows : (k + 1) * rows, pair], query, NT) for k in range(ranks)
            ]
            largest = functools.reduce(
                jnp.maximum, [jnp.max(block, axis=0, keepdims=True) for block in scores]
            )
            total, column = 0.0, 0.0
            for k in range(ranks):
                weights = jnp.exp(scores[k] - largest)
                total = total + jnp.sum(weights, axis=0, keepdims=True)
                column = column + mm(
                    value_columns[h * HD : (h + 1) * HD, k * rows : (k + 1) * rows],
                    weights.astype(BF),
                    NN,
                )
            columns.append(column / total)
            log_totals[h : h + 1, place] = largest + jnp.log(total)
        mix_heads[s] = jnp.concatenate(columns, axis=0).T.astype(BF)

    far = [[s for s in reversed(near[u])] + [u] for u in range(ranks)]
    @pl.when(middle)
    def _():
        gather_mixing()

    @pl.when(middle)
    def _():
        start_pairs()

    for j in range(ranks):
        s = chosen([far[u][j] for u in range(ranks)], t)
        attend(s)
        if j < ranks - 1:
            mix_copy(s).start()
        if j == 0:
            for kind in feed_gathers[0]:
                kind.advance_rest()
        if j == 9:

            @pl.when(jnp.logical_not(middle))
            def _():
                gather_mixing()

        if j == 3:

            @pl.when(jnp.logical_not(middle))
            def _():
                second_slice()

        if j == 1:

            @pl.when(middle)
            def _():
                second_slice()

        if j == 3:
            mixing_gather.forward()

    mixed[t] = mix_heads[t]
    second_step()
    for k in range(1, ranks):
        mix_arrival(t ^ k).wait_recv()
    mixing_gather.finish()

    def mix_tile(tile):
        total = input_ref[:, tile].astype(F32) + vectors_ref[5:6, tile]
        for j in range(ranks):
            total = total + mm(mixed[j], mixing_full[j, tile, :], NT)
        attended_ref[:, tile] = total

    tiles(width, mix_tile)

    def other(chunk):
        return pl.ds(rows + chunk * step, step)

    def exchange(kind, chunk, source, target):
        return pltpu.make_async_remote_copy(
            src_ref=source,
            dst_ref=target,
            send_sem=swap_send.at[kind, chunk],
            recv_sem=swap_recv.at[kind, chunk],
            device_id=partner,
            device_id_type=MESH,
        )

    copies = [
        [exchange(0, c, normed.at[own(c)], normed.at[other(c)]) for c in range(chunks)],
        [exchange(1, c, send_part.at[0, own(c)], recv_part.at[0, own(c)]) for c in range(chunks)],
        [exchange(2, c, summed_low.at[own(c)], summed_low.at[other(c)]) for c in range(chunks)],
        [exchange(3, c, send_part.at[1, own(c)], recv_part.at[1, own(c)]) for c in range(chunks)],
    ]
    for c in range(chunks):
        normal, _ = norm_parts(attended_ref[own(c), :])
        normed[own(c), :] = (normal * first_gain + first_shift).astype(BF)
        copies[0][c].start()

    def forward(place, store, ready):
        for s in range(slices):
            ready(s)

            def grow(tile):
                value = mm(normed[place, :], feed_full[s, 0, :, tile], NN)
                value = value + offset_full[s, :, tile]
                share = 0.5 * (1.0 + lax.erf(value * 0.7071067811865476))
                density = jnp.exp(-0.5 * value * value) * 0.3989422804014327
                hidden[s, place, tile] = (value * share).astype(BF)
                slope[s, place, tile] = (share + value * density).astype(BF)

            tiles(units, grow)

        def shrink(tile):
            total = mm(hidden[0, place, :], feed_full[0, 1, tile, :], NT)
            for s in range(1, slices):
                total = total + mm(hidden[s, place, :], feed_full[s, 1, tile, :], NT)
            store(tile, total)

        tiles(width, shrink)

    def backward(place, store):
        for s in range(slices):

            def narrow(tile):
                value = mm(summed_low[place, :], feed_full[s, 1, :, tile], NN)
                value = value * slope[s, place, tile].astype(F32)
                slope[s, place, tile] = value.astype(BF)

            tiles(units, narrow)

        def widen(tile):
            total = mm(slope[0, place, :], feed_full[0, 0, tile, :], NT)
            for s in range(1, slices):
                total = total + mm(slope[s, place, :], feed_full[s, 0, tile, :], NT)
            store(tile, total)

        tiles(width, widen)

    def keep(tile, total):
        own_part[:, tile] = total

    def pass_on(which, chunk):
        def store(tile, total):
            send_part[which, own(chunk), tile] = total.astype(BF)

        return store

    def arrive(s):
        for kind in feed_gathers[s]:
            if s > 0:
                kind.advance_rest()
            kind.finish()

    forward(pl.ds(0, rows), keep, arrive)
    for c in range(chunks):
        copies[0][c].wait_recv()
        forward(other(c), pass_on(0, c), lambda s: None)
        copies[1][c].start()

    vector_own[...] = jnp.zeros_like(vector_own)
    for c in range(chunks):
        copies[1][c].wait_recv()
        normal, _ = norm_parts(attended_ref[own(c), :])
        first_norm = normal * first_gain + first_shift
        summed = (
            first_norm
            + (own_part[own(c), :] + recv_part[0, own(c), :].astype(F32))
            + shrink_offset
        )
        normal, rate = norm_parts(summed)
        output_ref[own(c), :] = (normal * second_gain + second_shift).astype(BF)
        upstream = cotangent_ref[own(c), :].astype(F32)
        grad = norm_back(upstream, second_gain, normal, rate)
        summed_grad[own(c), :] = grad
        summed_low[own(c), :] = grad.astype(BF)
        copies[2][c].start()
        vector_own[0:1, :] += column_sum(upstream * normal)
        vector_own[1:2, :] += column_sum(upstream)
        vector_own[2:3, :] += column_sum(grad)

    def spare_rows(k):
        return pl.ds(pl.multiple_of(width // 2 + k * shard, shard), shard)

    def reduce(number, source, core_slot, chip_slot):
        return Reduce(
            here,
            source,
            core_slot,
            chip_slot,
            (chip_send.at[number], chip_recv.at[number]),
            (core_send.at[number], core_recv.at[number]),
        )

    def core_slot(s, kind):
        if (s, kind) == (1, 1):
            return lambda k: early_core.at[shard_rows(k)]
        return lambda k: feed_full.at[s, kind, shard_rows(k)]

    feed_reduces = [
        [
            TreeReduce(
                here,
                lambda i, s=s, kind=kind: feed_sum.at[s, kind, shard_rows(i)],
                core_slot(s, kind),
                lambda k, s=s, kind=kind: feed_chip.at[s, k - 1, kind],
                (chip_send.at[6 + 2 * s + kind], chip_recv.at[6 + 2 * s + kind]),
                (core_send.at[6 + 2 * s + kind], core_recv.at[6 + 2 * s + kind]),
                kind == 0,
            )
            for kind in range(2)
        ]
        for s in range(slices)
    ]
    mixing_reduce = reduce(
        10,
        lambda i: mixing_sum.at[shard_rows(i)],
        lambda k: feed_full.at[0, 0, spare_rows(k)],
        lambda k: mixing_chip.at[k - 1],
    )
    head_reduce = reduce(
        11,
        lambda i: head_sum.at[shard_rows(i)],
        lambda k: feed_full.at[0, 1, spare_rows(k), 0 : 3 * span],
        lambda k: head_chip.at[k - 1],
    )

    def weigh(s, kind):
        left, right = ((normed, slope), (summed_low, hidden))[kind]

        def one(tile):
            size = min(TILE, width)
            for m in range(width // size):
                part = pl.ds(m * size, size)
                feed_sum[s, kind, part, tile] = mm(left[:, part], right[s, :, tile], TN).astype(BF)
            if kind == 0:
                vector_own[6 + s : 7 + s, tile] = column_sum(slope[s, :, tile].astype(F32))

        tiles(units, one)

    backward(pl.ds(0, rows), keep)
    for c in range(chunks):
        copies[2][c].wait_recv()
        if c == chunks - 1:
            weigh(1, 1)
            feed_reduces[1][1].start()
        backward(other(c), pass_on(1, c))
        copies[3][c].start()

    for kind in feed_gathers[0] + feed_gathers[1]:
        kind.drain()
    for copy in pair_copies:
        copy.wait_send()
    pl.semaphore_signal(free_sem, inc=1, device_id=here.core(), device_id_type=MESH)

    weigh(1, 0)
    pl.semaphore_wait(free_sem, 1)
    feed_reduces[1][0].start()
    feed_reduces[1][1].combine()
    for kind in (1, 0):
        weigh(0, kind)
        feed_reduces[0][kind].start()

    def back_copy(s, chunk):
        return pltpu.make_async_remote_copy(
            src_ref=mix_back_send.at[s, own(chunk)],
            dst_ref=mix_back.at[t, own(chunk)],
            send_sem=back_send.at[chunk, s],
            recv_sem=back_recv.at[chunk, t],
            device_id=here.rank(s),
            device_id_type=MESH,
        )

    def back_arrival(s, chunk):
        return pltpu.make_async_remote_copy(
            src_ref=mix_back_send.at[s, own(chunk)],
            dst_ref=mix_back.at[s, own(chunk)],
            send_sem=back_send.at[chunk, s],
            recv_sem=back_recv.at[chunk, s],
            device_id=here.rank(s),
            device_id_type=MESH,
        )

    for c in range(chunks):
        copies[3][c].wait_recv()
        normal, rate = norm_parts(attended_ref[own(c), :])
        upstream = summed_grad[own(c), :] + (
            own_part[own(c), :] + recv_part[1, own(c), :].astype(F32)
        )
        grad = norm_back(upstream, first_gain, normal, rate)
        input_grad_ref[own(c), :] = grad
        attended_low[own(c), :] = grad.astype(BF)
        for j in range(ranks):
            s = chosen([far[u][j] for u in range(ranks)], t)
            block = mm(attended_low[own(c), :], mixing_full[s], NN).astype(BF)
            if j < ranks - 1:
                mix_back_send[s, own(c), :] = block
                back_copy(s, c).start()
            else:
                mix_back[s, own(c), :] = block
        vector_own[3:4, :] += column_sum(upstream * normal)
        vector_own[4:5, :] += column_sum(upstream)
        vector_own[5:6, :] += column_sum(grad)

    for j in range(ranks):
        mixing_sum[:, j * span : (j + 1) * span] = mm(attended_low[...], mixed[j], TN).astype(BF)
    mixing_reduce.start()
    feed_reduces[1][0].combine()

    own_part[...] = jnp.zeros_like(own_part)
    summed_grad[...] = jnp.zeros_like(summed_grad)

    def pair_back(kind):
        return remote(
            feed_sum.at[1, kind, mine],
            feed_pair.at[kind],
            (pair_send, pair_recv),
            2 + kind,
            here.rank(t ^ 2),
        )

    def pair_start(kind):
        feed_sum[1, kind, mine, :] = feed_reduces[1][kind].total().astype(BF)
        pair_back(kind).start()

    def attend_back(s):
        place = pl.ds(pl.multiple_of(s * rows, rows), rows)
        inner = (mix_back[s].astype(F32) * mix_heads[s].astype(F32)).T
        columns = []
        for h in range(heads):
            pair = slice(128 * (h // 2), 128 * (h // 2) + 128)
            side = (lane // HD) == (h % 2)
            none = jnp.zeros((), BF)
            query = jnp.where(side, queries[s, :, pair], none)
            upstream = jnp.where(side, mix_back[s, :, pair], none)
            delta = jnp.sum(inner[h * HD : (h + 1) * HD, :], axis=0, keepdims=True)
            log_total = log_totals[h : h + 1, place]
            column = None
            for k in range(ranks):
                part = slice(k * rows, (k + 1) * rows)
                lanes = slice(k * span + pair.start, k * span + pair.stop)
                scores = mm(key_rows[part, pair], query, NT)
                probs = jnp.exp(scores - log_total)
                prob_grad = mm(values[part, pair], upstream, NT)
                score_low = (probs * (prob_grad - delta)).astype(BF)
                summed_grad[:, lanes] += mm(probs.astype(BF), upstream, NN)
                own_part[:, lanes] += mm(score_low, query, NN)
                term = mm(key_columns[h * HD : (h + 1) * HD, part], score_low, NN)
                column = term if column is None else column + term
            columns.append(column)
        low = jnp.concatenate(columns, axis=0).T.astype(BF)
        query_low[place, :] = (low.astype(F32) * HD**-0.5).astype(BF)

    for j in range(ranks):
        s = t if j == 0 else chosen([near[u][j - 1] for u in range(ranks)], t)
        if j > 0:
            for c in range(chunks):
                back_arrival(s, c).wait_recv()
        attend_back(s)
        if j == 1:
            feed_reduces[1][1].advance(0)
        if j == 2:
            feed_reduces[1][1].advance_rest()
            pair_start(1)
        if j == 2:
            feed_reduces[1][0].advance(0)
    for k in range(ranks):
        part = slice(k * rows, (k + 1) * rows)
        lanes = slice(k * span, (k + 1) * span)
        key_low[part, :] = own_part[:, lanes].astype(BF)
        value_low[part, :] = summed_grad[:, lanes].astype(BF)

    def input_part(s, tile):
        place = pl.ds(pl.multiple_of(s * rows, rows), rows)
        return (
            mm(query_low[place, :], head_full[0, tile, :], NT)
            + mm(key_low[place, :], head_full[1, tile, :], NT)
            + mm(value_low[place, :], head_full[2, tile, :], NT)
        )

    def arrival_time(u, s):
        if s > u:
            u, s = last - u, last - s
        return s if u == last else s + 1 + last - 1 - u

    line_order = [
        sorted([s for s in range(ranks) if s != u], key=lambda s, u=u: (arrival_time(u, s), s))
        for u in range(ranks)
    ]

    def line_rows(j):
        return pl.ds((j % 2) * rows, rows)

    def line_send_ref(j, chunk):
        return hidden.at[j // 2, pl.ds((j % 2) * rows + chunk * step, step)]

    def line_copy(j, s, chunk):
        slot = jnp.where(s == t + 1, ranks, s)
        return pltpu.make_async_remote_copy(
            src_ref=line_send_ref(j, chunk),
            dst_ref=line_part.at[slot, own(chunk)],
            send_sem=line_send.at[j, chunk],
            recv_sem=line_recv.at[slot, chunk],
            device_id=here.rank(jnp.clip(jnp.where(s < t, t - 1, t + 1), 0, last)),
            device_id_type=MESH,
        )

    def line_arrival(slot, chunk):
        return pltpu.make_async_remote_copy(
            src_ref=line_part.at[slot, own(chunk)],
            dst_ref=line_part.at[slot, own(chunk)],
            send_sem=line_send.at[0, chunk],
            recv_sem=line_recv.at[slot, chunk],
            device_id=partner,
            device_id_type=MESH,
        )

    targets = [chosen([line_order[u][j] for u in range(ranks)], t) for j in range(ranks - 1)]
    opens = [
        jnp.logical_or(jnp.logical_and(s < t, t == last), jnp.logical_and(s > t, t == 0))
        for s in targets
    ]
    for j, s in enumerate(targets):

        def store(tile):
            hidden[j // 2, line_rows(j), tile] = input_part(s, tile).astype(BF)

        tiles(width, store)

        @pl.when(opens[j])
        def _():
            for c in range(chunks):
                line_copy(j, s, c).start()

    def weigh_heads(tile):
        for i, low in enumerate((query_low, key_low, value_low)):
            head_sum[tile, i * span : (i + 1) * span] = mm(sequence[:, tile], low[...], TN).astype(BF)

    feed_reduces[1][0].advance_rest()
    pair_start(0)
    for kind in feed_reduces[0]:
        kind.combine()
    mixing_reduce.combine()
    tiles(width, weigh_heads)
    head_reduce.start()
    vector_own[8:9, 0:span] = column_sum(query_low[...].astype(F32))
    vector_own[8:9, span : 2 * span] = column_sum(value_low[...].astype(F32))

    def vector_core_copy():
        return remote(
            vector_own, vector_core, (core_send.at[12], core_recv.at[12]), 0, here.core()
        )

    vector_core_copy().start()

    def store_own(tile):
        input_grad_ref[:, tile] = input_grad_ref[:, tile] + input_part(t, tile)

    tiles(width, store_own)

    def pass_line(j, s):
        @pl.when(jnp.logical_not(opens[j]))
        def _():
            for c in range(chunks):
                line_arrival(s, c).wait_recv()
                block = line_send_ref(j, c)
                block[...] = (
                    block[...].astype(F32) + line_part[s, own(c), :].astype(F32)
                ).astype(BF)
                line_copy(j, s, c).start()

    vector_core_copy().wait()
    vector_own[...] = vector_own[...] + vector_core[...]

    def vector_chip_copy(k):
        return remote(
            vector_own,
            vector_chip.at[k - 1],
            (chip_send.at[12], chip_recv.at[12]),
            k,
            here.chip(k),
        )

    each(chips, 1, lambda k: vector_chip_copy(k).start())
    head_reduce.combine()

    def span_lanes(j):
        return pl.ds(pl.multiple_of(j * span, span), span)

    def mixing_rank_copy(k):
        return remote(
            mixing_sum.at[mine, span_lanes(t ^ k)],
            mixing_rank.at[k - 1],
            (rank_send.at[0], rank_recv.at[0]),
            k,
            here.rank(t ^ k),
        )

    pass_line(0, targets[0])
    pass_line(1, targets[1])
    for kind in feed_reduces[0]:
        kind.advance(0)
    pass_line(2, targets[2])
    mixing_sum[mine, :] = mixing_reduce.total().astype(BF)
    for k in range(1, ranks):
        mixing_rank_copy(k).start()

    each(chips, 1, lambda k: vector_chip_copy(k).wait())
    vector_sum = vector_own[...]
    for k in range(1, chips):
        vector_sum = vector_sum + vector_chip[k - 1]
    vector_core[...] = vector_sum

    def vector_rank_copy(k):
        return remote(
            vector_core,
            vector_rank.at[k - 1],
            (rank_send.at[1], rank_recv.at[1]),
            k,
            here.rank(t ^ k),
        )

    for k in range(1, ranks):
        vector_rank_copy(k).start()

    head_total = head_reduce.total()
    for i in range(3):
        head_grad_ref[i] = head_total[:, i * span : (i + 1) * span]
    feed_own = []
    for kind in feed_reduces[0]:
        kind.advance_rest()
        feed_own.append(kind.total())
    for k in range(1, ranks):
        mixing_rank_copy(k).wait()
    mixing_grad = mixing_sum[mine, span_lanes(t)].astype(F32)
    for k in range(1, ranks):
        mixing_grad = mixing_grad + mixing_rank[k - 1].astype(F32)
    mixing_grad_ref[...] = mixing_grad
    pair_back(0).wait()
    pair_back(1).wait()
    expand_grad_ref[...] = feed_own[0] + feed_pair[0].astype(F32)
    shrink_grad_ref[...] = feed_own[1] + feed_pair[1].astype(F32)
    for k in range(1, ranks):
        vector_rank_copy(k).wait()
    vector_sum = vector_core[...]
    sums_ref[...] = vector_sum
    everywhere = vector_sum[0:6, :]
    for k in range(1, ranks):
        everywhere = everywhere + vector_rank[k - 1, 0:6, :]
    sums_ref[0:6, :] = everywhere
    sums_ref[6:7, :] = vector_sum[6:7, :] + vector_rank[1, 7:8, :]

    @pl.when(t < last)
    def _():
        for c in range(chunks):
            line_arrival(t, c).wait_recv()
            input_grad_ref[own(c), :] += line_part[t, own(c), :].astype(F32)

    @pl.when(t > 0)
    def _():
        for c in range(chunks):
            line_arrival(ranks, c).wait_recv()
            input_grad_ref[own(c), :] += line_part[ranks, own(c), :].astype(F32)

    for j in range(ranks - 1):
        for c in range(chunks):
            line_copy(j, targets[j], c).wait_send()
            back_copy(t ^ (j + 1), c).wait_send()
    for each_reduce in feed_reduces[0] + feed_reduces[1] + [mixing_reduce, head_reduce]:
        each_reduce.drain()
    for kind in range(4):
        for c in range(chunks):
            copies[kind][c].wait_send()
    for each_gather in (heads_gather, mixing_gather):
        each_gather.drain()
    for k in range(1, ranks):
        mix_copy(t ^ k).wait_send()
        weight_copy(k).wait_send()
    for s in range(ranks):

        @pl.when(jnp.logical_and(s <= t, t < last))
        def _():
            for c in range(chunks):
                row_copy(s, 1, c).wait_send()

        @pl.when(jnp.logical_and(s >= t, t > 0))
        def _():
            for c in range(chunks):
                row_copy(s, 0, c).wait_send()


def layer(devices, ranks, inputs):
    layer_input = inputs[0]
    rows, width = layer_input.shape
    span = inputs[1].shape[1]
    units = inputs[5].shape[1]
    slices = 2
    chunks = 2
    chips = devices // 2
    length = ranks * rows
    both = 2 * rows
    vmem = pl.BlockSpec(memory_space=pltpu.VMEM)
    dma = pltpu.SemaphoreType.DMA
    shard = width // devices
    outs = (
        jax.ShapeDtypeStruct((rows, width), BF),
        jax.ShapeDtypeStruct((rows, width), F32),
        jax.ShapeDtypeStruct((3, shard, span), F32),
        jax.ShapeDtypeStruct((shard, span), F32),
        jax.ShapeDtypeStruct((shard, units), F32),
        jax.ShapeDtypeStruct((shard, units), F32),
        jax.ShapeDtypeStruct((16, width), F32),
    )
    return pl.pallas_call(
        functools.partial(layer_kernel, devices, chunks),
        out_shape=outs,
        in_specs=[vmem] * len(inputs),
        out_specs=[vmem] * len(outs),
        scratch_shapes=[
            pltpu.VMEM((length, width), BF),
            pltpu.VMEM((ranks, rows, span), BF),
            pltpu.VMEM((length, span), BF),
            pltpu.VMEM((length, span), BF),
            pltpu.VMEM((ranks, rows, span), BF),
            pltpu.VMEM((8, length), F32),
            pltpu.VMEM((3, width, span), BF),
            pltpu.VMEM((ranks, width, span), BF),
            pltpu.VMEM((slices, 2, width, units), BF),
            pltpu.VMEM((slices, 1, units), F32),
            pltpu.VMEM((8, span), F32),
            pltpu.VMEM((8, width), F32),
            pltpu.VMEM((span, length), BF),
            pltpu.VMEM((span, length), BF),
            pltpu.VMEM((ranks, rows, span), BF),
            pltpu.VMEM((rows, width), F32),
            pltpu.VMEM((both, width), BF),
            pltpu.VMEM((slices, both, units), BF),
            pltpu.VMEM((slices, both, units), BF),
            pltpu.VMEM((both, width), BF),
            pltpu.VMEM((rows, width), F32),
            pltpu.VMEM((rows, width), F32),
            pltpu.VMEM((2, rows, width), BF),
            pltpu.VMEM((2, rows, width), BF),
            pltpu.VMEM((slices, 2, width, units), BF),
            pltpu.VMEM((slices, chips - 1, 2, shard, units), BF),
            pltpu.VMEM((2, shard, units), BF),
            pltpu.VMEM((width // 2, units), BF),
            pltpu.VMEM((width, ranks * span), BF),
            pltpu.VMEM((chips - 1, shard, ranks * span), BF),
            pltpu.VMEM((ranks - 1, shard, span), BF),
            pltpu.VMEM((width, 3 * span), BF),
            pltpu.VMEM((chips - 1, shard, 3 * span), BF),
            pltpu.VMEM((rows, width), BF),
            pltpu.VMEM((ranks, rows, span), BF),
            pltpu.VMEM((ranks, rows, span), BF),
            pltpu.VMEM((length, span), BF),
            pltpu.VMEM((length, span), BF),
            pltpu.VMEM((length, span), BF),
            pltpu.VMEM((ranks + 1, rows, width), BF),
            pltpu.VMEM((16, width), F32),
            pltpu.VMEM((16, width), F32),
            pltpu.VMEM((chips - 1, 16, width), F32),
            pltpu.VMEM((ranks - 1, 16, width), F32),
            dma((2, ranks, chunks)),
            dma((ranks, chunks)),
            dma((ranks,)),
            dma((ranks,)),
            dma((ranks,)),
            dma((ranks,)),
            dma((4,)),
            dma((4,)),
            dma((13, chips)),
            dma((13, chips)),
            dma((13, chips)),
            dma((13, chips)),
            dma((4, chunks)),
            dma((4, chunks)),
            dma((chunks, ranks)),
            dma((chunks, ranks)),
            dma((ranks - 1, chunks)),
            dma((ranks + 1, chunks)),
            dma((2, ranks)),
            dma((2, ranks)),
            pltpu.SemaphoreType.REGULAR,
        ],
        compiler_params=pltpu.CompilerParams(
            collective_id=1, has_side_effects=True, vmem_limit_bytes=VMEM_LIMIT
        ),
    )(*inputs)


def body(
    layer_input,
    query_weight,
    key_weight,
    value_weight,
    mixing_weight,
    expand_weight,
    shrink_weight,
    query_offset,
    value_offset,
    mixing_offset,
    expand_offset,
    shrink_offset,
    first_gain,
    first_shift,
    second_gain,
    second_shift,
    cotangent,
):
    results = layer(
        lax.axis_size("dp"),
        lax.axis_size("tensor"),
        (
            layer_input,
            query_weight,
            key_weight,
            value_weight,
            mixing_weight,
            expand_weight,
            shrink_weight,
            query_offset,
            value_offset,
            mixing_offset,
            expand_offset,
            shrink_offset,
            first_gain,
            first_shift,
            second_gain,
            second_shift,
            cotangent,
        ),
    )
    return place_outputs(results, expand_weight.shape[1], query_weight.shape[1])


def solution(mesh):
    rows = P(("dp", "tensor"), None)
    tall = P("dp", "tensor")
    wide = P("tensor", "dp")
    split = P("tensor")
    whole = P()
    return jax.shard_map(
        body,
        mesh=mesh,
        in_specs=(rows, tall, tall, tall, wide, tall, wide, split, split)
        + (whole, split, whole, whole, whole, whole, whole, rows),
        out_specs=(rows, rows, tall, tall, tall, wide, tall, wide, split, split)
        + (whole, split, whole, whole, whole, whole, whole),
        check_vma=False,
    )
```

```python
import functools

import jax
import jax.numpy as jnp
from jax import lax
from jax.experimental import pallas as pl
from jax.experimental.pallas import tpu as pltpu
from jax.sharding import PartitionSpec as P

HD = 64
EPSILON = 1e-05
MESH = pl.DeviceIdType.MESH
BF = jnp.bfloat16
F32 = jnp.float32
NN = (((1,), (0,)), ((), ()))
NT = (((1,), (1,)), ((), ()))
TN = (((0,), (0,)), ((), ()))
VMEM_LIMIT = 60 * 1024 * 1024
TILE = 512


def mm(left, right, dims):
    return lax.dot_general(left, right, dims, preferred_element_type=F32)


def norm_parts(inputs):
    centered = inputs - jnp.mean(inputs, axis=-1, keepdims=True)
    variance = jnp.mean(centered * centered, axis=-1, keepdims=True)
    rate = lax.rsqrt(variance + EPSILON)
    return centered * rate, rate


def norm_back(upstream, gain, normal, rate):
    scaled = upstream * gain
    mean_scaled = jnp.mean(scaled, axis=-1, keepdims=True)
    mean_normal = jnp.mean(scaled * normal, axis=-1, keepdims=True)
    return rate * (scaled - mean_scaled - normal * mean_normal)


def column_sum(block):
    return jnp.sum(block, axis=0, keepdims=True)


def tiles(width, body):
    step = min(TILE, width)

    def one(index, carry):
        body(pl.ds(pl.multiple_of(index * step, step), step))
        return carry

    lax.fori_loop(0, width // step, one, 0)


def chosen(table, index):
    value = jnp.int32(table[0])
    for place in range(1, len(table)):
        value = jnp.where(index == place, jnp.int32(table[place]), value)
    return value


def each(count, start, body):
    if count - start <= 8:
        for index in range(start, count):
            body(index)
        return

    def one(index, carry):
        body(index)
        return carry

    lax.fori_loop(start, count, one, 0)


class Place:
    def __init__(self, devices, ranks):
        self.d = lax.axis_index("dp")
        self.t = lax.axis_index("tensor")
        self.chips = devices // 2
        self.ranks = ranks
        self.c = self.d % 2
        self.p = self.d // 2

    def chip(self, k):
        return {"dp": 2 * (self.p ^ k) + self.c}

    def core(self):
        return {"dp": self.d ^ 1}

    def rank(self, t):
        return {"tensor": t}


def remote(source, target, sems, index, device):
    send, recv = sems
    return pltpu.make_async_remote_copy(
        src_ref=source,
        dst_ref=target,
        send_sem=send.at[index],
        recv_sem=recv.at[index],
        device_id=device,
        device_id_type=MESH,
    )


class Gather:
    def __init__(self, here, view, chip_sems, core_sems):
        self.here, self.view = here, view
        self.chip_sems, self.core_sems = chip_sems, core_sems

    def chip_copy(self, k):
        here = self.here
        mine = self.view(2 * here.p + here.c)
        return remote(mine, mine, self.chip_sems, k, here.chip(k))

    def chip_arrival(self, k):
        here = self.here
        theirs = self.view(2 * (here.p ^ k) + here.c)
        return remote(theirs, theirs, self.chip_sems, k, here.chip(k))

    def core_copy(self, k):
        here = self.here
        shard = self.view(2 * (here.p ^ k) + here.c)
        return remote(shard, shard, self.core_sems, k, here.core())

    def core_arrival(self, k):
        here = self.here
        shard = self.view(2 * (here.p ^ k) + 1 - here.c)
        return remote(shard, shard, self.core_sems, k, here.core())

    def start(self):
        each(self.here.chips, 1, lambda k: self.chip_copy(k).start())
        self.core_copy(0).start()

    def forward(self):
        def one(k):
            self.chip_arrival(k).wait_recv()
            self.core_copy(k).start()

        each(self.here.chips, 1, one)

    def finish(self):
        each(self.here.chips, 0, lambda k: self.core_arrival(k).wait_recv())

    def drain(self):
        each(self.here.chips, 1, lambda k: self.chip_copy(k).wait_send())
        each(self.here.chips, 0, lambda k: self.core_copy(k).wait_send())


class Reduce:
    def __init__(self, here, source, core_slot, chip_slot, chip_sems, core_sems):
        self.here, self.source = here, source
        self.core_slot, self.chip_slot = core_slot, chip_slot
        self.chip_sems, self.core_sems = chip_sems, core_sems

    def core_copy(self, k):
        here = self.here
        shard = self.source(2 * (here.p ^ k) + 1 - here.c)
        return remote(shard, self.core_slot(k), self.core_sems, k, here.core())

    def chip_copy(self, k):
        here = self.here
        shard = self.source(2 * (here.p ^ k) + here.c)
        return remote(shard, self.chip_slot(k), self.chip_sems, k, here.chip(k))

    def start(self):
        each(self.here.chips, 1, lambda k: self.core_copy(k).start())
        self.core_copy(0).start()

    def combine(self):
        here = self.here

        def one(k):
            self.core_copy(k).wait_recv()
            shard = self.source(2 * (here.p ^ k) + here.c)
            shard[...] = shard[...] + self.core_slot(k)[...]

        def send(k):
            one(k)
            self.chip_copy(k).start()

        each(here.chips, 1, send)
        one(0)

    def total(self):
        here = self.here
        each(here.chips, 1, lambda k: self.chip_copy(k).wait_recv())
        value = self.source(here.d)[...].astype(F32)
        for k in range(1, here.chips):
            value = value + self.chip_slot(k)[...].astype(F32)
        return value

    def drain(self):
        each(self.here.chips, 1, lambda k: self.chip_copy(k).wait_send())
        each(self.here.chips, 0, lambda k: self.core_copy(k).wait_send())


class TreeGather(Gather):
    def __init__(self, here, view, chip_sems, core_sems, rising):
        super().__init__(here, view, chip_sems, core_sems)
        self.rising = rising
        self.steps = here.chips.bit_length() - 1

    def bit(self, i):
        return 1 << i if self.rising else self.here.chips >> (i + 1)

    def held(self, i, j):
        return j if self.rising else j << (self.steps - i)

    def step_copy(self, i, j):
        here = self.here
        mask = self.held(i, j)
        shard = self.view(2 * (here.p ^ mask) + here.c)
        bit = self.bit(i)
        return remote(shard, shard, self.chip_sems, mask ^ bit, here.chip(bit))

    def step_arrival(self, i, j):
        here = self.here
        bit = self.bit(i)
        key = self.held(i, j) ^ bit
        shard = self.view(2 * (here.p ^ key) + here.c)
        return remote(shard, shard, self.chip_sems, key, here.chip(bit))

    def start(self):
        each(1, 0, lambda j: self.step_copy(0, j).start())
        self.core_copy(0).start()

    def advance(self, i):
        count = 1 << i
        each(count, 0, lambda j: self.step_arrival(i, j).wait_recv())
        if i + 1 < self.steps:
            each(2 * count, 0, lambda j: self.step_copy(i + 1, j).start())
        each(count, 0, lambda j: self.core_copy(self.held(i, j) ^ self.bit(i)).start())

    def advance_rest(self):
        for i in range(1, self.steps):
            self.advance(i)

    def drain(self):
        for i in range(self.steps):
            each(1 << i, 0, lambda j: self.step_copy(i, j).wait_send())
        each(self.here.chips, 0, lambda k: self.core_copy(k).wait_send())


class TreeReduce(Reduce):
    def __init__(self, here, source, core_slot, chip_slot, chip_sems, core_sems, rising):
        super().__init__(here, source, core_slot, chip_slot, chip_sems, core_sems)
        self.rising = rising
        self.steps = here.chips.bit_length() - 1

    def bit(self, i):
        return 1 << i if self.rising else self.here.chips >> (i + 1)

    def rest(self, i, j):
        return j << (i + 1) if self.rising else j

    def count(self, i):
        return 1 << (self.steps - 1 - i)

    def step_copy(self, i, j):
        here = self.here
        bit = self.bit(i)
        key = self.rest(i, j) ^ bit
        shard = self.source(2 * (here.p ^ key) + here.c)
        return remote(shard, self.chip_slot(key), self.chip_sems, key, here.chip(bit))

    def combine(self):
        here = self.here

        def one(k):
            self.core_copy(k).wait_recv()
            shard = self.source(2 * (here.p ^ k) + here.c)
            shard[...] = shard[...] + self.core_slot(k)[...]

        each(here.chips, 1, one)
        one(0)
        each(self.count(0), 0, lambda j: self.step_copy(0, j).start())

    def advance(self, i):
        here = self.here

        def one(j):
            mask = self.rest(i, j)
            self.step_copy(i, j).wait_recv()
            shard = self.source(2 * (here.p ^ mask) + here.c)
            shard[...] = shard[...] + self.chip_slot(mask ^ self.bit(i))[...]

        each(self.count(i), 0, one)
        each(self.count(i + 1), 0, lambda j: self.step_copy(i + 1, j).start())

    def advance_rest(self):
        for i in range(1, self.steps - 1):
            self.advance(i)

    def total(self):
        final = self.steps - 1
        self.step_copy(final, 0).wait_recv()
        value = self.source(self.here.d)[...].astype(F32)
        return value + self.chip_slot(self.bit(final))[...].astype(F32)

    def drain(self):
        for i in range(self.steps):
            each(self.count(i), 0, lambda j: self.step_copy(i, j).wait_send())
        each(self.here.chips, 0, lambda k: self.core_copy(k).wait_send())


def place_kernel(
    layer_output_ref,
    input_sum_ref,
    head_sum_ref,
    mixing_sum_ref,
    expand_sum_ref,
    shrink_sum_ref,
    sums_ref,
    output_ref,
    input_ref,
    query_ref,
    key_ref,
    value_ref,
    mixing_ref,
    expand_ref,
    shrink_ref,
    query_offset_ref,
    value_offset_ref,
    mixing_offset_ref,
    expand_offset_ref,
    shrink_offset_ref,
    first_gain_ref,
    first_shift_ref,
    second_gain_ref,
    second_shift_ref,
):
    output_ref[...] = layer_output_ref[...]
    input_ref[...] = input_sum_ref[...]
    query_ref[...] = head_sum_ref[0]
    key_ref[...] = head_sum_ref[1]
    value_ref[...] = head_sum_ref[2]
    mixing_ref[...] = mixing_sum_ref[...].T
    expand_ref[...] = expand_sum_ref[...]
    shrink_ref[...] = shrink_sum_ref[...].T

    def row(ref, index, start=0):
        size = ref.shape[0]
        ref[...] = sums_ref[index : index + 1, start : start + size].reshape(size)

    row(query_offset_ref, 8)
    row(value_offset_ref, 8, query_offset_ref.shape[0])
    row(mixing_offset_ref, 5)
    row(expand_offset_ref, 6)
    row(shrink_offset_ref, 2)
    row(first_gain_ref, 3)
    row(first_shift_ref, 4)
    row(second_gain_ref, 0)
    row(second_shift_ref, 1)


def place_outputs(results, units, span):
    rows, width = results[1].shape
    shard = results[2].shape[1]
    shapes = [
        ((rows, width), BF),
        ((rows, width), F32),
        ((shard, span), F32),
        ((shard, span), F32),
        ((shard, span), F32),
        ((span, shard), F32),
        ((shard, units), F32),
        ((units, shard), F32),
        ((span,), F32),
        ((span,), F32),
        ((width,), F32),
        ((units,), F32),
    ] + [((width,), F32)] * 5
    vmem = pl.BlockSpec(memory_space=pltpu.VMEM)
    return pl.pallas_call(
        place_kernel,
        out_shape=tuple(jax.ShapeDtypeStruct(shape, kind) for shape, kind in shapes),
        in_specs=[vmem] * len(results),
        out_specs=[vmem] * len(shapes),
    )(*results)


def layer_kernel(
    devices,
    chunks,
    input_ref,
    query_ref,
    key_ref,
    value_ref,
    mixing_ref,
    expand_ref,
    shrink_ref,
    query_offset_ref,
    value_offset_ref,
    mixing_offset_ref,
    expand_offset_ref,
    shrink_offset_ref,
    first_gain_ref,
    first_shift_ref,
    second_gain_ref,
    second_shift_ref,
    cotangent_ref,
    output_ref,
    input_grad_ref,
    head_grad_ref,
    mixing_grad_ref,
    expand_grad_ref,
    shrink_grad_ref,
    sums_ref,
    sequence,
    queries,
    key_rows,
    values,
    mixed,
    log_totals,
    head_full,
    mixing_full,
    feed_full,
    offset_full,
    head_offset_ref,
    vectors_ref,
    key_columns,
    value_columns,
    mix_heads,
    attended_ref,
    normed,
    hidden,
    slope,
    summed_low,
    own_part,
    summed_grad,
    send_part,
    recv_part,
    feed_sum,
    feed_chip,
    feed_pair,
    early_core,
    mixing_sum,
    mixing_chip,
    mixing_rank,
    head_sum,
    head_chip,
    attended_low,
    mix_back_send,
    mix_back,
    query_low,
    key_low,
    value_low,
    line_part,
    vector_own,
    vector_core,
    vector_chip,
    vector_rank,
    row_send,
    row_recv,
    mix_send,
    mix_recv,
    weight_send,
    weight_recv,
    pair_send,
    pair_recv,
    chip_send,
    chip_recv,
    core_send,
    core_recv,
    swap_send,
    swap_recv,
    back_send,
    back_recv,
    line_send,
    line_recv,
    rank_send,
    rank_recv,
    free_sem,
):
    ranks = mixed.shape[0]
    rows, width = input_ref.shape
    shard = query_ref.shape[0]
    span = query_ref.shape[1]
    heads = span // HD
    units = expand_ref.shape[1]
    slices = 2
    step = rows // chunks
    length = ranks * rows
    here = Place(devices, ranks)
    d, t, chips = here.d, here.t, here.chips
    last = ranks - 1
    middle = jnp.logical_and(t > 0, t < last)
    partner = here.rank(t ^ 1)
    barrier = pltpu.get_barrier_semaphore()
    for k in range(1, ranks):
        pl.semaphore_signal(barrier, inc=1, device_id=here.rank(t ^ k), device_id_type=MESH)
    each(
        chips,
        1,
        lambda k: pl.semaphore_signal(
            barrier, inc=1, device_id=here.chip(k), device_id_type=MESH
        ),
    )
    pl.semaphore_signal(barrier, inc=1, device_id=here.core(), device_id_type=MESH)

    mine = pl.ds(pl.multiple_of(d * shard, shard), shard)
    sequence[pl.ds(pl.multiple_of(t * rows, rows), rows), :] = input_ref[...]
    head_full[0, mine, :] = query_ref[...]
    head_full[1, mine, :] = key_ref[...]
    head_full[2, mine, :] = value_ref[...]

    pl.semaphore_wait(barrier, ranks - 1 + chips - 1 + 1)

    def shard_rows(index):
        return pl.ds(pl.multiple_of(index * shard, shard), shard)

    def gather(number, view):
        return Gather(
            here,
            view,
            (chip_send.at[number], chip_recv.at[number]),
            (core_send.at[number], core_recv.at[number]),
        )

    heads_gather = gather(0, lambda i: head_full.at[:, shard_rows(i)])
    mixing_gather = gather(1, lambda i: mixing_full.at[:, shard_rows(i)])
    feed_gathers = [
        [
            TreeGather(
                here,
                lambda i, s=s, kind=kind: feed_full.at[s, kind, shard_rows(i)],
                (chip_send.at[2 + 2 * s + kind], chip_recv.at[2 + 2 * s + kind]),
                (core_send.at[2 + 2 * s + kind], core_recv.at[2 + 2 * s + kind]),
                kind == 0,
            )
            for kind in range(2)
        ]
        for s in range(slices)
    ]

    def own(chunk):
        return pl.ds(chunk * step, step)

    def row_copy(s, side, chunk):
        block = sequence.at[pl.ds(pl.multiple_of(s * rows + chunk * step, step), step)]
        return pltpu.make_async_remote_copy(
            src_ref=block,
            dst_ref=block,
            send_sem=row_send.at[side, s, chunk],
            recv_sem=row_recv.at[s, chunk],
            device_id=here.rank(jnp.clip(t + (1 if side else -1), 0, last)),
            device_id_type=MESH,
        )

    @pl.when(t < last)
    def _():
        for c in range(chunks):
            row_copy(t, 1, c).start()

    @pl.when(t > 0)
    def _():
        for c in range(chunks):
            row_copy(t, 0, c).start()

    heads_gather.start()
    feed_full[0, 0, mine, :] = expand_ref[...]
    feed_full[0, 1, mine, :] = shrink_ref[...].T
    mixing_full[t, mine, :] = mixing_ref[...].T

    def weight_copy(k):
        return remote(
            mixing_full.at[t, mine],
            mixing_full.at[t, mine],
            (weight_send, weight_recv),
            k,
            here.rank(t ^ k),
        )

    def weight_arrival(k):
        theirs = mixing_full.at[t ^ k, mine]
        return remote(theirs, theirs, (weight_send, weight_recv), k, here.rank(t ^ k))

    pair_copies = [
        remote(
            feed_full.at[0, :, mine],
            feed_full.at[1, :, mine],
            (pair_send, pair_recv),
            0,
            here.rank(t ^ 2),
        ),
        remote(
            offset_full.at[0], offset_full.at[1], (pair_send, pair_recv), 1, here.rank(t ^ 2)
        ),
    ]

    def start_weights():
        for k in range(1, ranks):
            weight_copy(k).start()

    def start_pairs():
        for copy in pair_copies:
            copy.start()

    start_weights()

    def as_row(ref):
        return ref[...].astype(F32).reshape(1, ref.shape[0])

    head_offset_ref[0:1, :] = as_row(query_offset_ref)
    head_offset_ref[1:2, :] = as_row(value_offset_ref)
    offset_full[0] = as_row(expand_offset_ref)
    for index, ref in enumerate(
        (
            first_gain_ref,
            first_shift_ref,
            second_gain_ref,
            second_shift_ref,
            shrink_offset_ref,
            mixing_offset_ref,
        )
    ):
        vectors_ref[index : index + 1, :] = as_row(ref)
    first_gain = vectors_ref[0:1, :]
    first_shift = vectors_ref[1:2, :]
    second_gain = vectors_ref[2:3, :]
    second_shift = vectors_ref[3:4, :]
    shrink_offset = vectors_ref[4:5, :]
    mixing_offset = vectors_ref[5:6, :]

    heads_gather.forward()
    for kind in feed_gathers[0]:
        kind.start()
    heads_gather.finish()

    def project(s):
        place = pl.ds(pl.multiple_of(s * rows, rows), rows)
        block = sequence[place, :]
        query = (mm(block, head_full[0], NN) + head_offset_ref[0:1, :]) * (HD**-0.5)
        queries[s] = query.astype(BF)
        key = mm(block, head_full[1], NN)
        key_rows[place, :] = key.astype(BF)
        value = mm(block, head_full[2], NN) + head_offset_ref[1:2, :]
        values[place, :] = value.astype(BF)
        value_columns[:, place] = value.T.astype(BF)
        key_columns[:, place] = key.T.astype(BF)

    project(t)

    def gather_mixing():
        for k in range(1, ranks):
            weight_arrival(k).wait_recv()
        mixing_gather.start()

    def second_slice():
        for copy in pair_copies:
            copy.wait_recv()
        for kind in feed_gathers[1]:
            kind.start()

    def second_step():
        for kind in feed_gathers[1]:
            kind.advance(0)

    near = [
        [s for _, s in sorted((abs(s - u), s) for s in range(ranks) if s != u)]
        for u in range(ranks)
    ]
    for j in range(ranks - 1):
        s = chosen([near[u][j] for u in range(ranks)], t)
        for c in range(chunks):
            row_copy(s, 0, c).wait_recv()

            @pl.when(jnp.logical_and(s < t, t < last))
            def _():
                row_copy(s, 1, c).start()

            @pl.when(jnp.logical_and(s > t, t > 0))
            def _():
                row_copy(s, 0, c).start()

        if j == 1:

            @pl.when(jnp.logical_not(middle))
            def _():
                start_pairs()

            project(arrived)
            project(s)
            for kind in feed_gathers[0]:
                kind.advance(0)

            @pl.when(jnp.logical_not(middle))
            def _():
                gather_mixing()

        if j == 2:
            project(s)

        arrived = s

    def mix_copy(s):
        return pltpu.make_async_remote_copy(
            src_ref=mix_heads.at[s],
            dst_ref=mixed.at[t],
            send_sem=mix_send.at[s],
            recv_sem=mix_recv.at[t],
            device_id=here.rank(s),
            device_id_type=MESH,
        )

    def mix_arrival(s):
        return pltpu.make_async_remote_copy(
            src_ref=mix_heads.at[s],
            dst_ref=mixed.at[s],
            send_sem=mix_send.at[s],
            recv_sem=mix_recv.at[s],
            device_id=here.rank(s),
            device_id_type=MESH,
        )

    lane = lax.broadcasted_iota(jnp.int32, (1, 128), 1)

    def attend(s):
        place = pl.ds(pl.multiple_of(s * rows, rows), rows)
        columns = []
        for h in range(heads):
            pair = slice(128 * (h // 2), 128 * (h // 2) + 128)
            side = (lane // HD) == (h % 2)
            query = jnp.where(side, queries[s, :, pair], jnp.zeros((), BF))
            scores = [
                mm(key_rows[k * rows : (k + 1) * rows, pair], query, NT) for k in range(ranks)
            ]
            largest = functools.reduce(
                jnp.maximum, [jnp.max(block, axis=0, keepdims=True) for block in scores]
            )
            total, column = 0.0, 0.0
            for k in range(ranks):
                weights = jnp.exp(scores[k] - largest)
                total = total + jnp.sum(weights, axis=0, keepdims=True)
                column = column + mm(
                    value_columns[h * HD : (h + 1) * HD, k * rows : (k + 1) * rows],
                    weights.astype(BF),
                    NN,
                )
            columns.append(column / total)
            log_totals[h : h + 1, place] = largest + jnp.log(total)
        mix_heads[s] = jnp.concatenate(columns, axis=0).T.astype(BF)

    far = [[s for s in reversed(near[u])] + [u] for u in range(ranks)]
    @pl.when(middle)
    def _():
        gather_mixing()

    @pl.when(middle)
    def _():
        start_pairs()

    for j in range(ranks):
        s = chosen([far[u][j] for u in range(ranks)], t)
        attend(s)
        if j < ranks - 1:
            mix_copy(s).start()
        if j == 0:
            for kind in feed_gathers[0]:
                kind.advance_rest()
        if j == 9:

            @pl.when(jnp.logical_not(middle))
            def _():
                gather_mixing()

        if j == 3:

            @pl.when(jnp.logical_not(middle))
            def _():
                second_slice()

        if j == 1:

            @pl.when(middle)
            def _():
                second_slice()

        if j == 3:
            mixing_gather.forward()

    mixed[t] = mix_heads[t]
    second_step()
    for k in range(1, ranks):
        mix_arrival(t ^ k).wait_recv()
    mixing_gather.finish()

    def mix_tile(tile):
        total = input_ref[:, tile].astype(F32) + vectors_ref[5:6, tile]
        for j in range(ranks):
            total = total + mm(mixed[j], mixing_full[j, tile, :], NT)
        attended_ref[:, tile] = total

    tiles(width, mix_tile)

    def other(chunk):
        return pl.ds(rows + chunk * step, step)

    def exchange(kind, chunk, source, target):
        return pltpu.make_async_remote_copy(
            src_ref=source,
            dst_ref=target,
            send_sem=swap_send.at[kind, chunk],
            recv_sem=swap_recv.at[kind, chunk],
            device_id=partner,
            device_id_type=MESH,
        )

    copies = [
        [exchange(0, c, normed.at[own(c)], normed.at[other(c)]) for c in range(chunks)],
        [exchange(1, c, send_part.at[0, own(c)], recv_part.at[0, own(c)]) for c in range(chunks)],
        [exchange(2, c, summed_low.at[own(c)], summed_low.at[other(c)]) for c in range(chunks)],
        [exchange(3, c, send_part.at[1, own(c)], recv_part.at[1, own(c)]) for c in range(chunks)],
    ]
    for c in range(chunks):
        normal, _ = norm_parts(attended_ref[own(c), :])
        normed[own(c), :] = (normal * first_gain + first_shift).astype(BF)
        copies[0][c].start()

    def forward(place, store, ready):
        for s in range(slices):
            ready(s)

            def grow(tile):
                value = mm(normed[place, :], feed_full[s, 0, :, tile], NN)
                value = value + offset_full[s, :, tile]
                share = 0.5 * (1.0 + lax.erf(value * 0.7071067811865476))
                density = jnp.exp(-0.5 * value * value) * 0.3989422804014327
                hidden[s, place, tile] = (value * share).astype(BF)
                slope[s, place, tile] = (share + value * density).astype(BF)

            tiles(units, grow)

        def shrink(tile):
            total = mm(hidden[0, place, :], feed_full[0, 1, tile, :], NT)
            for s in range(1, slices):
                total = total + mm(hidden[s, place, :], feed_full[s, 1, tile, :], NT)
            store(tile, total)

        tiles(width, shrink)

    def backward(place, store):
        for s in range(slices):

            def narrow(tile):
                value = mm(summed_low[place, :], feed_full[s, 1, :, tile], NN)
                value = value * slope[s, place, tile].astype(F32)
                slope[s, place, tile] = value.astype(BF)

            tiles(units, narrow)

        def widen(tile):
            total = mm(slope[0, place, :], feed_full[0, 0, tile, :], NT)
            for s in range(1, slices):
                total = total + mm(slope[s, place, :], feed_full[s, 0, tile, :], NT)
            store(tile, total)

        tiles(width, widen)

    def keep(tile, total):
        own_part[:, tile] = total

    def pass_on(which, chunk):
        def store(tile, total):
            send_part[which, own(chunk), tile] = total.astype(BF)

        return store

    def arrive(s):
        for kind in feed_gathers[s]:
            if s > 0:
                kind.advance_rest()
            kind.finish()

    forward(pl.ds(0, rows), keep, arrive)
    for c in range(chunks):
        copies[0][c].wait_recv()
        forward(other(c), pass_on(0, c), lambda s: None)
        copies[1][c].start()

    vector_own[...] = jnp.zeros_like(vector_own)
    for c in range(chunks):
        copies[1][c].wait_recv()
        normal, _ = norm_parts(attended_ref[own(c), :])
        first_norm = normal * first_gain + first_shift
        summed = (
            first_norm
            + (own_part[own(c), :] + recv_part[0, own(c), :].astype(F32))
            + shrink_offset
        )
        normal, rate = norm_parts(summed)
        output_ref[own(c), :] = (normal * second_gain + second_shift).astype(BF)
        upstream = cotangent_ref[own(c), :].astype(F32)
        grad = norm_back(upstream, second_gain, normal, rate)
        summed_grad[own(c), :] = grad
        summed_low[own(c), :] = grad.astype(BF)
        copies[2][c].start()
        vector_own[0:1, :] += column_sum(upstream * normal)
        vector_own[1:2, :] += column_sum(upstream)
        vector_own[2:3, :] += column_sum(grad)

    def spare_rows(k):
        return pl.ds(pl.multiple_of(width // 2 + k * shard, shard), shard)

    def reduce(number, source, core_slot, chip_slot):
        return Reduce(
            here,
            source,
            core_slot,
            chip_slot,
            (chip_send.at[number], chip_recv.at[number]),
            (core_send.at[number], core_recv.at[number]),
        )

    def core_slot(s, kind):
        if (s, kind) == (1, 1):
            return lambda k: early_core.at[shard_rows(k)]
        return lambda k: feed_full.at[s, kind, shard_rows(k)]

    feed_reduces = [
        [
            TreeReduce(
                here,
                lambda i, s=s, kind=kind: feed_sum.at[s, kind, shard_rows(i)],
                core_slot(s, kind),
                lambda k, s=s, kind=kind: feed_chip.at[s, k - 1, kind],
                (chip_send.at[6 + 2 * s + kind], chip_recv.at[6 + 2 * s + kind]),
                (core_send.at[6 + 2 * s + kind], core_recv.at[6 + 2 * s + kind]),
                kind == 0,
            )
            for kind in range(2)
        ]
        for s in range(slices)
    ]
    mixing_reduce = reduce(
        10,
        lambda i: mixing_sum.at[shard_rows(i)],
        lambda k: feed_full.at[0, 0, spare_rows(k)],
        lambda k: mixing_chip.at[k - 1],
    )
    head_reduce = reduce(
        11,
        lambda i: head_sum.at[shard_rows(i)],
        lambda k: feed_full.at[0, 1, spare_rows(k), 0 : 3 * span],
        lambda k: head_chip.at[k - 1],
    )

    def weigh(s, kind):
        left, right = ((normed, slope), (summed_low, hidden))[kind]

        def one(tile):
            size = min(TILE, width)
            for m in range(width // size):
                part = pl.ds(m * size, size)
                feed_sum[s, kind, part, tile] = mm(left[:, part], right[s, :, tile], TN).astype(BF)
            if kind == 0:
                vector_own[6 + s : 7 + s, tile] = column_sum(slope[s, :, tile].astype(F32))

        tiles(units, one)

    backward(pl.ds(0, rows), keep)
    for c in range(chunks):
        copies[2][c].wait_recv()
        if c == chunks - 1:
            weigh(1, 1)
            feed_reduces[1][1].start()
        backward(other(c), pass_on(1, c))
        copies[3][c].start()

    for kind in feed_gathers[0] + feed_gathers[1]:
        kind.drain()
    for copy in pair_copies:
        copy.wait_send()
    pl.semaphore_signal(free_sem, inc=1, device_id=here.core(), device_id_type=MESH)

    weigh(1, 0)
    pl.semaphore_wait(free_sem, 1)
    feed_reduces[1][0].start()
    feed_reduces[1][1].combine()
    for kind in (1, 0):
        weigh(0, kind)
        feed_reduces[0][kind].start()

    def back_copy(s, chunk):
        return pltpu.make_async_remote_copy(
            src_ref=mix_back_send.at[s, own(chunk)],
            dst_ref=mix_back.at[t, own(chunk)],
            send_sem=back_send.at[chunk, s],
            recv_sem=back_recv.at[chunk, t],
            device_id=here.rank(s),
            device_id_type=MESH,
        )

    def back_arrival(s, chunk):
        return pltpu.make_async_remote_copy(
            src_ref=mix_back_send.at[s, own(chunk)],
            dst_ref=mix_back.at[s, own(chunk)],
            send_sem=back_send.at[chunk, s],
            recv_sem=back_recv.at[chunk, s],
            device_id=here.rank(s),
            device_id_type=MESH,
        )

    for c in range(chunks):
        copies[3][c].wait_recv()
        normal, rate = norm_parts(attended_ref[own(c), :])
        upstream = summed_grad[own(c), :] + (
            own_part[own(c), :] + recv_part[1, own(c), :].astype(F32)
        )
        grad = norm_back(upstream, first_gain, normal, rate)
        input_grad_ref[own(c), :] = grad
        attended_low[own(c), :] = grad.astype(BF)
        for j in range(ranks):
            s = chosen([far[u][j] for u in range(ranks)], t)
            block = mm(attended_low[own(c), :], mixing_full[s], NN).astype(BF)
            if j < ranks - 1:
                mix_back_send[s, own(c), :] = block
                back_copy(s, c).start()
            else:
                mix_back[s, own(c), :] = block
        vector_own[3:4, :] += column_sum(upstream * normal)
        vector_own[4:5, :] += column_sum(upstream)
        vector_own[5:6, :] += column_sum(grad)

    for j in range(ranks):
        mixing_sum[:, j * span : (j + 1) * span] = mm(attended_low[...], mixed[j], TN).astype(BF)
    mixing_reduce.start()
    feed_reduces[1][0].combine()

    own_part[...] = jnp.zeros_like(own_part)
    summed_grad[...] = jnp.zeros_like(summed_grad)

    def pair_back(kind):
        return remote(
            feed_sum.at[1, kind, mine],
            feed_pair.at[kind],
            (pair_send, pair_recv),
            2 + kind,
            here.rank(t ^ 2),
        )

    def pair_start(kind):
        feed_sum[1, kind, mine, :] = feed_reduces[1][kind].total().astype(BF)
        pair_back(kind).start()

    def attend_back(s):
        place = pl.ds(pl.multiple_of(s * rows, rows), rows)
        inner = (mix_back[s].astype(F32) * mix_heads[s].astype(F32)).T
        columns = []
        for h in range(heads):
            pair = slice(128 * (h // 2), 128 * (h // 2) + 128)
            side = (lane // HD) == (h % 2)
            none = jnp.zeros((), BF)
            query = jnp.where(side, queries[s, :, pair], none)
            upstream = jnp.where(side, mix_back[s, :, pair], none)
            delta = jnp.sum(inner[h * HD : (h + 1) * HD, :], axis=0, keepdims=True)
            log_total = log_totals[h : h + 1, place]
            column = None
            for k in range(ranks):
                part = slice(k * rows, (k + 1) * rows)
                lanes = slice(k * span + pair.start, k * span + pair.stop)
                scores = mm(key_rows[part, pair], query, NT)
                probs = jnp.exp(scores - log_total)
                prob_grad = mm(values[part, pair], upstream, NT)
                score_low = (probs * (prob_grad - delta)).astype(BF)
                summed_grad[:, lanes] += mm(probs.astype(BF), upstream, NN)
                own_part[:, lanes] += mm(score_low, query, NN)
                term = mm(key_columns[h * HD : (h + 1) * HD, part], score_low, NN)
                column = term if column is None else column + term
            columns.append(column)
        low = jnp.concatenate(columns, axis=0).T.astype(BF)
        query_low[place, :] = (low.astype(F32) * HD**-0.5).astype(BF)

    for j in range(ranks):
        s = t if j == 0 else chosen([near[u][j - 1] for u in range(ranks)], t)
        if j > 0:
            for c in range(chunks):
                back_arrival(s, c).wait_recv()
        attend_back(s)
        if j == 0:
            feed_reduces[1][1].advance(0)
        if j == 2:
            feed_reduces[1][1].advance_rest()
            pair_start(1)
        if j == 2:
            feed_reduces[1][0].advance(0)
    for k in range(ranks):
        part = slice(k * rows, (k + 1) * rows)
        lanes = slice(k * span, (k + 1) * span)
        key_low[part, :] = own_part[:, lanes].astype(BF)
        value_low[part, :] = summed_grad[:, lanes].astype(BF)

    def input_part(s, tile):
        place = pl.ds(pl.multiple_of(s * rows, rows), rows)
        return (
            mm(query_low[place, :], head_full[0, tile, :], NT)
            + mm(key_low[place, :], head_full[1, tile, :], NT)
            + mm(value_low[place, :], head_full[2, tile, :], NT)
        )

    def arrival_time(u, s):
        if s > u:
            u, s = last - u, last - s
        return s if u == last else s + 1 + last - 1 - u

    line_order = [
        sorted([s for s in range(ranks) if s != u], key=lambda s, u=u: (arrival_time(u, s), s))
        for u in range(ranks)
    ]

    def line_rows(j):
        return pl.ds((j % 2) * rows, rows)

    def line_send_ref(j, chunk):
        return hidden.at[j // 2, pl.ds((j % 2) * rows + chunk * step, step)]

    def line_copy(j, s, chunk):
        slot = jnp.where(s == t + 1, ranks, s)
        return pltpu.make_async_remote_copy(
            src_ref=line_send_ref(j, chunk),
            dst_ref=line_part.at[slot, own(chunk)],
            send_sem=line_send.at[j, chunk],
            recv_sem=line_recv.at[slot, chunk],
            device_id=here.rank(jnp.clip(jnp.where(s < t, t - 1, t + 1), 0, last)),
            device_id_type=MESH,
        )

    def line_arrival(slot, chunk):
        return pltpu.make_async_remote_copy(
            src_ref=line_part.at[slot, own(chunk)],
            dst_ref=line_part.at[slot, own(chunk)],
            send_sem=line_send.at[0, chunk],
            recv_sem=line_recv.at[slot, chunk],
            device_id=partner,
            device_id_type=MESH,
        )

    targets = [chosen([line_order[u][j] for u in range(ranks)], t) for j in range(ranks - 1)]
    opens = [
        jnp.logical_or(jnp.logical_and(s < t, t == last), jnp.logical_and(s > t, t == 0))
        for s in targets
    ]
    for j, s in enumerate(targets):

        def store(tile):
            hidden[j // 2, line_rows(j), tile] = input_part(s, tile).astype(BF)

        tiles(width, store)

        @pl.when(opens[j])
        def _():
            for c in range(chunks):
                line_copy(j, s, c).start()

    def weigh_heads(tile):
        for i, low in enumerate((query_low, key_low, value_low)):
            head_sum[tile, i * span : (i + 1) * span] = mm(sequence[:, tile], low[...], TN).astype(BF)

    feed_reduces[1][0].advance_rest()
    pair_start(0)
    for kind in feed_reduces[0]:
        kind.combine()
    mixing_reduce.combine()
    tiles(width, weigh_heads)
    head_reduce.start()
    vector_own[8:9, 0:span] = column_sum(query_low[...].astype(F32))
    vector_own[8:9, span : 2 * span] = column_sum(value_low[...].astype(F32))

    def vector_core_copy():
        return remote(
            vector_own, vector_core, (core_send.at[12], core_recv.at[12]), 0, here.core()
        )

    vector_core_copy().start()

    def store_own(tile):
        input_grad_ref[:, tile] = input_grad_ref[:, tile] + input_part(t, tile)

    tiles(width, store_own)

    def pass_line(j, s):
        @pl.when(jnp.logical_not(opens[j]))
        def _():
            for c in range(chunks):
                line_arrival(s, c).wait_recv()
                block = line_send_ref(j, c)
                block[...] = (
                    block[...].astype(F32) + line_part[s, own(c), :].astype(F32)
                ).astype(BF)
                line_copy(j, s, c).start()

    vector_core_copy().wait()
    vector_own[...] = vector_own[...] + vector_core[...]

    def vector_chip_copy(k):
        return remote(
            vector_own,
            vector_chip.at[k - 1],
            (chip_send.at[12], chip_recv.at[12]),
            k,
            here.chip(k),
        )

    each(chips, 1, lambda k: vector_chip_copy(k).start())
    head_reduce.combine()

    def span_lanes(j):
        return pl.ds(pl.multiple_of(j * span, span), span)

    def mixing_rank_copy(k):
        return remote(
            mixing_sum.at[mine, span_lanes(t ^ k)],
            mixing_rank.at[k - 1],
            (rank_send.at[0], rank_recv.at[0]),
            k,
            here.rank(t ^ k),
        )

    pass_line(0, targets[0])
    pass_line(1, targets[1])
    for kind in feed_reduces[0]:
        kind.advance(0)
    pass_line(2, targets[2])
    mixing_sum[mine, :] = mixing_reduce.total().astype(BF)
    for k in range(1, ranks):
        mixing_rank_copy(k).start()

    each(chips, 1, lambda k: vector_chip_copy(k).wait())
    vector_sum = vector_own[...]
    for k in range(1, chips):
        vector_sum = vector_sum + vector_chip[k - 1]
    vector_core[...] = vector_sum

    def vector_rank_copy(k):
        return remote(
            vector_core,
            vector_rank.at[k - 1],
            (rank_send.at[1], rank_recv.at[1]),
            k,
            here.rank(t ^ k),
        )

    for k in range(1, ranks):
        vector_rank_copy(k).start()

    head_total = head_reduce.total()
    for i in range(3):
        head_grad_ref[i] = head_total[:, i * span : (i + 1) * span]
    feed_own = []
    for kind in feed_reduces[0]:
        kind.advance_rest()
        feed_own.append(kind.total())
    for k in range(1, ranks):
        mixing_rank_copy(k).wait()
    mixing_grad = mixing_sum[mine, span_lanes(t)].astype(F32)
    for k in range(1, ranks):
        mixing_grad = mixing_grad + mixing_rank[k - 1].astype(F32)
    mixing_grad_ref[...] = mixing_grad
    pair_back(0).wait()
    pair_back(1).wait()
    expand_grad_ref[...] = feed_own[0] + feed_pair[0].astype(F32)
    shrink_grad_ref[...] = feed_own[1] + feed_pair[1].astype(F32)
    for k in range(1, ranks):
        vector_rank_copy(k).wait()
    vector_sum = vector_core[...]
    sums_ref[...] = vector_sum
    everywhere = vector_sum[0:6, :]
    for k in range(1, ranks):
        everywhere = everywhere + vector_rank[k - 1, 0:6, :]
    sums_ref[0:6, :] = everywhere
    sums_ref[6:7, :] = vector_sum[6:7, :] + vector_rank[1, 7:8, :]

    @pl.when(t < last)
    def _():
        for c in range(chunks):
            line_arrival(t, c).wait_recv()
            input_grad_ref[own(c), :] += line_part[t, own(c), :].astype(F32)

    @pl.when(t > 0)
    def _():
        for c in range(chunks):
            line_arrival(ranks, c).wait_recv()
            input_grad_ref[own(c), :] += line_part[ranks, own(c), :].astype(F32)

    for j in range(ranks - 1):
        for c in range(chunks):
            line_copy(j, targets[j], c).wait_send()
            back_copy(t ^ (j + 1), c).wait_send()
    for each_reduce in feed_reduces[0] + feed_reduces[1] + [mixing_reduce, head_reduce]:
        each_reduce.drain()
    for kind in range(4):
        for c in range(chunks):
            copies[kind][c].wait_send()
    for each_gather in (heads_gather, mixing_gather):
        each_gather.drain()
    for k in range(1, ranks):
        mix_copy(t ^ k).wait_send()
        weight_copy(k).wait_send()
    for s in range(ranks):

        @pl.when(jnp.logical_and(s <= t, t < last))
        def _():
            for c in range(chunks):
                row_copy(s, 1, c).wait_send()

        @pl.when(jnp.logical_and(s >= t, t > 0))
        def _():
            for c in range(chunks):
                row_copy(s, 0, c).wait_send()


def layer(devices, ranks, inputs):
    layer_input = inputs[0]
    rows, width = layer_input.shape
    span = inputs[1].shape[1]
    units = inputs[5].shape[1]
    slices = 2
    chunks = 2
    chips = devices // 2
    length = ranks * rows
    both = 2 * rows
    vmem = pl.BlockSpec(memory_space=pltpu.VMEM)
    dma = pltpu.SemaphoreType.DMA
    shard = width // devices
    outs = (
        jax.ShapeDtypeStruct((rows, width), BF),
        jax.ShapeDtypeStruct((rows, width), F32),
        jax.ShapeDtypeStruct((3, shard, span), F32),
        jax.ShapeDtypeStruct((shard, span), F32),
        jax.ShapeDtypeStruct((shard, units), F32),
        jax.ShapeDtypeStruct((shard, units), F32),
        jax.ShapeDtypeStruct((16, width), F32),
    )
    return pl.pallas_call(
        functools.partial(layer_kernel, devices, chunks),
        out_shape=outs,
        in_specs=[vmem] * len(inputs),
        out_specs=[vmem] * len(outs),
        scratch_shapes=[
            pltpu.VMEM((length, width), BF),
            pltpu.VMEM((ranks, rows, span), BF),
            pltpu.VMEM((length, span), BF),
            pltpu.VMEM((length, span), BF),
            pltpu.VMEM((ranks, rows, span), BF),
            pltpu.VMEM((8, length), F32),
            pltpu.VMEM((3, width, span), BF),
            pltpu.VMEM((ranks, width, span), BF),
            pltpu.VMEM((slices, 2, width, units), BF),
            pltpu.VMEM((slices, 1, units), F32),
            pltpu.VMEM((8, span), F32),
            pltpu.VMEM((8, width), F32),
            pltpu.VMEM((span, length), BF),
            pltpu.VMEM((span, length), BF),
            pltpu.VMEM((ranks, rows, span), BF),
            pltpu.VMEM((rows, width), F32),
            pltpu.VMEM((both, width), BF),
            pltpu.VMEM((slices, both, units), BF),
            pltpu.VMEM((slices, both, units), BF),
            pltpu.VMEM((both, width), BF),
            pltpu.VMEM((rows, width), F32),
            pltpu.VMEM((rows, width), F32),
            pltpu.VMEM((2, rows, width), BF),
            pltpu.VMEM((2, rows, width), BF),
            pltpu.VMEM((slices, 2, width, units), BF),
            pltpu.VMEM((slices, chips - 1, 2, shard, units), BF),
            pltpu.VMEM((2, shard, units), BF),
            pltpu.VMEM((width // 2, units), BF),
            pltpu.VMEM((width, ranks * span), BF),
            pltpu.VMEM((chips - 1, shard, ranks * span), BF),
            pltpu.VMEM((ranks - 1, shard, span), BF),
            pltpu.VMEM((width, 3 * span), BF),
            pltpu.VMEM((chips - 1, shard, 3 * span), BF),
            pltpu.VMEM((rows, width), BF),
            pltpu.VMEM((ranks, rows, span), BF),
            pltpu.VMEM((ranks, rows, span), BF),
            pltpu.VMEM((length, span), BF),
            pltpu.VMEM((length, span), BF),
            pltpu.VMEM((length, span), BF),
            pltpu.VMEM((ranks + 1, rows, width), BF),
            pltpu.VMEM((16, width), F32),
            pltpu.VMEM((16, width), F32),
            pltpu.VMEM((chips - 1, 16, width), F32),
            pltpu.VMEM((ranks - 1, 16, width), F32),
            dma((2, ranks, chunks)),
            dma((ranks, chunks)),
            dma((ranks,)),
            dma((ranks,)),
            dma((ranks,)),
            dma((ranks,)),
            dma((4,)),
            dma((4,)),
            dma((13, chips)),
            dma((13, chips)),
            dma((13, chips)),
            dma((13, chips)),
            dma((4, chunks)),
            dma((4, chunks)),
            dma((chunks, ranks)),
            dma((chunks, ranks)),
            dma((ranks - 1, chunks)),
            dma((ranks + 1, chunks)),
            dma((2, ranks)),
            dma((2, ranks)),
            pltpu.SemaphoreType.REGULAR,
        ],
        compiler_params=pltpu.CompilerParams(
            collective_id=1, has_side_effects=True, vmem_limit_bytes=VMEM_LIMIT
        ),
    )(*inputs)


def body(
    layer_input,
    query_weight,
    key_weight,
    value_weight,
    mixing_weight,
    expand_weight,
    shrink_weight,
    query_offset,
    value_offset,
    mixing_offset,
    expand_offset,
    shrink_offset,
    first_gain,
    first_shift,
    second_gain,
    second_shift,
    cotangent,
):
    results = layer(
        lax.axis_size("dp"),
        lax.axis_size("tensor"),
        (
            layer_input,
            query_weight,
            key_weight,
            value_weight,
            mixing_weight,
            expand_weight,
            shrink_weight,
            query_offset,
            value_offset,
            mixing_offset,
            expand_offset,
            shrink_offset,
            first_gain,
            first_shift,
            second_gain,
            second_shift,
            cotangent,
        ),
    )
    return place_outputs(results, expand_weight.shape[1], query_weight.shape[1])


def solution(mesh):
    rows = P(("dp", "tensor"), None)
    tall = P("dp", "tensor")
    wide = P("tensor", "dp")
    split = P("tensor")
    whole = P()
    return jax.shard_map(
        body,
        mesh=mesh,
        in_specs=(rows, tall, tall, tall, wide, tall, wide, split, split)
        + (whole, split, whole, whole, whole, whole, whole, rows),
        out_specs=(rows, rows, tall, tall, tall, wide, tall, wide, split, split)
        + (whole, split, whole, whole, whole, whole, whole),
        check_vma=False,
    )
```
